32 devices in a mesh: dp: 16 (over z, y, x), tensor: 2 (over core).
Axes of the slice: x: 2, y: 2, z: 4, core: 2. Of those that a mesh axis runs over, the one named last changes fastest.
Arguments:
- latents: float32 [32, 16, 256], P('dp', None, 'tensor'), may hold values from -6 to 6
- gaussian: float32 [32, 16, 256], P('dp', None, 'tensor'), may hold values from -6 to 6
- velocity: float32 [32, 16, 256], P('dp', None, 'tensor'), may hold values from -6 to 6
- time_ids: int32 [32], P('dp'), may hold values from 0 to 999, as said below
- labels: int32 [32], P('dp'), may hold values from 0 to 1000
- small_w: float32 [288, 768], replicated
- small_m: float32 [288, 768], replicated, may hold values from -0.0009765625 to 0.0009765625
- small_v: float32 [288, 768], replicated, may hold values from 1.904297e-09 to 7.629395e-09
- cond_w: float32 [1769, 768], P(None, 'dp')
- cond_m: float32 [1769, 768], P(None, 'dp'), may hold values from -0.0009765625 to 0.0009765625
- cond_v: float32 [1769, 768], P(None, 'dp'), as said below
- mod_w: float32 [768, 10752], P('dp')
- mod_m: float32 [768, 10752], P('dp'), may hold values from -0.0009765625 to 0.0009765625
- mod_v: float32 [768, 10752], P('dp'), as said below
- qkv_w: float32 [2, 768, 3, 768], P(None, 'dp', None, 'tensor')
- qkv_m: float32 [2, 768, 3, 768], P(None, 'dp', None, 'tensor'), may hold values from -0.0009765625 to 0.0009765625
- qkv_v: float32 [2, 768, 3, 768], P(None, 'dp', None, 'tensor'), as said below
- proj_w: float32 [2, 768, 768], P(None, 'tensor', 'dp')
- proj_m: float32 [2, 768, 768], P(None, 'tensor', 'dp'), may hold values from -0.0009765625 to 0.0009765625
- proj_v: float32 [2, 768, 768], P(None, 'tensor', 'dp'), as said below
- up_w: float32 [2, 768, 3072], P(None, 'dp', 'tensor')
- up_m: float32 [2, 768, 3072], P(None, 'dp', 'tensor'), may hold values from -0.0009765625 to 0.0009765625
- up_v: float32 [2, 768, 3072], P(None, 'dp', 'tensor'), as said below
- down_w: float32 [2, 3072, 768], P(None, 'tensor', 'dp')
- down_m: float32 [2, 3072, 768], P(None, 'tensor', 'dp'), may hold values from -0.0009765625 to 0.0009765625
- down_v: float32 [2, 3072, 768], P(None, 'tensor', 'dp'), as said below
Outputs:
- small_new: float32 [288, 768], replicated
- small_m_new: float32 [288, 768], replicated
- small_v_new: float32 [288, 768], replicated
- cond_new: float32 [1769, 768], P(None, 'dp')
- cond_m_new: float32 [1769, 768], P(None, 'dp')
- cond_v_new: float32 [1769, 768], P(None, 'dp')
- mod_new: float32 [768, 10752], P('dp')
- mod_m_new: float32 [768, 10752], P('dp')
- mod_v_new: float32 [768, 10752], P('dp')
- qkv_new: float32 [2, 768, 3, 768], P(None, 'dp', None, 'tensor')
- qkv_m_new: float32 [2, 768, 3, 768], P(None, 'dp', None, 'tensor')
- qkv_v_new: float32 [2, 768, 3, 768], P(None, 'dp', None, 'tensor')
- proj_new: float32 [2, 768, 768], P(None, 'tensor', 'dp')
- proj_m_new: float32 [2, 768, 768], P(None, 'tensor', 'dp')
- proj_v_new: float32 [2, 768, 768], P(None, 'tensor', 'dp')
- up_new: float32 [2, 768, 3072], P(None, 'dp', 'tensor')
- up_m_new: float32 [2, 768, 3072], P(None, 'dp', 'tensor')
- up_v_new: float32 [2, 768, 3072], P(None, 'dp', 'tensor')
- down_new: float32 [2, 3072, 768], P(None, 'tensor', 'dp')
- down_m_new: float32 [2, 3072, 768], P(None, 'tensor', 'dp')
- down_v_new: float32 [2, 3072, 768], P(None, 'tensor', 'dp')
- loss_sum: float32 [], replicated
- norms: float32 [2, 11], replicated
The draws below stay inside these ranges and needn't reach their ends.
Inputs may be any that keep to these rules, and one draw needn't show every extreme that they name: time_ids[b] is at least b * 1000 // 32 and less than that plus max(2, 31). `cond_v`: positive. `mod_v`: positive. `qkv_v`: positive. `proj_v`: positive. `up_v`: positive. `down_v`: positive.
All inputs are finite; a program needn't handle non-finite values.
Results may differ from the reference program's by a relative error of at most 0.015.
The reference program's roundings to bfloat16 on the way count: a program that leaves them out, or rounds other values in their place, can miss the bound.
Values may be sent and summed in bfloat16 or wider, within the bound.
A program may use at most 256 MiB of HBM per device.

```python
import math
import jax
import jax.numpy as jnp
from jax import lax

D = 768
HEADS = 12
HDIM = 64
FF = 3072
PATCH = 16
GRID = 16
FREQ = 256
CLASSES = 1001
L = 2
TSTEPS = 1000
STEP = 10
SEQ = 256
BATCH = 32
SROWS = 288
CROWS = 1769
MODCOLS = 10752


def draw_time_ids(key, part):
    sample_ids = jnp.arange(BATCH)
    start_ids = sample_ids * TSTEPS // BATCH
    band_width = max(2, TSTEPS // BATCH)
    picked = start_ids + jax.random.randint(key, (BATCH,), 0, band_width)
    return jnp.minimum(picked, TSTEPS - 1).astype(jnp.int32)


def rising_line(count):
    place = jnp.arange(count).astype(jnp.float32) / max(count - 1, 1)
    return 1.0 + 2.0 * place


def along_axis(vector, shape, axis_id):
    view = [1] * len(shape)
    view[axis_id] = shape[axis_id]
    return vector.reshape(view)


def rising_weight(key, shape, axis_id, fan_size):
    line = rising_line(shape[axis_id])
    line = line * lax.rsqrt(jnp.mean(line * line))
    base = jax.random.truncated_normal(key, -6.0, 6.0, shape, jnp.float32) * fan_size ** (-0.5)
    return base * along_axis(line, shape, axis_id)


def falling_second(key, shape, axis_id):
    low_end = (BATCH * SEQ) ** (-1) * 1.56e-05
    high_end = (BATCH * SEQ) ** (-1) * 6.25e-05
    base = jnp.exp(jax.random.uniform(key, shape, jnp.float32, math.log(low_end), math.log(high_end)))
    line = rising_line(shape[axis_id])
    factor = (line[-1] / line) ** 2
    return base * along_axis(factor, shape, axis_id)


def draw_small_w(key, part):
    row_ids = jnp.arange(2 * PATCH + FREQ)
    fan_size = jnp.where(row_ids < PATCH, PATCH, jnp.where(row_ids < PATCH + FREQ, FREQ, D)).astype(jnp.float32)
    return jax.random.normal(key, (2 * PATCH + FREQ, D), jnp.float32) * lax.rsqrt(fan_size)[:, None]


def draw_cond_w(key, part):
    row_ids = jnp.arange(D + CLASSES)
    row_scale = jnp.where(row_ids < D, D ** (-0.5), 1.0).astype(jnp.float32)
    return rising_weight(key, (D + CLASSES, D), 1, 1.0) * row_scale[:, None]


def draw_mod_w(key, part):
    return rising_weight(key, (D, (6 * L + 2) * D), 0, D)


def draw_qkv_w(key, part):
    return rising_weight(key, (L, D, 3, D), 1, D)


def draw_proj_w(key, part):
    return rising_weight(key, (L, D, D), 2, D // 16)


def draw_up_w(key, part):
    return rising_weight(key, (L, D, FF), 1, D)


def draw_down_w(key, part):
    return rising_weight(key, (L, FF, D), 2, FF)


def draw_cond_v(key, part):
    return falling_second(key, (D + CLASSES, D), 1)


def draw_mod_v(key, part):
    return falling_second(key, (D, (6 * L + 2) * D), 0)


def draw_qkv_v(key, part):
    return falling_second(key, (L, D, 3, D), 1)


def draw_proj_v(key, part):
    return falling_second(key, (L, D, D), 2)


def draw_up_v(key, part):
    return falling_second(key, (L, D, FF), 1)


def draw_down_v(key, part):
    return falling_second(key, (L, FF, D), 2)


def plant(result, stream_key, low, high):
    spot = [jax.random.randint(jax.random.fold_in(stream_key, axis), (), 0, length) for axis, length in enumerate(result.shape)]
    longest = result.shape.index(max(result.shape))
    neighbour = spot[:longest] + [(spot[longest] + 1) % result.shape[longest]] + spot[longest + 1:]
    return result.at[tuple(spot)].set(low).at[tuple(neighbour)].set(high)


def levels(stream_key, shape, split, least, high):
    loudness, own = 1.0, jax.random.fold_in(stream_key, 6)
    for position, blocks in split:
        steps = jnp.exp(jax.random.uniform(jax.random.fold_in(own, position), (blocks,), jnp.float32, least / len(split), high / len(split)))
        loudness = loudness * jnp.repeat(steps, shape[position] // blocks).reshape([-1 if axis == position else 1 for axis in range(len(shape))])
    return loudness


def bell_draw(key, shape, deviation, reach, cuts=(), kind=jnp.bfloat16):
    factor_of = levels(key, shape, cuts, -0.22, 0.18) if cuts else 1.0
    array = jax.random.normal(key, shape, jnp.float32) * deviation * factor_of
    return jnp.minimum(jnp.maximum(array, -reach), reach).astype(kind)


def setup_inputs(seed: int = 0) -> dict:
    arg_keys = jax.random.split(jax.random.key(seed), 27)
    return {
        "latents": bell_draw(arg_keys[0], (BATCH, PATCH, SEQ), 1.0, 6.0, ((0, 16), (2, 2)), jnp.float32),
        "gaussian": bell_draw(arg_keys[1], (BATCH, PATCH, SEQ), 1.0, 6.0, ((0, 16), (2, 2)), jnp.float32),
        "velocity": bell_draw(arg_keys[2], (BATCH, PATCH, SEQ), 1.0, 6.0, ((0, 16), (2, 2)), jnp.float32),
        "time_ids": draw_time_ids(jax.random.fold_in(arg_keys[26], 71), 0),
        "labels": plant(jax.random.randint(arg_keys[4], (BATCH,), 0, CLASSES), jax.random.fold_in(arg_keys[4], 1), 0, CLASSES - 1).astype(jnp.int32),
        "small_w": draw_small_w(jax.random.fold_in(arg_keys[26], 71), 0),
        "small_m": bell_draw(arg_keys[6], (SROWS, D), ((BATCH * SEQ) ** -0.5 * 0.0139), 0.0009765625, (), jnp.float32),
        "small_v": jnp.clip(jnp.exp(jax.random.uniform(arg_keys[7], (SROWS, D), jnp.float32, math.log(1.904296942356609e-09), math.log(7.629394893626795e-09))), 1.904296942356609e-09, 7.629394893626795e-09),
        "cond_w": draw_cond_w(jax.random.fold_in(arg_keys[26], 71), 0),
        "cond_m": bell_draw(arg_keys[9], (CROWS, D), ((BATCH * SEQ) ** -0.5 * 0.0139), 0.0009765625, ((1, 16),), jnp.float32),
        "cond_v": draw_cond_v(jax.random.fold_in(arg_keys[26], 71), 0),
        "mod_w": draw_mod_w(jax.random.fold_in(arg_keys[26], 71), 0),
        "mod_m": bell_draw(arg_keys[12], (D, MODCOLS), ((BATCH * SEQ) ** -0.5 * 0.0139), 0.0009765625, ((0, 16),), jnp.float32),
        "mod_v": draw_mod_v(jax.random.fold_in(arg_keys[26], 71), 0),
        "qkv_w": draw_qkv_w(jax.random.fold_in(arg_keys[26], 71), 0),
        "qkv_m": bell_draw(arg_keys[15], (L, D, 3, D), ((BATCH * SEQ) ** -0.5 * 0.0139), 0.0009765625, ((1, 16), (3, 2)), jnp.float32),
        "qkv_v": draw_qkv_v(jax.random.fold_in(arg_keys[26], 71), 0),
        "proj_w": draw_proj_w(jax.random.fold_in(arg_keys[26], 71), 0),
        "proj_m": bell_draw(arg_keys[18], (L, D, D), ((BATCH * SEQ) ** -0.5 * 0.0139), 0.0009765625, ((1, 2), (2, 16)), jnp.float32),
        "proj_v": draw_proj_v(jax.random.fold_in(arg_keys[26], 71), 0),
        "up_w": draw_up_w(jax.random.fold_in(arg_keys[26], 71), 0),
        "up_m": bell_draw(arg_keys[21], (L, D, FF), ((BATCH * SEQ) ** -0.5 * 0.0139), 0.0009765625, ((1, 16), (2, 2)), jnp.float32),
        "up_v": draw_up_v(jax.random.fold_in(arg_keys[26], 71), 0),
        "down_w": draw_down_w(jax.random.fold_in(arg_keys[26], 71), 0),
        "down_m": bell_draw(arg_keys[24], (L, FF, D), ((BATCH * SEQ) ** -0.5 * 0.0139), 0.0009765625, ((1, 2), (2, 16)), jnp.float32),
        "down_v": draw_down_v(jax.random.fold_in(arg_keys[26], 71), 0),
    }


HIGHEST_PREC = lax.Precision.HIGHEST
BETA_ONE = 0.9
BETA_TWO = 0.999
EPS_ADAM = 1e-06
EPS_LAYER = 1e-06
EPS_NORM = 1e-12
WEIGHT_DECAY = 0.01
LEARN_RATE = 0.25

@jax.custom_vjp
def low(v):
    return lax.optimization_barrier(v.astype(jnp.bfloat16)).astype(jnp.float32)

@jax.custom_vjp
def low_back(v):
    return v

def low_keep(v):
    return (low(v), None)

def low_pass(kept, grad):
    return (grad,)

def back_keep(v):
    return (v, None)

def back_low(kept, grad):
    return (low(grad),)
low.defvjp(low_keep, low_pass)
low_back.defvjp(back_keep, back_low)

def rounded_both(values_in):
    return low(low_back(values_in))

def product(form, left, right):
    return jnp.einsum(form, left, right, precision=HIGHEST_PREC)

def time_features(moment):
    half_freq = FREQ // 2
    frequency = jnp.exp(-math.log(10000.0) * jnp.arange(half_freq).astype(jnp.float32) / half_freq)
    angles = (1000.0 * moment)[:, None] * frequency[None, :]
    return jnp.concatenate([jnp.cos(angles), jnp.sin(angles)], axis=1)

def position_table(token_index, model_width):
    quarter = model_width // 4
    omega_rate = 1.0 / 10000.0 ** (jnp.arange(quarter).astype(jnp.float32) / quarter)
    grid_row = (token_index // GRID).astype(jnp.float32)[:, None] * omega_rate[None, :]
    grid_col = (token_index % GRID).astype(jnp.float32)[:, None] * omega_rate[None, :]
    return jnp.concatenate([jnp.sin(grid_col), jnp.cos(grid_col), jnp.sin(grid_row), jnp.cos(grid_row)], axis=1)

def modulated_norm(hidden_in, shift_vec, scale_vec):
    centre = hidden_in - lax.optimization_barrier(jnp.mean(hidden_in, axis=-1, keepdims=True))
    spread = lax.optimization_barrier(jnp.mean(centre * centre, axis=-1, keepdims=True))
    return centre * lax.rsqrt(spread + EPS_LAYER) * (1.0 + scale_vec[:, None, :]) + shift_vec[:, None, :]

def lamb_parts(weight, first, second, grad):
    first_new = BETA_ONE * first + (1.0 - BETA_ONE) * grad
    second_new = BETA_TWO * second + (1.0 - BETA_TWO) * grad * grad
    update = first_new / (1.0 - BETA_ONE ** STEP) / (jnp.sqrt(second_new / (1.0 - BETA_TWO ** STEP)) + EPS_ADAM) + WEIGHT_DECAY * weight
    return (first_new, second_new, update)

def group_loss(params, latents, gaussian, velocity, time_ids, labels):
    small_w, cond_w, mod_w, qkv_w, proj_w, up_w, down_w = params
    group = latents.shape[0]
    moment = (time_ids.astype(jnp.float32) + 0.5) / TSTEPS
    features = low(time_features(moment))
    time_pre = low_back(product('bf,fd->bd', features, small_w[PATCH:PATCH + FREQ]))
    time_act = low(jax.nn.silu(time_pre))
    time_emb = low_back(product('bd,de->be', time_act, cond_w[:D]))
    onehot = (labels[:, None] == jnp.arange(CLASSES)[None, :]).astype(jnp.float32)
    cond = time_emb + product('bc,cd->bd', onehot, cond_w[D:])
    cond_act = low(jax.nn.silu(cond))
    modulation = low_back(product('bd,de->be', cond_act, mod_w))
    blended = low((1.0 - moment)[:, None, None] * latents + moment[:, None, None] * gaussian)
    hidden = low_back(product('bpn,pd->bnd', blended, small_w[:PATCH])) + position_table(jnp.arange(SEQ), D)[None]
    for layer_id in range(L):
        layer_mod = modulation[:, 6 * layer_id * D:(6 * layer_id + 6) * D].reshape(group, 6, D)
        normed = low(modulated_norm(hidden, layer_mod[:, 0], layer_mod[:, 1]))
        mixed = rounded_both(product('bnd,dte->bnte', normed, qkv_w[layer_id])).reshape(group, SEQ, 3, HEADS, HDIM)
        scores = low_back(product('bnhe,bmhe->bhnm', mixed[:, :, 0], mixed[:, :, 1]) * HDIM ** (-0.5))
        softmax_w = low(jax.nn.softmax(scores, axis=-1))
        attended = rounded_both(product('bhnm,bmhe->bnhe', softmax_w, mixed[:, :, 2])).reshape(group, SEQ, D)
        branch = low_back(product('bne,ed->bnd', attended, proj_w[layer_id]))
        middle = hidden + layer_mod[:, 2][:, None, :] * branch
        normed_two = low(modulated_norm(middle, layer_mod[:, 3], layer_mod[:, 4]))
        inner_pre = low_back(product('bnd,df->bnf', normed_two, up_w[layer_id]))
        activ = low(jax.nn.gelu(inner_pre, approximate=True))
        outer_out = low_back(product('bnf,fd->bnd', activ, down_w[layer_id]))
        hidden = middle + layer_mod[:, 5][:, None, :] * outer_out
    final_mod = modulation[:, 6 * L * D:].reshape(group, 2, D)
    final_normed = low(modulated_norm(hidden, final_mod[:, 0], final_mod[:, 1]))
    predicted = low_back(product('bnd,pd->bpn', final_normed, small_w[PATCH + FREQ:]))
    error = predicted - velocity
    return jnp.sum((0.5 + moment)[:, None, None] * error * error)

def reference(latents, gaussian, velocity, time_ids, labels, small_w, small_m, small_v, cond_w, cond_m, cond_v, mod_w, mod_m, mod_v, qkv_w, qkv_m, qkv_v, proj_w, proj_m, proj_v, up_w, up_m, up_v, down_w, down_m, down_v):
    params = (small_w, cond_w, mod_w, qkv_w, proj_w, up_w, down_w)
    firsts = (small_m, cond_m, mod_m, qkv_m, proj_m, up_m, down_m)
    seconds = (small_v, cond_v, mod_v, qkv_v, proj_v, up_v, down_v)
    group = math.gcd(BATCH, max(1, 4096 // SEQ))
    group_count = BATCH // group

    def grouped(array_in):
        return array_in.reshape((group_count, group) + array_in.shape[1:])
    batches = (grouped(latents), grouped(gaussian), grouped(velocity), grouped(time_ids), grouped(labels))

    def objective(weights):
        low_params = tuple((low(p) for p in weights))

        def group_step(running, group_data):
            return (running + jax.checkpoint(group_loss)(low_params, *group_data), None)
        total_loss, _ = lax.scan(group_step, jnp.zeros((), jnp.float32), batches)
        return (total_loss / (BATCH * SEQ * PATCH), total_loss)
    _, pullback, loss_sum = jax.vjp(objective, params, has_aux=True)
    grads = pullback(jnp.ones((), jnp.float32))[0]
    matrices = []
    for kind_id in range(3):
        matrices.append((params[kind_id], firsts[kind_id], seconds[kind_id], grads[kind_id]))
    for kind_id in range(3, 7):
        for layer_id in range(L):
            matrices.append((params[kind_id][layer_id], firsts[kind_id][layer_id], seconds[kind_id][layer_id], grads[kind_id][layer_id]))
    results = [lamb_parts(*m) for m in matrices]
    weight_norm = jnp.stack([jnp.sqrt(jnp.sum(m[0] * m[0]) + EPS_NORM) for m in matrices])
    update_norm = jnp.stack([jnp.sqrt(jnp.sum(r[2] * r[2]) + EPS_NORM) for r in results])
    renewed = [matrices[i][0] - LEARN_RATE * (weight_norm[i] / update_norm[i]) * results[i][2] for i in range(len(matrices))]
    firsts_new = [r[0] for r in results]
    seconds_new = [r[1] for r in results]
    span_list = [[0], [1], [2]] + [[3 + kind_id * L + l for l in range(L)] for kind_id in range(4)]
    outputs = []
    for kind_id, span_ids in enumerate(span_list):
        for source in (renewed, firsts_new, seconds_new):
            picked = [source[i] for i in span_ids]
            outputs.append(picked[0] if kind_id < 3 else jnp.stack(picked))
    norms = jnp.stack([weight_norm, update_norm])
    return (outputs[0], outputs[1], outputs[2], outputs[3], outputs[4], outputs[5], outputs[6], outputs[7], outputs[8], outputs[9], outputs[10], outputs[11], outputs[12], outputs[13], outputs[14], outputs[15], outputs[16], outputs[17], outputs[18], outputs[19], outputs[20], loss_sum, norms)
```

```python
import math

import jax
import jax.numpy as jnp
from jax import lax
from jax.experimental import pallas as pl
from jax.experimental.pallas import tpu as pltpu
from jax.sharding import PartitionSpec as P

HDIM = 64
PATCH = 16
GRID = 16
FREQ = 256
CLASSES = 1001
TSTEPS = 1000
STEP = 10


HIGHEST_PREC = lax.Precision.HIGHEST
BETA_ONE = 0.9
BETA_TWO = 0.999
EPS_ADAM = 1e-06
EPS_LAYER = 1e-06
EPS_NORM = 1e-12
WEIGHT_DECAY = 0.01
LEARN_RATE = 0.25


def time_features(moment):
    half_freq = FREQ // 2
    frequency = jnp.exp(-math.log(10000.0) * jnp.arange(half_freq).astype(jnp.float32) / half_freq)
    angles = (1000.0 * moment)[:, None] * frequency[None, :]
    return jnp.concatenate([jnp.cos(angles), jnp.sin(angles)], axis=1)


def position_table(token_index, model_width):
    quarter = model_width // 4
    omega_rate = 1.0 / 10000.0 ** (jnp.arange(quarter).astype(jnp.float32) / quarter)
    grid_row = (token_index // GRID).astype(jnp.float32)[:, None] * omega_rate[None, :]
    grid_col = (token_index % GRID).astype(jnp.float32)[:, None] * omega_rate[None, :]
    return jnp.concatenate(
        [jnp.sin(grid_col), jnp.cos(grid_col), jnp.sin(grid_row), jnp.cos(grid_row)], axis=1
    )


def modulated_norm(hidden_in, shift_vec, scale_vec):
    centre = hidden_in - jnp.mean(hidden_in, axis=-1, keepdims=True)
    spread = jnp.mean(centre * centre, axis=-1, keepdims=True)
    return (
        centre * lax.rsqrt(spread + EPS_LAYER) * (1.0 + scale_vec[:, None, :])
        + shift_vec[:, None, :]
    )


def lamb_parts(weight, first, second, grad):
    first_new = BETA_ONE * first + (1.0 - BETA_ONE) * grad
    second_new = BETA_TWO * second + (1.0 - BETA_TWO) * grad * grad
    update = (
        first_new
        / (1.0 - BETA_ONE**STEP)
        / (jnp.sqrt(second_new / (1.0 - BETA_TWO**STEP)) + EPS_ADAM)
        + WEIGHT_DECAY * weight
    )
    return (first_new, second_new, update)


def gelu_tanh(values_in):
    return jax.nn.gelu(values_in, approximate=True)


def spread_rows(part_rows):
    return lax.all_gather(part_rows, "tensor", axis=1, tiled=True)


def fold_rows(term_rows):
    return lax.psum_scatter(
        term_rows.astype(jnp.bfloat16), "tensor", scatter_dimension=1, tiled=True
    ).astype(jnp.float32)


def split_heads(gathered, w_qkv):
    mixed = jnp.einsum("bnd,dte->bnte", gathered, w_qkv, preferred_element_type=jnp.float32).astype(
        jnp.bfloat16
    )
    shaped = mixed.reshape(mixed.shape[0], mixed.shape[1], 3, -1, HDIM)
    return (shaped[:, :, 0], shaped[:, :, 1], shaped[:, :, 2])


def score_block(queries, key_heads):
    return jnp.einsum(
        "bnhe,bmhe->bhnm", queries, key_heads, preferred_element_type=jnp.float32
    ) * HDIM ** (-0.5)


def block_forward(hidden, layer_mod, weights):
    w_qkv, w_proj, w_up, w_down = weights
    normed = modulated_norm(hidden, layer_mod[:, 0], layer_mod[:, 1]).astype(jnp.bfloat16)
    gathered = spread_rows(normed)
    queries, key_heads, values = split_heads(gathered, w_qkv)
    scores = score_block(queries, key_heads)
    row_top = jnp.max(scores, axis=-1, keepdims=True)
    logsum = row_top + jnp.log(jnp.sum(jnp.exp(scores - row_top), axis=-1, keepdims=True))
    softmax_w = jnp.exp(scores - logsum).astype(jnp.bfloat16)
    attended = jnp.einsum(
        "bhnm,bmhe->bnhe", softmax_w, values, preferred_element_type=jnp.float32
    ).astype(jnp.bfloat16)
    attended = attended.reshape(attended.shape[0], attended.shape[1], -1)
    branch = fold_rows(
        jnp.einsum("bne,de->bnd", attended, w_proj, preferred_element_type=jnp.float32)
    )
    middle = hidden + layer_mod[:, 2][:, None, :] * branch
    normed_two = modulated_norm(middle, layer_mod[:, 3], layer_mod[:, 4]).astype(jnp.bfloat16)
    gathered_two = spread_rows(normed_two)
    inner_pre = jnp.einsum("bnd,df->bnf", gathered_two, w_up, preferred_element_type=jnp.float32)
    activ = gelu_tanh(inner_pre).astype(jnp.bfloat16)
    outer_out = fold_rows(
        jnp.einsum("bnf,df->bnd", activ, w_down, preferred_element_type=jnp.float32)
    )
    output = middle + layer_mod[:, 5][:, None, :] * outer_out
    saved_state = (
        hidden,
        gathered,
        queries,
        key_heads,
        values,
        attended,
        logsum,
        branch,
        middle,
        gathered_two,
        inner_pre,
        outer_out,
    )
    return (output, saved_state)


def block_backward(grad_out, layer_mod, weights, saved_state):
    (
        hidden,
        gathered,
        queries,
        key_heads,
        values,
        attended,
        logsum,
        branch,
        middle,
        gathered_two,
        inner_pre,
        outer_out,
    ) = saved_state
    w_qkv, w_proj, w_up, w_down = weights
    grad_gate_m = jnp.sum(grad_out * outer_out, axis=1)
    grad_outer = spread_rows((layer_mod[:, 5][:, None, :] * grad_out).astype(jnp.bfloat16))
    activ = gelu_tanh(inner_pre).astype(jnp.bfloat16)
    grad_down = jnp.einsum("bnd,bnf->df", grad_outer, activ, preferred_element_type=jnp.float32)
    grad_activ = jnp.einsum("bnd,df->bnf", grad_outer, w_down, preferred_element_type=jnp.float32)
    _, gelu_back = jax.vjp(gelu_tanh, inner_pre)
    grad_inner = gelu_back(grad_activ)[0].astype(jnp.bfloat16)
    grad_up = jnp.einsum(
        "bnd,bnf->df", gathered_two, grad_inner, preferred_element_type=jnp.float32
    )
    grad_normed_two = fold_rows(
        jnp.einsum("bnf,df->bnd", grad_inner, w_up, preferred_element_type=jnp.float32)
    )
    _, norm_back = jax.vjp(modulated_norm, middle, layer_mod[:, 3], layer_mod[:, 4])
    grad_middle, grad_shift_m, grad_scale_m = norm_back(grad_normed_two)
    grad_middle = grad_middle + grad_out
    grad_gate_a = jnp.sum(grad_middle * branch, axis=1)
    grad_branch = spread_rows((layer_mod[:, 2][:, None, :] * grad_middle).astype(jnp.bfloat16))
    grad_proj = jnp.einsum("bnd,bne->de", grad_branch, attended, preferred_element_type=jnp.float32)
    grad_att = jnp.einsum(
        "bnd,de->bne", grad_branch, w_proj, preferred_element_type=jnp.float32
    ).astype(jnp.bfloat16)
    grad_att = grad_att.reshape(queries.shape)
    scores = score_block(queries, key_heads)
    soft_float = jnp.exp(scores - logsum)
    softmax_w = soft_float.astype(jnp.bfloat16)
    grad_values = jnp.einsum(
        "bhnm,bnhe->bmhe", softmax_w, grad_att, preferred_element_type=jnp.float32
    ).astype(jnp.bfloat16)
    grad_soft = jnp.einsum("bnhe,bmhe->bhnm", grad_att, values, preferred_element_type=jnp.float32)
    row_delta = jnp.sum(soft_float * grad_soft, axis=-1, keepdims=True)
    grad_scores = (soft_float * (grad_soft - row_delta)).astype(jnp.bfloat16)
    grad_queries = (
        jnp.einsum("bhnm,bmhe->bnhe", grad_scores, key_heads, preferred_element_type=jnp.float32)
        * HDIM ** (-0.5)
    ).astype(jnp.bfloat16)
    grad_keys = (
        jnp.einsum("bhnm,bnhe->bmhe", grad_scores, queries, preferred_element_type=jnp.float32)
        * HDIM ** (-0.5)
    ).astype(jnp.bfloat16)
    grad_mixed = jnp.stack([grad_queries, grad_keys, grad_values], axis=2)
    grad_mixed = grad_mixed.reshape(grad_mixed.shape[0], grad_mixed.shape[1], 3, -1)
    grad_qkv = jnp.einsum("bnd,bnte->dte", gathered, grad_mixed, preferred_element_type=jnp.float32)
    grad_normed = fold_rows(
        jnp.einsum("bnte,dte->bnd", grad_mixed, w_qkv, preferred_element_type=jnp.float32)
    )
    _, norm_back_two = jax.vjp(modulated_norm, hidden, layer_mod[:, 0], layer_mod[:, 1])
    grad_hidden, grad_shift_a, grad_scale_a = norm_back_two(grad_normed)
    grad_hidden = grad_hidden + grad_middle
    grad_layer_mod = jnp.stack(
        [grad_shift_a, grad_scale_a, grad_gate_a, grad_shift_m, grad_scale_m, grad_gate_m], axis=1
    )
    return (grad_hidden, grad_layer_mod, (grad_qkv, grad_proj, grad_up, grad_down))


def grid_of(dp_count):
    if dp_count == 16:
        return (4, 2, 2)
    sizes = [1, 1, 1]
    rest, prime = dp_count, 2
    while rest > 1:
        while rest % prime == 0:
            sizes[sizes.index(min(sizes))] *= prime
            rest //= prime
        prime += 1
    return tuple(sorted(sizes, reverse=True))


ORDERS = ((0, 1, 2), (0, 2, 1))


def place(sizes):
    index = lax.axis_index("dp")
    return (index // (sizes[1] * sizes[2]), index // sizes[2] % sizes[1], index % sizes[2])


def peer_of(sizes, spot, axis, other):
    moved = [other if a == axis else spot[a] for a in range(3)]
    return (moved[0] * sizes[1] + moved[1]) * sizes[2] + moved[2], lax.axis_index("tensor")


def entry_barrier(sizes, spot):
    barrier = pltpu.get_barrier_semaphore()
    count = 0
    for axis in range(3):
        for offset in range(1, sizes[axis]):
            other = (spot[axis] + offset) % sizes[axis]
            pl.semaphore_signal(
                barrier,
                inc=1,
                device_id=peer_of(sizes, spot, axis, other),
                device_id_type=pl.DeviceIdType.MESH,
            )
            count += 1
    pl.semaphore_wait(barrier, count)


def gather_kernel(sizes, blob_ref, out_ref, send_sem, recv_sem, own_sem):
    spot = place(sizes)
    waves, columns = out_ref.shape[0], out_ref.shape[5]
    half = columns // 2
    own = pltpu.make_async_copy(blob_ref, out_ref.at[:, spot[0], spot[1], spot[2]], own_sem)
    own.start()
    entry_barrier(sizes, spot)

    def copies(wave, order_id, phase):
        order = ORDERS[order_id]
        axis = order[phase]
        pick = [spot[a] for a in range(3)]
        for earlier in order[:phase]:
            pick[earlier] = slice(None)
        lanes = pl.ds(order_id * half, half)
        target = out_ref.at[wave, pick[0], pick[1], pick[2], :, lanes]
        source = blob_ref.at[wave, :, lanes] if phase == 0 else target
        made = []
        for offset in range(1, sizes[axis]):
            other = (spot[axis] + offset) % sizes[axis]
            made.append(
                pltpu.make_async_remote_copy(
                    src_ref=source,
                    dst_ref=target,
                    send_sem=send_sem.at[wave, order_id, phase, offset],
                    recv_sem=recv_sem.at[wave, order_id, phase, offset],
                    device_id=peer_of(sizes, spot, axis, other),
                    device_id_type=pl.DeviceIdType.MESH,
                )
            )
        return made

    started = []
    for step in range(waves + 3):
        for phase in reversed(range(4)):
            wave = step - phase
            if not 0 <= wave < waves:
                continue
            for order_id in range(2):
                if phase > 0:
                    for copy in copies(wave, order_id, phase - 1):
                        copy.wait_recv()
                if wave == 0 and phase == 1 and order_id == 0:
                    own.wait()
                if phase < 3:
                    for copy in copies(wave, order_id, phase):
                        copy.start()
                        started.append(copy)
    for copy in started:
        copy.wait_send()


def gather_weights(blob, dp_count):
    sizes = grid_of(dp_count)
    waves, rows, columns = blob.shape
    most = max(sizes)
    out = pl.pallas_call(
        lambda *refs: gather_kernel(sizes, *refs),
        out_shape=jax.ShapeDtypeStruct((waves,) + sizes + (rows, columns), blob.dtype),
        in_specs=[pl.BlockSpec(memory_space=pl.ANY)],
        out_specs=pl.BlockSpec(memory_space=pl.ANY),
        scratch_shapes=[
            pltpu.SemaphoreType.DMA((waves, 2, 3, most)),
            pltpu.SemaphoreType.DMA((waves, 2, 3, most)),
            pltpu.SemaphoreType.DMA,
        ],
        compiler_params=pltpu.CompilerParams(collective_id=0, has_side_effects=True),
    )(blob)
    return out.reshape(waves, dp_count * rows, columns)


def reduce_grads_kernel(sizes, waves, *refs):
    grads = refs[:waves]
    out_ref = refs[waves]
    held, got_one, got_two, got_three, send_sem, recv_sem, load_sem = refs[waves + 1 :]
    spot = place(sizes)
    half = out_ref.shape[2] // 2
    loads = []
    for wave in range(waves):
        load = pltpu.make_async_copy(grads[wave], held.at[wave], load_sem.at[wave])
        load.start()
        loads.append(load)
    entry_barrier(sizes, spot)
    inbox = (got_one, got_two, got_three)

    def copies(wave, order_id, phase):
        order = ORDERS[order_id][::-1]
        axis = order[phase]
        lanes = pl.ds(order_id * half, half)
        made = []
        for offset in range(1, sizes[axis]):
            other = (spot[axis] + offset) % sizes[axis]
            pick = [slice(None)] * 3
            for earlier in order[:phase]:
                pick[earlier] = spot[earlier]
            pick[axis] = other
            source = held.at[wave, pick[0], pick[1], pick[2], :, lanes]
            target = inbox[phase].at[wave, order_id, offset - 1]
            made.append(
                pltpu.make_async_remote_copy(
                    src_ref=source,
                    dst_ref=target,
                    send_sem=send_sem.at[wave, order_id, phase, offset],
                    recv_sem=recv_sem.at[wave, order_id, phase, offset],
                    device_id=peer_of(sizes, spot, axis, other),
                    device_id_type=pl.DeviceIdType.MESH,
                )
            )
        return made

    def absorb(wave, order_id, phase):
        order = ORDERS[order_id][::-1]
        lanes = pl.ds(order_id * half, half)
        box = inbox[phase]
        peers = sizes[order[phase]] - 1
        if phase == 2:
            total = held[wave, spot[0], spot[1], spot[2], :, lanes].astype(jnp.float32)
            for p in range(peers):
                total = total + box[wave, order_id, p].astype(jnp.float32)
            out_ref[wave, :, lanes] = total
            return
        left = order[phase + 1 :]
        if phase == 0:
            first, second = left
            first, second = max(first, second), min(first, second)

            def body(step, carry):
                low, high = step % sizes[first], step // sizes[first]
                pick = [spot[0], spot[1], spot[2]]
                pick[first], pick[second] = low, high
                total = held[wave, pick[0], pick[1], pick[2], :, lanes].astype(jnp.float32)
                for p in range(peers):
                    total = total + box[wave, order_id, p, high, low].astype(jnp.float32)
                held[wave, pick[0], pick[1], pick[2], :, lanes] = total.astype(held.dtype)
                return carry

            lax.fori_loop(0, sizes[first] * sizes[second], body, 0)
        else:
            (only,) = left

            def body_one(step, carry):
                pick = [spot[0], spot[1], spot[2]]
                pick[only] = step
                total = held[wave, pick[0], pick[1], pick[2], :, lanes].astype(jnp.float32)
                for p in range(peers):
                    total = total + box[wave, order_id, p, step].astype(jnp.float32)
                held[wave, pick[0], pick[1], pick[2], :, lanes] = total.astype(held.dtype)
                return carry

            lax.fori_loop(0, sizes[only], body_one, 0)

    started = []
    for step in range(waves + 3):
        for phase in reversed(range(4)):
            wave = step - phase
            if not 0 <= wave < waves:
                continue
            if phase == 0:
                loads[wave].wait()
            for order_id in range(2):
                if phase > 0:
                    for copy in copies(wave, order_id, phase - 1):
                        copy.wait_recv()
                    absorb(wave, order_id, phase - 1)
                if phase < 3:
                    for copy in copies(wave, order_id, phase):
                        copy.start()
                        started.append(copy)
    for copy in started:
        copy.wait_send()


def reduce_grads(grads, dp_count):
    sizes = grid_of(dp_count)
    waves = len(grads)
    rows, columns = grads[0].shape[0] // dp_count, grads[0].shape[1]
    half = columns // 2
    most = max(sizes)
    grads = [g.reshape(sizes + (rows, columns)) for g in grads]
    low = jnp.bfloat16
    return pl.pallas_call(
        lambda *refs: reduce_grads_kernel(sizes, waves, *refs),
        out_shape=jax.ShapeDtypeStruct((waves, rows, columns), jnp.float32),
        in_specs=[pl.BlockSpec(memory_space=pl.ANY)] * waves,
        out_specs=pl.BlockSpec(memory_space=pltpu.VMEM),
        scratch_shapes=[
            pltpu.VMEM((waves,) + sizes + (rows, columns), low),
            pltpu.VMEM((waves, 2, sizes[2] - 1, sizes[0], sizes[1], rows, half), low),
            pltpu.VMEM((waves, 2, sizes[1] - 1, sizes[0], rows, half), low),
            pltpu.VMEM((waves, 2, sizes[0] - 1, rows, half), low),
            pltpu.SemaphoreType.DMA((waves, 2, 3, most)),
            pltpu.SemaphoreType.DMA((waves, 2, 3, most)),
            pltpu.SemaphoreType.DMA((waves,)),
        ],
        compiler_params=pltpu.CompilerParams(
            collective_id=1, has_side_effects=True, vmem_limit_bytes=60 * 2**20
        ),
    )(*grads)


def gather_plain(blob, dp_count):
    waves, rows, columns = blob.shape
    return lax.all_gather(blob, "dp", axis=1, tiled=True)


def reduce_plain(grads, dp_count):
    return jnp.stack(
        [
            lax.psum_scatter(g.astype(jnp.float32), "dp", scatter_dimension=0, tiled=True)
            for g in grads
        ]
    )


def local(
    latents,
    gaussian,
    velocity,
    time_ids,
    labels,
    small_w,
    small_m,
    small_v,
    cond_w,
    cond_m,
    cond_v,
    mod_w,
    mod_m,
    mod_v,
    qkv_w,
    qkv_m,
    qkv_v,
    proj_w,
    proj_m,
    proj_v,
    up_w,
    up_m,
    up_v,
    down_w,
    down_m,
    down_v,
):
    layer_count = qkv_w.shape[0]
    model_width = mod_w.shape[1] // (6 * layer_count + 2)
    dp_count = lax.axis_size("dp")
    tensor_count = lax.axis_size("tensor")
    samples = latents.shape[0]
    half_rows = latents.shape[2]
    rows = qkv_w.shape[1]
    kernels = rows % 16 == 0
    my_dp = lax.axis_index("dp")
    low = jnp.bfloat16

    parts = []
    for i in range(layer_count):
        parts.append(
            jnp.concatenate(
                [qkv_w[i, :, 0], qkv_w[i, :, 1], qkv_w[i, :, 2], proj_w[i].T], axis=1
            ).astype(low)
        )
        parts.append(up_w[i].astype(low))
        parts.append(down_w[i].T.astype(low))
    blob = jnp.stack(parts)
    full = (gather_weights if kernels else gather_plain)(blob, dp_count)
    heads_wide = qkv_w.shape[3]

    ids = lax.all_gather(jnp.stack([time_ids, labels]), "dp", axis=1, tiled=True)
    all_times, all_labels = ids[0], ids[1]
    small_low = small_w.astype(low)
    patch_rows = small_low[:PATCH]
    time_rows = small_low[PATCH : PATCH + FREQ]
    head_rows = small_low[PATCH + FREQ :]
    moment_all = (all_times.astype(jnp.float32) + 0.5) / TSTEPS
    features = time_features(moment_all).astype(low)
    time_pre = jnp.dot(features, time_rows, preferred_element_type=jnp.float32)
    time_act = jax.nn.silu(time_pre).astype(low)
    cond_low = cond_w.astype(low)
    mod_low = mod_w.astype(low)
    onehot = all_labels[:, None] == jnp.arange(CLASSES)[None, :]
    cond = jnp.dot(
        time_act, cond_low[:model_width], preferred_element_type=jnp.float32
    ) + jnp.dot(onehot.astype(low), cond_low[model_width:], preferred_element_type=jnp.float32)
    cond_act = jax.nn.silu(cond).astype(low)
    modulation = lax.psum_scatter(
        jnp.dot(cond_act, mod_low, preferred_element_type=jnp.float32),
        "dp",
        scatter_dimension=0,
        tiled=True,
    )

    moment = (time_ids.astype(jnp.float32) + 0.5) / TSTEPS
    blended = ((1.0 - moment)[:, None, None] * latents + moment[:, None, None] * gaussian).astype(
        jnp.bfloat16
    )
    token_index = lax.axis_index("tensor") * half_rows + jnp.arange(half_rows)
    hidden = (
        jnp.einsum("bpn,pd->bnd", blended, patch_rows, preferred_element_type=jnp.float32)
        + position_table(token_index, model_width)[None]
    )
    saved_list = []
    fetched = []
    for layer_id in range(layer_count):
        packed = full[3 * layer_id]
        weights = (
            packed[:, : 3 * heads_wide].reshape(model_width, 3, heads_wide),
            packed[:, 3 * heads_wide :],
            full[3 * layer_id + 1],
            full[3 * layer_id + 2],
        )
        layer_mod = modulation[
            :, 6 * layer_id * model_width : (6 * layer_id + 6) * model_width
        ].reshape(samples, 6, model_width)
        hidden, saved_state = block_forward(hidden, layer_mod, weights)
        saved_list.append(saved_state)
        fetched.append(weights)
    final_mod = modulation[:, 6 * layer_count * model_width :].reshape(samples, 2, model_width)
    final_normed = modulated_norm(hidden, final_mod[:, 0], final_mod[:, 1]).astype(jnp.bfloat16)
    predicted = jnp.einsum(
        "bnd,pd->bpn", final_normed, head_rows, preferred_element_type=jnp.float32
    )
    time_weight = 0.5 + moment
    error = predicted - velocity
    loss_part = jnp.sum(time_weight[:, None, None] * error * error)
    total_count = samples * dp_count * half_rows * tensor_count * PATCH
    grad_pred = (time_weight[:, None, None] * (2.0 * error) / total_count).astype(jnp.bfloat16)
    grad_head = jnp.einsum(
        "bpn,bnd->pd", grad_pred, final_normed, preferred_element_type=jnp.float32
    )
    grad_final = jnp.einsum("bpn,pd->bnd", grad_pred, head_rows, preferred_element_type=jnp.float32)
    _, final_back = jax.vjp(modulated_norm, hidden, final_mod[:, 0], final_mod[:, 1])
    grad_hidden, grad_fshift, grad_fscale = final_back(grad_final)
    mod_grads = [None] * layer_count
    layer_grads = [None] * (3 * layer_count)
    for layer_id in reversed(range(layer_count)):
        layer_mod = modulation[
            :, 6 * layer_id * model_width : (6 * layer_id + 6) * model_width
        ].reshape(samples, 6, model_width)
        grad_hidden, grad_layer_mod, grads = block_backward(
            grad_hidden, layer_mod, fetched[layer_id], saved_list[layer_id]
        )
        layer_grads[3 * layer_id] = jnp.concatenate(
            [grads[0].reshape(model_width, 3 * heads_wide).astype(low), grads[1].astype(low)],
            axis=1,
        )
        layer_grads[3 * layer_id + 1] = grads[2].astype(low)
        layer_grads[3 * layer_id + 2] = grads[3].astype(low)
        mod_grads[layer_id] = grad_layer_mod.reshape(samples, 6 * model_width)
    flow = list(reversed(range(3 * layer_count)))
    if kernels:
        summed = reduce_grads([layer_grads[i] for i in flow], dp_count)
    else:
        summed = reduce_plain([layer_grads[i] for i in flow], dp_count)
    own_grads = [summed[flow.index(i)] for i in range(3 * layer_count)]

    grad_patch = jnp.einsum(
        "bpn,bnd->pd", blended, grad_hidden.astype(jnp.bfloat16), preferred_element_type=jnp.float32
    )
    all_mods = jnp.concatenate(
        mod_grads
        + [jnp.stack([grad_fshift, grad_fscale], axis=1).reshape(samples, 2 * model_width)],
        axis=1,
    )
    grad_mods = lax.all_gather(
        lax.psum(all_mods.astype(low), "tensor"), "dp", axis=0, tiled=True
    )
    grad_cond_act = jnp.einsum("be,de->bd", grad_mods, mod_low, preferred_element_type=jnp.float32)
    _, silu_back = jax.vjp(jax.nn.silu, cond)
    grad_cond = silu_back(grad_cond_act)[0]
    grad_temb = grad_cond.astype(low)
    grad_time_act = jnp.einsum(
        "be,de->bd", grad_temb, cond_low[:model_width], preferred_element_type=jnp.float32
    )
    grad_mod_w = jnp.einsum("bd,be->de", cond_act, grad_mods, preferred_element_type=jnp.float32)
    grad_table = jnp.einsum(
        "bc,bd->cd", onehot.astype(jnp.float32), grad_cond, precision=HIGHEST_PREC
    )
    grad_time_two = jnp.einsum("bd,be->de", time_act, grad_temb, preferred_element_type=jnp.float32)
    grad_cond_w = jnp.concatenate([grad_time_two, grad_table], axis=0)
    ends, grad_time_act, loss_sum = lax.psum(
        (
            jnp.concatenate([grad_patch, grad_head], axis=0),
            grad_time_act / tensor_count,
            loss_part,
        ),
        ("dp", "tensor"),
    )
    _, silu_back_two = jax.vjp(jax.nn.silu, time_pre)
    grad_pre = silu_back_two(grad_time_act)[0].astype(low)
    grad_time_one = jnp.einsum("bf,bd->fd", features, grad_pre, preferred_element_type=jnp.float32)
    grad_small = jnp.concatenate([ends[:PATCH], grad_time_one, ends[PATCH:]], axis=0)

    def stacked(kind):
        return jnp.stack([kind(i) for i in range(layer_count)])

    grads_list = [
        grad_small,
        grad_cond_w,
        grad_mod_w,
        stacked(lambda i: own_grads[3 * i][:, : 3 * heads_wide].reshape(rows, 3, heads_wide)),
        stacked(lambda i: own_grads[3 * i][:, 3 * heads_wide :].T),
        stacked(lambda i: own_grads[3 * i + 1]),
        stacked(lambda i: own_grads[3 * i + 2].T),
    ]
    weights_list = [small_w, cond_w, mod_w, qkv_w, proj_w, up_w, down_w]
    firsts_list = [small_m, cond_m, mod_m, qkv_m, proj_m, up_m, down_m]
    seconds_list = [small_v, cond_v, mod_v, qkv_v, proj_v, up_v, down_v]
    shares = [1.0 / (dp_count * tensor_count), 1.0 / tensor_count, 1.0 / tensor_count]
    shares = shares + [1.0] * 4

    def squares(arrays):
        sums = []
        for kind_id, a in enumerate(arrays):
            axes = None if kind_id < 3 else tuple(range(1, a.ndim))
            sums.append(jnp.sum(a * a, axis=axes).reshape(-1) * shares[kind_id])
        return jnp.concatenate(sums)

    results = [
        lamb_parts(weights_list[i], firsts_list[i], seconds_list[i], grads_list[i])
        for i in range(len(weights_list))
    ]
    updates = [r[2] for r in results]
    total_sq = lax.psum(
        jnp.stack([squares(weights_list), squares(updates)]), ("dp", "tensor")
    )
    norms = jnp.sqrt(total_sq + EPS_NORM)
    ratio = norms[0] / norms[1]
    outputs = []
    for kind_id in range(7):
        if kind_id < 3:
            factor = ratio[kind_id]
        else:
            first = 3 + (kind_id - 3) * layer_count
            factor = ratio[first : first + layer_count].reshape(
                (layer_count,) + (1,) * (weights_list[kind_id].ndim - 1)
            )
        outputs.append(weights_list[kind_id] - LEARN_RATE * factor * updates[kind_id])
        outputs.append(results[kind_id][0])
        outputs.append(results[kind_id][1])
    return tuple(outputs) + (loss_sum, norms)


def solution(mesh):
    return jax.shard_map(
        local,
        mesh=mesh,
        in_specs=(
            P("dp", None, "tensor"),
            P("dp", None, "tensor"),
            P("dp", None, "tensor"),
            P("dp"),
            P("dp"),
            P(),
            P(),
            P(),
            P(None, "dp"),
            P(None, "dp"),
            P(None, "dp"),
            P("dp", None),
            P("dp", None),
            P("dp", None),
            P(None, "dp", None, "tensor"),
            P(None, "dp", None, "tensor"),
            P(None, "dp", None, "tensor"),
            P(None, "tensor", "dp"),
            P(None, "tensor", "dp"),
            P(None, "tensor", "dp"),
            P(None, "dp", "tensor"),
            P(None, "dp", "tensor"),
            P(None, "dp", "tensor"),
            P(None, "tensor", "dp"),
            P(None, "tensor", "dp"),
            P(None, "tensor", "dp"),
        ),
        out_specs=(
            P(),
            P(),
            P(),
            P(None, "dp"),
            P(None, "dp"),
            P(None, "dp"),
            P("dp", None),
            P("dp", None),
            P("dp", None),
            P(None, "dp", None, "tensor"),
            P(None, "dp", None, "tensor"),
            P(None, "dp", None, "tensor"),
            P(None, "tensor", "dp"),
            P(None, "tensor", "dp"),
            P(None, "tensor", "dp"),
            P(None, "dp", "tensor"),
            P(None, "dp", "tensor"),
            P(None, "dp", "tensor"),
            P(None, "tensor", "dp"),
            P(None, "tensor", "dp"),
            P(None, "tensor", "dp"),
            P(),
            P(),
        ),
        check_vma=False,
    )
```

```python
import math

import jax
import jax.numpy as jnp
from jax import lax
from jax.experimental import pallas as pl
from jax.experimental.pallas import tpu as pltpu
from jax.sharding import PartitionSpec as P

HDIM = 64
PATCH = 16
GRID = 16
FREQ = 256
CLASSES = 1001
TSTEPS = 1000
STEP = 10


HIGHEST_PREC = lax.Precision.HIGHEST
BETA_ONE = 0.9
BETA_TWO = 0.999
EPS_ADAM = 1e-06
EPS_LAYER = 1e-06
EPS_NORM = 1e-12
WEIGHT_DECAY = 0.01
LEARN_RATE = 0.25


def time_features(moment):
    half_freq = FREQ // 2
    frequency = jnp.exp(-math.log(10000.0) * jnp.arange(half_freq).astype(jnp.float32) / half_freq)
    angles = (1000.0 * moment)[:, None] * frequency[None, :]
    return jnp.concatenate([jnp.cos(angles), jnp.sin(angles)], axis=1)


def position_table(token_index, model_width):
    quarter = model_width // 4
    omega_rate = 1.0 / 10000.0 ** (jnp.arange(quarter).astype(jnp.float32) / quarter)
    grid_row = (token_index // GRID).astype(jnp.float32)[:, None] * omega_rate[None, :]
    grid_col = (token_index % GRID).astype(jnp.float32)[:, None] * omega_rate[None, :]
    return jnp.concatenate(
        [jnp.sin(grid_col), jnp.cos(grid_col), jnp.sin(grid_row), jnp.cos(grid_row)], axis=1
    )


def modulated_norm(hidden_in, shift_vec, scale_vec):
    centre = hidden_in - jnp.mean(hidden_in, axis=-1, keepdims=True)
    spread = jnp.mean(centre * centre, axis=-1, keepdims=True)
    return (
        centre * lax.rsqrt(spread + EPS_LAYER) * (1.0 + scale_vec[:, None, :])
        + shift_vec[:, None, :]
    )


def lamb_parts(weight, first, second, grad):
    first_new = BETA_ONE * first + (1.0 - BETA_ONE) * grad
    second_new = BETA_TWO * second + (1.0 - BETA_TWO) * grad * grad
    update = (
        first_new
        / (1.0 - BETA_ONE**STEP)
        / (jnp.sqrt(second_new / (1.0 - BETA_TWO**STEP)) + EPS_ADAM)
        + WEIGHT_DECAY * weight
    )
    return (first_new, second_new, update)


def gelu_tanh(values_in):
    return jax.nn.gelu(values_in, approximate=True)


def spread_rows(part_rows):
    return lax.all_gather(part_rows, "tensor", axis=1, tiled=True)


def fold_rows(term_rows):
    return lax.psum_scatter(
        term_rows.astype(jnp.bfloat16), "tensor", scatter_dimension=1, tiled=True
    ).astype(jnp.float32)


def split_heads(gathered, w_qkv):
    mixed = jnp.einsum("bnd,dte->bnte", gathered, w_qkv, preferred_element_type=jnp.float32).astype(
        jnp.bfloat16
    )
    shaped = mixed.reshape(mixed.shape[0], mixed.shape[1], 3, -1, HDIM)
    return (shaped[:, :, 0], shaped[:, :, 1], shaped[:, :, 2])


def score_block(queries, key_heads):
    return jnp.einsum(
        "bnhe,bmhe->bhnm", queries, key_heads, preferred_element_type=jnp.float32
    ) * HDIM ** (-0.5)


def block_forward(hidden, layer_mod, weights):
    w_qkv, w_proj, w_up, w_down = weights
    normed = modulated_norm(hidden, layer_mod[:, 0], layer_mod[:, 1]).astype(jnp.bfloat16)
    gathered = spread_rows(normed)
    queries, key_heads, values = split_heads(gathered, w_qkv)
    scores = score_block(queries, key_heads)
    row_top = jnp.max(scores, axis=-1, keepdims=True)
    logsum = row_top + jnp.log(jnp.sum(jnp.exp(scores - row_top), axis=-1, keepdims=True))
    softmax_w = jnp.exp(scores - logsum).astype(jnp.bfloat16)
    attended = jnp.einsum(
        "bhnm,bmhe->bnhe", softmax_w, values, preferred_element_type=jnp.float32
    ).astype(jnp.bfloat16)
    attended = attended.reshape(attended.shape[0], attended.shape[1], -1)
    branch = fold_rows(
        jnp.einsum("bne,de->bnd", attended, w_proj, preferred_element_type=jnp.float32)
    )
    middle = hidden + layer_mod[:, 2][:, None, :] * branch
    normed_two = modulated_norm(middle, layer_mod[:, 3], layer_mod[:, 4]).astype(jnp.bfloat16)
    gathered_two = spread_rows(normed_two)
    inner_pre = jnp.einsum("bnd,df->bnf", gathered_two, w_up, preferred_element_type=jnp.float32)
    activ = gelu_tanh(inner_pre).astype(jnp.bfloat16)
    outer_out = fold_rows(
        jnp.einsum("bnf,df->bnd", activ, w_down, preferred_element_type=jnp.float32)
    )
    output = middle + layer_mod[:, 5][:, None, :] * outer_out
    saved_state = (
        hidden,
        gathered,
        queries,
        key_heads,
        values,
        attended,
        logsum,
        branch,
        middle,
        gathered_two,
        inner_pre,
        outer_out,
    )
    return (output, saved_state)


def block_backward(grad_out, layer_mod, weights, saved_state):
    (
        hidden,
        gathered,
        queries,
        key_heads,
        values,
        attended,
        logsum,
        branch,
        middle,
        gathered_two,
        inner_pre,
        outer_out,
    ) = saved_state
    w_qkv, w_proj, w_up, w_down = weights
    grad_gate_m = jnp.sum(grad_out * outer_out, axis=1)
    grad_outer = spread_rows((layer_mod[:, 5][:, None, :] * grad_out).astype(jnp.bfloat16))
    activ = gelu_tanh(inner_pre).astype(jnp.bfloat16)
    grad_down = jnp.einsum("bnd,bnf->df", grad_outer, activ, preferred_element_type=jnp.float32)
    grad_activ = jnp.einsum("bnd,df->bnf", grad_outer, w_down, preferred_element_type=jnp.float32)
    _, gelu_back = jax.vjp(gelu_tanh, inner_pre)
    grad_inner = gelu_back(grad_activ)[0].astype(jnp.bfloat16)
    grad_up = jnp.einsum(
        "bnd,bnf->df", gathered_two, grad_inner, preferred_element_type=jnp.float32
    )
    grad_normed_two = fold_rows(
        jnp.einsum("bnf,df->bnd", grad_inner, w_up, preferred_element_type=jnp.float32)
    )
    _, norm_back = jax.vjp(modulated_norm, middle, layer_mod[:, 3], layer_mod[:, 4])
    grad_middle, grad_shift_m, grad_scale_m = norm_back(grad_normed_two)
    grad_middle = grad_middle + grad_out
    grad_gate_a = jnp.sum(grad_middle * branch, axis=1)
    grad_branch = spread_rows((layer_mod[:, 2][:, None, :] * grad_middle).astype(jnp.bfloat16))
    grad_proj = jnp.einsum("bnd,bne->de", grad_branch, attended, preferred_element_type=jnp.float32)
    grad_att = jnp.einsum(
        "bnd,de->bne", grad_branch, w_proj, preferred_element_type=jnp.float32
    ).astype(jnp.bfloat16)
    grad_att = grad_att.reshape(queries.shape)
    scores = score_block(queries, key_heads)
    soft_float = jnp.exp(scores - logsum)
    softmax_w = soft_float.astype(jnp.bfloat16)
    grad_values = jnp.einsum(
        "bhnm,bnhe->bmhe", softmax_w, grad_att, preferred_element_type=jnp.float32
    ).astype(jnp.bfloat16)
    grad_soft = jnp.einsum("bnhe,bmhe->bhnm", grad_att, values, preferred_element_type=jnp.float32)
    row_delta = jnp.sum(soft_float * grad_soft, axis=-1, keepdims=True)
    grad_scores = (soft_float * (grad_soft - row_delta)).astype(jnp.bfloat16)
    grad_queries = (
        jnp.einsum("bhnm,bmhe->bnhe", grad_scores, key_heads, preferred_element_type=jnp.float32)
        * HDIM ** (-0.5)
    ).astype(jnp.bfloat16)
    grad_keys = (
        jnp.einsum("bhnm,bnhe->bmhe", grad_scores, queries, preferred_element_type=jnp.float32)
        * HDIM ** (-0.5)
    ).astype(jnp.bfloat16)
    grad_mixed = jnp.stack([grad_queries, grad_keys, grad_values], axis=2)
    grad_mixed = grad_mixed.reshape(grad_mixed.shape[0], grad_mixed.shape[1], 3, -1)
    grad_qkv = jnp.einsum("bnd,bnte->dte", gathered, grad_mixed, preferred_element_type=jnp.float32)
    grad_normed = fold_rows(
        jnp.einsum("bnte,dte->bnd", grad_mixed, w_qkv, preferred_element_type=jnp.float32)
    )
    _, norm_back_two = jax.vjp(modulated_norm, hidden, layer_mod[:, 0], layer_mod[:, 1])
    grad_hidden, grad_shift_a, grad_scale_a = norm_back_two(grad_normed)
    grad_hidden = grad_hidden + grad_middle
    grad_layer_mod = jnp.stack(
        [grad_shift_a, grad_scale_a, grad_gate_a, grad_shift_m, grad_scale_m, grad_gate_m], axis=1
    )
    return (grad_hidden, grad_layer_mod, (grad_qkv, grad_proj, grad_up, grad_down))


ORDERS = ((0, 1, 2), (0, 2, 1))
MESH_ID = pl.DeviceIdType.MESH
NN = (((1,), (0,)), ((), ()))
NT = (((1,), (1,)), ((), ()))
TN = (((0,), (0,)), ((), ()))


def grid_of(dp_count):
    if dp_count == 16:
        return (4, 2, 2)
    sizes = [1, 1, 1]
    rest, prime = dp_count, 2
    while rest > 1:
        while rest % prime == 0:
            sizes[sizes.index(min(sizes))] *= prime
            rest //= prime
        prime += 1
    return tuple(sorted(sizes, reverse=True))


def place(sizes):
    index = lax.axis_index("dp")
    return (index // (sizes[1] * sizes[2]), index // sizes[2] % sizes[1], index % sizes[2])


def peer_of(sizes, spot, axis, other):
    moved = [other if a == axis else spot[a] for a in range(3)]
    return (moved[0] * sizes[1] + moved[1]) * sizes[2] + moved[2], lax.axis_index("tensor")


def dot(left, right, form):
    return lax.dot_general(left, right, form, preferred_element_type=jnp.float32)


def greet(peers):
    barrier = pltpu.get_barrier_semaphore()
    for peer in peers:
        pl.semaphore_signal(barrier, inc=1, device_id=peer, device_id_type=MESH_ID)
    pl.semaphore_wait(barrier, len(peers))


def axis_peers(sizes, spot):
    peers = []
    for axis in range(3):
        for offset in range(1, sizes[axis]):
            peers.append(peer_of(sizes, spot, axis, (spot[axis] + offset) % sizes[axis]))
    return peers


def norm_parts(x):
    centre = x - jnp.mean(x, axis=-1, keepdims=True)
    spread = jnp.mean(centre * centre, axis=-1, keepdims=True)
    rstd = lax.rsqrt(spread + EPS_LAYER)
    return centre * rstd, rstd


def norm_forward(x, shift, scale):
    return (norm_parts(x)[0] * (1.0 + scale) + shift).astype(jnp.bfloat16)


def norm_backward(x, scale, dy):
    xh, rstd = norm_parts(x)
    dxh = dy * (1.0 + scale)
    dx = (
        dxh
        - jnp.mean(dxh, axis=-1, keepdims=True)
        - xh * jnp.mean(dxh * xh, axis=-1, keepdims=True)
    ) * rstd
    return dx, jnp.sum(dy, axis=0, keepdims=True), jnp.sum(dy * xh, axis=0, keepdims=True)


GELU_C = math.sqrt(2.0 / math.pi)


def step_kernel(sizes, layers, total_count, *refs):
    (
        blob,
        hidden_in,
        mod,
        velocity,
        time_weight,
        blended,
        head_rows,
        own_grads,
        mod_grads,
        ends,
        loss_out,
        full,
        got_one,
        got_two,
        got_three,
        gathered,
        grad_spread,
        outbox,
        inbox,
        qkv,
        attended,
        hidden,
        middle,
        branch,
        outer,
        inner,
        act,
        grad_inner,
        grad_mixed,
        resid,
        part,
        turned,
        ag_send,
        ag_recv,
        rs_send,
        rs_recv,
        pair_send,
        pair_recv,
        own_sem,
    ) = refs
    low = jnp.bfloat16
    spot = place(sizes)
    my_dp, my_core = lax.axis_index("dp"), lax.axis_index("tensor")
    partner = (my_dp, 1 - my_core)
    waves, rows, columns = blob.shape
    half = columns // 2
    samples, half_rows, width = hidden_in.shape
    tokens = 2 * half_rows
    heads_wide = qkv.shape[3] // 3
    pairs = heads_wide // (2 * HDIM)
    mine = pl.ds(pl.multiple_of(my_core * half_rows, half_rows), half_rows)
    theirs = pl.ds(pl.multiple_of((1 - my_core) * half_rows, half_rows), half_rows)
    tile = 512

    own = pltpu.make_async_copy(blob, full.at[:, spot[0], spot[1], spot[2]], own_sem)
    own.start()
    greet(axis_peers(sizes, spot) + [partner])

    unsent = []

    def gather_copies(wave, order_id, phase):
        order = ORDERS[order_id]
        axis = order[phase]
        pick = [spot[a] for a in range(3)]
        for earlier in order[:phase]:
            pick[earlier] = slice(None)
        lanes = pl.ds(order_id * half, half)
        target = full.at[wave, pick[0], pick[1], pick[2], :, lanes]
        source = blob.at[wave, :, lanes] if phase == 0 else target
        return [
            pltpu.make_async_remote_copy(
                src_ref=source,
                dst_ref=target,
                send_sem=ag_send.at[wave, order_id, phase, offset],
                recv_sem=ag_recv.at[wave, order_id, phase, offset],
                device_id=peer_of(sizes, spot, axis, (spot[axis] + offset) % sizes[axis]),
                device_id_type=MESH_ID,
            )
            for offset in range(1, sizes[axis])
        ]

    def gather_step(step):
        for phase in reversed(range(4)):
            wave = step - phase
            if not 0 <= wave < waves:
                continue
            for order_id in range(2):
                if phase > 0:
                    for copy in gather_copies(wave, order_id, phase - 1):
                        copy.wait_recv()
                if wave == 0 and phase == 1 and order_id == 0:
                    own.wait()
                if phase < 3:
                    for copy in gather_copies(wave, order_id, phase):
                        copy.start()
                        unsent.append(copy)

    inboxes = (got_one, got_two, got_three)
    rs_unsent = []

    def reduce_copies(wave, order_id, phase):
        order = ORDERS[order_id][::-1]
        axis = order[phase]
        lanes = pl.ds(order_id * half, half)
        made = []
        for offset in range(1, sizes[axis]):
            other = (spot[axis] + offset) % sizes[axis]
            pick = [slice(None)] * 3
            for earlier in order[:phase]:
                pick[earlier] = spot[earlier]
            pick[axis] = other
            made.append(
                pltpu.make_async_remote_copy(
                    src_ref=full.at[wave, pick[0], pick[1], pick[2], :, lanes],
                    dst_ref=inboxes[phase].at[wave, order_id, offset - 1],
                    send_sem=rs_send.at[wave, order_id, phase, offset],
                    recv_sem=rs_recv.at[wave, order_id, phase, offset],
                    device_id=peer_of(sizes, spot, axis, other),
                    device_id_type=MESH_ID,
                )
            )
        return made

    def reduce_send(wave, phase):
        for order_id in range(2):
            for copy in reduce_copies(wave, order_id, phase):
                copy.start()
                rs_unsent.append(copy)

    def reduce_absorb(wave, phase):
        for order_id in range(2):
            for copy in reduce_copies(wave, order_id, phase):
                copy.wait_recv()
            order = ORDERS[order_id][::-1]
            lanes = pl.ds(order_id * half, half)
            box = inboxes[phase]
            peers = sizes[order[phase]] - 1
            left = sorted(order[phase + 1 :])
            if not left:
                total = full[wave, spot[0], spot[1], spot[2], :, lanes].astype(jnp.float32)
                for p in range(peers):
                    total = total + box[wave, order_id, p].astype(jnp.float32)
                own_grads[wave, :, lanes] = total
                continue
            span = math.prod(sizes[a] for a in left)

            def body(step, carry, order_id=order_id, left=left, box=box, peers=peers, lanes=lanes):
                index = (step,) if len(left) == 1 else (step // sizes[left[1]], step % sizes[left[1]])
                pick = list(spot)
                for a, i in zip(left, index):
                    pick[a] = i
                total = full[wave, pick[0], pick[1], pick[2], :, lanes].astype(jnp.float32)
                for p in range(peers):
                    total = total + box[(wave, order_id, p) + index].astype(jnp.float32)
                full[wave, pick[0], pick[1], pick[2], :, lanes] = total.astype(low)
                return carry

            lax.fori_loop(0, span, body, 0)

    def reduce_advance(wave, phase):
        reduce_absorb(wave, phase - 1)
        if phase < 3:
            reduce_send(wave, phase)

    def spread_copy(buffer, slot, stage, b):
        return pltpu.make_async_remote_copy(
            src_ref=buffer.at[slot, b, mine],
            dst_ref=buffer.at[slot, b, mine],
            send_sem=pair_send.at[stage, b],
            recv_sem=pair_recv.at[stage, b],
            device_id=partner,
            device_id_type=MESH_ID,
        )

    def spread(buffer, slot, stage, b, value):
        buffer[slot, b, mine] = value
        spread_copy(buffer, slot, stage, b).start()

    def fold_copy(slot, stage, b):
        return pltpu.make_async_remote_copy(
            src_ref=outbox.at[slot, b],
            dst_ref=inbox.at[slot, b],
            send_sem=pair_send.at[stage, b],
            recv_sem=pair_recv.at[stage, b],
            device_id=partner,
            device_id_type=MESH_ID,
        )

    def fold(slot, stage, b, value):
        part[b] = value
        outbox[slot, b] = part[b, theirs].astype(low)
        fold_copy(slot, stage, b).start()

    def folded(slot, stage, b):
        fold_copy(slot, stage, b).wait_recv()
        return part[b, mine] + inbox[slot, b].astype(jnp.float32)

    pair_stages = []

    def each_sample(body):
        lax.fori_loop(0, samples, lambda b, carry: (body(b), carry)[1], 0)

    def weight(wave):
        return full[wave].reshape(width, columns)

    def weight_lanes(wave, lanes, count):
        return full[wave, :, :, :, :, lanes].reshape(width, count)

    def vec(b, row):
        return mod[b, row : row + 1]

    lane = lax.broadcasted_iota(jnp.int32, (1, 2 * HDIM), 1)
    first_head = lane < HDIM
    keep = (
        jnp.where(first_head, 1.0, 0.0).astype(low),
        jnp.where(first_head, 0.0, 1.0).astype(low),
    )
    factor = HDIM ** (-0.5)

    def pair_lanes(kind, p):
        return pl.ds(kind * heads_wide + p * 2 * HDIM, 2 * HDIM)

    gather_step(0)
    gather_step(1)
    gather_step(2)
    for layer in range(layers):
        row = 6 * layer
        sa, sb, sc, sd = (8 * layer + i for i in range(4))
        pair_stages += [
            (lambda b, s=sa, g=2 * layer: spread_copy(gathered, g, s, b)),
            (lambda b, s=sb, g=4 * layer: fold_copy(g, s, b)),
            (lambda b, s=sc, g=2 * layer + 1: spread_copy(gathered, g, s, b)),
            (lambda b, s=sd, g=4 * layer + 1: fold_copy(g, s, b)),
        ]

        def first(b):
            if layer == 0:
                x = hidden_in[b]
            else:
                x = middle[layer - 1, b] + vec(b, row - 1) * outer[layer - 1, b]
            hidden[layer, b] = x
            spread(gathered, 2 * layer, sa, b, norm_forward(x, vec(b, row), vec(b, row + 1)))

        each_sample(first)
        gather_step(3 * layer + 3)

        def attention(b):
            spread_copy(gathered, 2 * layer, sa, b).wait_recv()
            for kind in range(3):
                lanes = pl.ds(kind * heads_wide, heads_wide)
                qkv[layer, b, :, lanes] = dot(
                    gathered[2 * layer, b], weight_lanes(3 * layer, lanes, heads_wide), NN
                ).astype(low)
            for p in range(pairs):
                q = qkv[layer, b, :, pair_lanes(0, p)]
                k = qkv[layer, b, :, pair_lanes(1, p)]
                v = qkv[layer, b, :, pair_lanes(2, p)]
                got = []
                for h in range(2):
                    s = dot(q, k * keep[h], NT) * factor
                    e = jnp.exp(s - jnp.max(s, axis=-1, keepdims=True))
                    e = e / jnp.sum(e, axis=-1, keepdims=True)
                    got.append(dot(e.astype(low), v, NN))
                attended[layer, b, :, pl.ds(p * 2 * HDIM, 2 * HDIM)] = jnp.where(
                    first_head, got[0], got[1]
                ).astype(low)
            fold(
                4 * layer,
                sb,
                b,
                dot(
                    attended[layer, b],
                    weight_lanes(3 * layer, pl.ds(3 * heads_wide, heads_wide), heads_wide),
                    NT,
                ),
            )

        each_sample(attention)

        def second(b):
            got = folded(4 * layer, sb, b)
            branch[layer, b] = got
            x = hidden[layer, b] + vec(b, row + 2) * got
            middle[layer, b] = x
            spread(gathered, 2 * layer + 1, sc, b, norm_forward(x, vec(b, row + 3), vec(b, row + 4)))

        each_sample(second)
        gather_step(3 * layer + 4)

        def widen(b):
            spread_copy(gathered, 2 * layer + 1, sc, b).wait_recv()

            def body(n, carry):
                lanes = pl.ds(pl.multiple_of(n * tile, tile), tile)
                x = dot(gathered[2 * layer + 1, b], weight_lanes(3 * layer + 1, lanes, tile), NN)
                inner[b, :, lanes] = x
                t = jnp.tanh(GELU_C * (x + 0.044715 * x * x * x))
                act[b, :, lanes] = (0.5 * x * (1.0 + t)).astype(low)
                return carry

            lax.fori_loop(0, columns // tile, body, 0)

        each_sample(widen)
        gather_step(3 * layer + 5)

        def narrow(b):
            fold(4 * layer + 1, sd, b, dot(act[b], weight(3 * layer + 2), NT))

        each_sample(narrow)

        def third(b):
            outer[layer, b] = folded(4 * layer + 1, sd, b)

        each_sample(third)

    for copy in unsent:
        copy.wait_send()

    last = layers - 1
    loss_out[...] = jnp.zeros_like(loss_out)
    ends[...] = jnp.zeros_like(ends)
    pad = pl.ds(PATCH, PATCH)

    def head(b):
        x = middle[last, b] + vec(b, 6 * layers - 1) * outer[last, b]
        shift, scale = vec(b, 6 * layers), vec(b, 6 * layers + 1)
        xh, _ = norm_parts(x)
        normed = (xh * (1.0 + scale) + shift).astype(low)
        predicted = dot(head_rows[...], normed, NT)
        error = predicted - velocity[b]
        weighted = time_weight[b] * error
        loss_out[...] += jnp.sum(weighted * error, axis=0, keepdims=True)
        grad_pred = (2.0 * weighted / total_count).astype(low)
        ends[pad, :] += dot(grad_pred, normed, NN)
        dx, gshift, gscale = norm_backward(x, scale, dot(grad_pred, head_rows[...], TN))
        mod_grads[b, 6 * layers : 6 * layers + 1] = gshift
        mod_grads[b, 6 * layers + 1 : 6 * layers + 2] = gscale
        resid[b] = dx

    each_sample(head)

    def weight_grad(wave, left, right_of, spans):
        turned[...] = left.reshape(samples * tokens, width).T

        def body(n, carry):
            start, count = spans
            lanes = pl.ds(pl.multiple_of(start + n * count, 128), count)
            got = dot(turned[...], right_of(pl.ds(pl.multiple_of(n * count, 128), count), count), NN)
            full[wave, :, :, :, :, lanes] = got.astype(low).reshape(sizes + (rows, count))
            return carry

        return body

    started = []

    def pump():
        for entry in started:
            if entry[1] <= 3:
                reduce_advance(entry[0], entry[1])
                entry[1] += 1

    for layer in reversed(range(layers)):
        row = 6 * layer
        se, sf, sg, sh = (8 * layer + 4 + i for i in range(4))
        pair_stages += [
            (lambda b, s=se, g=2 * layer: spread_copy(grad_spread, g, s, b)),
            (lambda b, s=sf, g=4 * layer + 2: fold_copy(g, s, b)),
            (lambda b, s=sg, g=2 * layer + 1: spread_copy(grad_spread, g, s, b)),
            (lambda b, s=sh, g=4 * layer + 3: fold_copy(g, s, b)),
        ]

        def grad_first(b):
            g = resid[b]
            mod_grads[b, row + 5 : row + 6] = jnp.sum(g * outer[layer, b], axis=0, keepdims=True)
            spread(grad_spread, 2 * layer, se, b, (vec(b, row + 5) * g).astype(low))

        each_sample(grad_first)

        def grad_wide(b):
            spread_copy(grad_spread, 2 * layer, se, b).wait_recv()

            def body(n, carry):
                lanes = pl.ds(pl.multiple_of(n * tile, tile), tile)
                if layer == last:
                    x = inner[b, :, lanes]
                else:
                    x = dot(
                        gathered[2 * layer + 1, b], weight_lanes(3 * layer + 1, lanes, tile), NN
                    )
                g = dot(grad_spread[2 * layer, b], weight_lanes(3 * layer + 2, lanes, tile), NN)
                t = jnp.tanh(GELU_C * (x + 0.044715 * x * x * x))
                if layer != last:
                    act[b, :, lanes] = (0.5 * x * (1.0 + t)).astype(low)
                slope = 0.5 * (1.0 + t) + 0.5 * x * (1.0 - t * t) * (
                    GELU_C * (1.0 + 3.0 * 0.044715 * x * x)
                )
                grad_inner[b, :, lanes] = (g * slope).astype(low)
                return carry

            lax.fori_loop(0, columns // tile, body, 0)
            fold(4 * layer + 2, sf, b, dot(grad_inner[b], weight(3 * layer + 1), NT))

        each_sample(grad_wide)

        def wide_of(source):
            def right_of(lanes, count):
                return source[:, :, lanes].reshape(samples * tokens, count)

            return right_of

        lax.fori_loop(
            0,
            columns // tile,
            weight_grad(3 * layer + 2, grad_spread[2 * layer], wide_of(act), (0, tile)),
            0,
        )
        reduce_send(3 * layer + 2, 0)
        lax.fori_loop(
            0,
            columns // tile,
            weight_grad(3 * layer + 1, gathered[2 * layer + 1], wide_of(grad_inner), (0, tile)),
            0,
        )
        reduce_send(3 * layer + 1, 0)

        def grad_second(b):
            dy = folded(4 * layer + 2, sf, b)
            dx, gshift, gscale = norm_backward(middle[layer, b], vec(b, row + 4), dy)
            g = dx + resid[b]
            resid[b] = g
            mod_grads[b, row + 3 : row + 4] = gshift
            mod_grads[b, row + 4 : row + 5] = gscale
            mod_grads[b, row + 2 : row + 3] = jnp.sum(g * branch[layer, b], axis=0, keepdims=True)
            spread(grad_spread, 2 * layer + 1, sg, b, (vec(b, row + 2) * g).astype(low))

        each_sample(grad_second)
        pump()
        started.append([3 * layer + 2, 1])
        started.append([3 * layer + 1, 1])

        def grad_attention(b):
            spread_copy(grad_spread, 2 * layer + 1, sg, b).wait_recv()
            got_all = dot(
                grad_spread[2 * layer + 1, b],
                weight_lanes(3 * layer, pl.ds(3 * heads_wide, heads_wide), heads_wide),
                NN,
            ).astype(low)
            for p in range(pairs):
                ga = got_all[:, p * 2 * HDIM : (p + 1) * 2 * HDIM]
                q = qkv[layer, b, :, pair_lanes(0, p)]
                k = qkv[layer, b, :, pair_lanes(1, p)]
                v = qkv[layer, b, :, pair_lanes(2, p)]
                gq, gk, gv = [], [], []
                for h in range(2):
                    s = dot(k * keep[h], q, NT) * factor
                    e = jnp.exp(s - jnp.max(s, axis=0, keepdims=True))
                    e = e / jnp.sum(e, axis=0, keepdims=True)
                    dp = dot(v * keep[h], ga, NT)
                    ds = (e * (dp - jnp.sum(e * dp, axis=0, keepdims=True))).astype(low)
                    gv.append(dot(e.astype(low), ga, NN))
                    gk.append(dot(ds, q, NN))
                    gq.append(dot(ds, k, TN))
                for kind, got, scale in ((0, gq, factor), (1, gk, factor), (2, gv, 1.0)):
                    grad_mixed[b, :, pair_lanes(kind, p)] = (
                        jnp.where(first_head, got[0], got[1]) * scale
                    ).astype(low)
            fold(
                4 * layer + 3,
                sh,
                b,
                dot(
                    grad_mixed[b],
                    weight_lanes(3 * layer, pl.ds(0, 3 * heads_wide), 3 * heads_wide),
                    NT,
                ),
            )

        each_sample(grad_attention)
        lax.fori_loop(
            0,
            3,
            weight_grad(3 * layer, gathered[2 * layer], wide_of(grad_mixed), (0, heads_wide)),
            0,
        )
        lax.fori_loop(
            0,
            1,
            weight_grad(
                3 * layer,
                grad_spread[2 * layer + 1],
                wide_of(attended.at[layer]),
                (3 * heads_wide, heads_wide),
            ),
            0,
        )
        reduce_send(3 * layer, 0)
        pump()
        started.append([3 * layer, 1])

        def grad_third(b):
            dy = folded(4 * layer + 3, sh, b)
            dx, gshift, gscale = norm_backward(hidden[layer, b], vec(b, row + 1), dy)
            resid[b] = dx + resid[b]
            mod_grads[b, row : row + 1] = gshift
            mod_grads[b, row + 1 : row + 2] = gscale

        each_sample(grad_third)

    def patch(b):
        ends[pl.ds(0, PATCH), :] += dot(blended[b], resid[b].astype(low), NN)

    each_sample(patch)
    for _ in range(3):
        pump()
    for copy in rs_unsent:
        copy.wait_send()

    def finish(b):
        for stage in pair_stages:
            stage(b).wait_send()

    each_sample(finish)


def train_step(blob, hidden, mod, velocity, time_weight, blended, head_rows, dp_count, layers, total):
    sizes = grid_of(dp_count)
    waves, rows, columns = blob.shape
    samples, half_rows, width = hidden.shape
    tokens = 2 * half_rows
    half = columns // 2
    heads_wide = columns // 4
    most = max(sizes)
    low, wide = jnp.bfloat16, jnp.float32
    in_vmem = pl.BlockSpec(memory_space=pltpu.VMEM)
    stages = 8 * layers
    resid_shape = (layers, samples, half_rows, width)
    dma = pltpu.SemaphoreType.DMA
    return pl.pallas_call(
        lambda *refs: step_kernel(sizes, layers, total, *refs),
        out_shape=(
            jax.ShapeDtypeStruct((waves, rows, columns), wide),
            jax.ShapeDtypeStruct(mod.shape, wide),
            jax.ShapeDtypeStruct((2 * PATCH, width), wide),
            jax.ShapeDtypeStruct((8, half_rows), wide),
        ),
        in_specs=[pl.BlockSpec(memory_space=pl.ANY)] + [in_vmem] * 6,
        out_specs=(in_vmem,) * 4,
        scratch_shapes=[
            pltpu.VMEM((waves,) + sizes + (rows, columns), low),
            pltpu.VMEM((waves, 2, sizes[2] - 1, sizes[0], sizes[1], rows, half), low),
            pltpu.VMEM((waves, 2, sizes[1] - 1, sizes[0], rows, half), low),
            pltpu.VMEM((waves, 2, sizes[0] - 1, rows, half), low),
            pltpu.VMEM((2 * layers, samples, tokens, width), low),
            pltpu.VMEM((2 * layers, samples, tokens, width), low),
            pltpu.VMEM((4 * layers, samples, half_rows, width), low),
            pltpu.VMEM((4 * layers, samples, half_rows, width), low),
            pltpu.VMEM((layers, samples, tokens, 3 * heads_wide), low),
            pltpu.VMEM((layers, samples, tokens, heads_wide), low),
            pltpu.VMEM(resid_shape, wide),
            pltpu.VMEM(resid_shape, wide),
            pltpu.VMEM(resid_shape, wide),
            pltpu.VMEM(resid_shape, wide),
            pltpu.VMEM((samples, tokens, columns), wide),
            pltpu.VMEM((samples, tokens, columns), low),
            pltpu.VMEM((samples, tokens, columns), low),
            pltpu.VMEM((samples, tokens, 3 * heads_wide), low),
            pltpu.VMEM((samples, half_rows, width), wide),
            pltpu.VMEM((samples, tokens, width), wide),
            pltpu.VMEM((width, samples * tokens), low),
            dma((waves, 2, 3, most)),
            dma((waves, 2, 3, most)),
            dma((waves, 2, 3, most)),
            dma((waves, 2, 3, most)),
            dma((stages, samples)),
            dma((stages, samples)),
            dma,
        ],
        compiler_params=pltpu.CompilerParams(
            collective_id=0, has_side_effects=True, vmem_limit_bytes=64 * 2**20 - 2**17
        ),
    )(blob, hidden, mod, velocity, time_weight, blended, head_rows)


def gather_plain(blob, dp_count):
    waves, rows, columns = blob.shape
    return lax.all_gather(blob, "dp", axis=1, tiled=True)


def reduce_plain(grads, dp_count):
    return jnp.stack(
        [
            lax.psum_scatter(g.astype(jnp.float32), "dp", scatter_dimension=0, tiled=True)
            for g in grads
        ]
    )


def local(
    latents,
    gaussian,
    velocity,
    time_ids,
    labels,
    small_w,
    small_m,
    small_v,
    cond_w,
    cond_m,
    cond_v,
    mod_w,
    mod_m,
    mod_v,
    qkv_w,
    qkv_m,
    qkv_v,
    proj_w,
    proj_m,
    proj_v,
    up_w,
    up_m,
    up_v,
    down_w,
    down_m,
    down_v,
):
    layer_count = qkv_w.shape[0]
    model_width = mod_w.shape[1] // (6 * layer_count + 2)
    dp_count = lax.axis_size("dp")
    tensor_count = lax.axis_size("tensor")
    samples = latents.shape[0]
    half_rows = latents.shape[2]
    rows = qkv_w.shape[1]
    kernels = rows % 16 == 0
    my_dp = lax.axis_index("dp")
    low = jnp.bfloat16

    parts = []
    for i in range(layer_count):
        parts.append(
            jnp.concatenate(
                [qkv_w[i, :, 0], qkv_w[i, :, 1], qkv_w[i, :, 2], proj_w[i].T], axis=1
            ).astype(low)
        )
        parts.append(up_w[i].astype(low))
        parts.append(down_w[i].T.astype(low))
    blob = jnp.stack(parts)
    heads_wide = qkv_w.shape[3]

    ids = lax.all_gather(jnp.stack([time_ids, labels]), "dp", axis=1, tiled=True)
    all_times, all_labels = ids[0], ids[1]
    small_low = small_w.astype(low)
    patch_rows = small_low[:PATCH]
    time_rows = small_low[PATCH : PATCH + FREQ]
    head_rows = small_low[PATCH + FREQ :]
    moment_all = (all_times.astype(jnp.float32) + 0.5) / TSTEPS
    features = time_features(moment_all).astype(low)
    time_pre = jnp.dot(features, time_rows, preferred_element_type=jnp.float32)
    time_act = jax.nn.silu(time_pre).astype(low)
    cond_low = cond_w.astype(low)
    mod_low = mod_w.astype(low)
    onehot = all_labels[:, None] == jnp.arange(CLASSES)[None, :]
    cond = jnp.dot(
        time_act, cond_low[:model_width], preferred_element_type=jnp.float32
    ) + jnp.dot(onehot.astype(low), cond_low[model_width:], preferred_element_type=jnp.float32)
    cond_act = jax.nn.silu(cond).astype(low)
    modulation = lax.psum_scatter(
        jnp.dot(cond_act, mod_low, preferred_element_type=jnp.float32),
        "dp",
        scatter_dimension=0,
        tiled=True,
    )

    moment = (time_ids.astype(jnp.float32) + 0.5) / TSTEPS
    blended = ((1.0 - moment)[:, None, None] * latents + moment[:, None, None] * gaussian).astype(
        jnp.bfloat16
    )
    token_index = lax.axis_index("tensor") * half_rows + jnp.arange(half_rows)
    hidden = (
        jnp.einsum("bpn,pd->bnd", blended, patch_rows, preferred_element_type=jnp.float32)
        + position_table(token_index, model_width)[None]
    )
    time_weight = 0.5 + moment
    total_count = samples * dp_count * half_rows * tensor_count * PATCH
    if kernels:
        table = modulation.reshape(samples, -1, model_width)
        own_grads, all_mods, ends, loss_rows = train_step(
            blob,
            hidden,
            jnp.pad(table, ((0, 0), (0, 2), (0, 0))),
            velocity,
            jnp.broadcast_to(time_weight[:, None, None], velocity.shape),
            blended,
            head_rows,
            dp_count,
            layer_count,
            float(total_count),
        )
        loss_part = jnp.sum(loss_rows[0])
        all_mods = all_mods[:, : table.shape[1]].reshape(samples, -1)
    else:
        full = gather_plain(blob, dp_count)
        saved_list = []
        fetched = []
        for layer_id in range(layer_count):
            packed = full[3 * layer_id]
            weights = (
                packed[:, : 3 * heads_wide].reshape(model_width, 3, heads_wide),
                packed[:, 3 * heads_wide :],
                full[3 * layer_id + 1],
                full[3 * layer_id + 2],
            )
            layer_mod = modulation[
                :, 6 * layer_id * model_width : (6 * layer_id + 6) * model_width
            ].reshape(samples, 6, model_width)
            hidden, saved_state = block_forward(hidden, layer_mod, weights)
            saved_list.append(saved_state)
            fetched.append(weights)
        final_mod = modulation[:, 6 * layer_count * model_width :].reshape(samples, 2, model_width)
        final_normed = modulated_norm(hidden, final_mod[:, 0], final_mod[:, 1]).astype(jnp.bfloat16)
        predicted = jnp.einsum(
            "bnd,pd->bpn", final_normed, head_rows, preferred_element_type=jnp.float32
        )
        error = predicted - velocity
        loss_part = jnp.sum(time_weight[:, None, None] * error * error)
        grad_pred = (time_weight[:, None, None] * (2.0 * error) / total_count).astype(jnp.bfloat16)
        grad_head = jnp.einsum(
            "bpn,bnd->pd", grad_pred, final_normed, preferred_element_type=jnp.float32
        )
        grad_final = jnp.einsum("bpn,pd->bnd", grad_pred, head_rows, preferred_element_type=jnp.float32)
        _, final_back = jax.vjp(modulated_norm, hidden, final_mod[:, 0], final_mod[:, 1])
        grad_hidden, grad_fshift, grad_fscale = final_back(grad_final)
        mod_grads = [None] * layer_count
        layer_grads = [None] * (3 * layer_count)
        for layer_id in reversed(range(layer_count)):
            layer_mod = modulation[
                :, 6 * layer_id * model_width : (6 * layer_id + 6) * model_width
            ].reshape(samples, 6, model_width)
            grad_hidden, grad_layer_mod, grads = block_backward(
                grad_hidden, layer_mod, fetched[layer_id], saved_list[layer_id]
            )
            layer_grads[3 * layer_id] = jnp.concatenate(
                [grads[0].reshape(model_width, 3 * heads_wide).astype(low), grads[1].astype(low)],
                axis=1,
            )
            layer_grads[3 * layer_id + 1] = grads[2].astype(low)
            layer_grads[3 * layer_id + 2] = grads[3].astype(low)
            mod_grads[layer_id] = grad_layer_mod.reshape(samples, 6 * model_width)
        own_grads = reduce_plain(layer_grads, dp_count)
        grad_patch = jnp.einsum(
            "bpn,bnd->pd", blended, grad_hidden.astype(jnp.bfloat16), preferred_element_type=jnp.float32
        )
        ends = jnp.concatenate([grad_patch, grad_head], axis=0)
        all_mods = jnp.concatenate(
            mod_grads
            + [jnp.stack([grad_fshift, grad_fscale], axis=1).reshape(samples, 2 * model_width)],
            axis=1,
        )
    grad_mods = lax.all_gather(
        lax.psum(all_mods.astype(low), "tensor"), "dp", axis=0, tiled=True
    )
    grad_cond_act = jnp.einsum("be,de->bd", grad_mods, mod_low, preferred_element_type=jnp.float32)
    _, silu_back = jax.vjp(jax.nn.silu, cond)
    grad_cond = silu_back(grad_cond_act)[0]
    grad_temb = grad_cond.astype(low)
    grad_time_act = jnp.einsum(
        "be,de->bd", grad_temb, cond_low[:model_width], preferred_element_type=jnp.float32
    )
    grad_mod_w = jnp.einsum("bd,be->de", cond_act, grad_mods, preferred_element_type=jnp.float32)
    grad_table = jnp.einsum(
        "bc,bd->cd", onehot.astype(jnp.float32), grad_cond, precision=HIGHEST_PREC
    )
    grad_time_two = jnp.einsum("bd,be->de", time_act, grad_temb, preferred_element_type=jnp.float32)
    grad_cond_w = jnp.concatenate([grad_time_two, grad_table], axis=0)
    ends, grad_time_act, loss_sum = lax.psum(
        (
            ends,
            grad_time_act / tensor_count,
            loss_part,
        ),
        ("dp", "tensor"),
    )
    _, silu_back_two = jax.vjp(jax.nn.silu, time_pre)
    grad_pre = silu_back_two(grad_time_act)[0].astype(low)
    grad_time_one = jnp.einsum("bf,bd->fd", features, grad_pre, preferred_element_type=jnp.float32)
    grad_small = jnp.concatenate([ends[:PATCH], grad_time_one, ends[PATCH:]], axis=0)

    def stacked(kind):
        return jnp.stack([kind(i) for i in range(layer_count)])

    grads_list = [
        grad_small,
        grad_cond_w,
        grad_mod_w,
        stacked(lambda i: own_grads[3 * i][:, : 3 * heads_wide].reshape(rows, 3, heads_wide)),
        stacked(lambda i: own_grads[3 * i][:, 3 * heads_wide :].T),
        stacked(lambda i: own_grads[3 * i + 1]),
        stacked(lambda i: own_grads[3 * i + 2].T),
    ]
    weights_list = [small_w, cond_w, mod_w, qkv_w, proj_w, up_w, down_w]
    firsts_list = [small_m, cond_m, mod_m, qkv_m, proj_m, up_m, down_m]
    seconds_list = [small_v, cond_v, mod_v, qkv_v, proj_v, up_v, down_v]
    shares = [1.0 / (dp_count * tensor_count), 1.0 / tensor_count, 1.0 / tensor_count]
    shares = shares + [1.0] * 4

    def squares(arrays):
        sums = []
        for kind_id, a in enumerate(arrays):
            axes = None if kind_id < 3 else tuple(range(1, a.ndim))
            sums.append(jnp.sum(a * a, axis=axes).reshape(-1) * shares[kind_id])
        return jnp.concatenate(sums)

    results = [
        lamb_parts(weights_list[i], firsts_list[i], seconds_list[i], grads_list[i])
        for i in range(len(weights_list))
    ]
    updates = [r[2] for r in results]
    total_sq = lax.psum(
        jnp.stack([squares(weights_list), squares(updates)]), ("dp", "tensor")
    )
    norms = jnp.sqrt(total_sq + EPS_NORM)
    ratio = norms[0] / norms[1]
    outputs = []
    for kind_id in range(7):
        if kind_id < 3:
            factor = ratio[kind_id]
        else:
            first = 3 + (kind_id - 3) * layer_count
            factor = ratio[first : first + layer_count].reshape(
                (layer_count,) + (1,) * (weights_list[kind_id].ndim - 1)
            )
        outputs.append(weights_list[kind_id] - LEARN_RATE * factor * updates[kind_id])
        outputs.append(results[kind_id][0])
        outputs.append(results[kind_id][1])
    return tuple(outputs) + (loss_sum, norms)


def solution(mesh):
    return jax.shard_map(
        local,
        mesh=mesh,
        in_specs=(
            P("dp", None, "tensor"),
            P("dp", None, "tensor"),
            P("dp", None, "tensor"),
            P("dp"),
            P("dp"),
            P(),
            P(),
            P(),
            P(None, "dp"),
            P(None, "dp"),
            P(None, "dp"),
            P("dp", None),
            P("dp", None),
            P("dp", None),
            P(None, "dp", None, "tensor"),
            P(None, "dp", None, "tensor"),
            P(None, "dp", None, "tensor"),
            P(None, "tensor", "dp"),
            P(None, "tensor", "dp"),
            P(None, "tensor", "dp"),
            P(None, "dp", "tensor"),
            P(None, "dp", "tensor"),
            P(None, "dp", "tensor"),
            P(None, "tensor", "dp"),
            P(None, "tensor", "dp"),
            P(None, "tensor", "dp"),
        ),
        out_specs=(
            P(),
            P(),
            P(),
            P(None, "dp"),
            P(None, "dp"),
            P(None, "dp"),
            P("dp", None),
            P("dp", None),
            P("dp", None),
            P(None, "dp", None, "tensor"),
            P(None, "dp", None, "tensor"),
            P(None, "dp", None, "tensor"),
            P(None, "tensor", "dp"),
            P(None, "tensor", "dp"),
            P(None, "tensor", "dp"),
            P(None, "dp", "tensor"),
            P(None, "dp", "tensor"),
            P(None, "dp", "tensor"),
            P(None, "tensor", "dp"),
            P(None, "tensor", "dp"),
            P(None, "tensor", "dp"),
            P(),
            P(),
        ),
        check_vma=False,
    )
```

```python
import math

import jax
import jax.numpy as jnp
from jax import lax
from jax.experimental import pallas as pl
from jax.experimental.pallas import tpu as pltpu
from jax.sharding import PartitionSpec as P

HDIM = 64
PATCH = 16
GRID = 16
FREQ = 256
CLASSES = 1001
TSTEPS = 1000
STEP = 10


HIGHEST_PREC = lax.Precision.HIGHEST
BETA_ONE = 0.9
BETA_TWO = 0.999
EPS_ADAM = 1e-06
EPS_LAYER = 1e-06
EPS_NORM = 1e-12
WEIGHT_DECAY = 0.01
LEARN_RATE = 0.25


def time_features(moment):
    half_freq = FREQ // 2
    frequency = jnp.exp(-math.log(10000.0) * jnp.arange(half_freq).astype(jnp.float32) / half_freq)
    angles = (1000.0 * moment)[:, None] * frequency[None, :]
    return jnp.concatenate([jnp.cos(angles), jnp.sin(angles)], axis=1)


def position_table(token_index, model_width):
    quarter = model_width // 4
    omega_rate = 1.0 / 10000.0 ** (jnp.arange(quarter).astype(jnp.float32) / quarter)
    grid_row = (token_index // GRID).astype(jnp.float32)[:, None] * omega_rate[None, :]
    grid_col = (token_index % GRID).astype(jnp.float32)[:, None] * omega_rate[None, :]
    return jnp.concatenate(
        [jnp.sin(grid_col), jnp.cos(grid_col), jnp.sin(grid_row), jnp.cos(grid_row)], axis=1
    )


def modulated_norm(hidden_in, shift_vec, scale_vec):
    centre = hidden_in - jnp.mean(hidden_in, axis=-1, keepdims=True)
    spread = jnp.mean(centre * centre, axis=-1, keepdims=True)
    return (
        centre * lax.rsqrt(spread + EPS_LAYER) * (1.0 + scale_vec[:, None, :])
        + shift_vec[:, None, :]
    )


def lamb_parts(weight, first, second, grad):
    first_new = BETA_ONE * first + (1.0 - BETA_ONE) * grad
    second_new = BETA_TWO * second + (1.0 - BETA_TWO) * grad * grad
    update = (
        first_new
        / (1.0 - BETA_ONE**STEP)
        / (jnp.sqrt(second_new / (1.0 - BETA_TWO**STEP)) + EPS_ADAM)
        + WEIGHT_DECAY * weight
    )
    return (first_new, second_new, update)


def gelu_tanh(values_in):
    return jax.nn.gelu(values_in, approximate=True)


def spread_rows(part_rows):
    return lax.all_gather(part_rows, "tensor", axis=1, tiled=True)


def fold_rows(term_rows):
    return lax.psum_scatter(
        term_rows.astype(jnp.bfloat16), "tensor", scatter_dimension=1, tiled=True
    ).astype(jnp.float32)


def split_heads(gathered, w_qkv):
    mixed = jnp.einsum("bnd,dte->bnte", gathered, w_qkv, preferred_element_type=jnp.float32).astype(
        jnp.bfloat16
    )
    shaped = mixed.reshape(mixed.shape[0], mixed.shape[1], 3, -1, HDIM)
    return (shaped[:, :, 0], shaped[:, :, 1], shaped[:, :, 2])


def score_block(queries, key_heads):
    return jnp.einsum(
        "bnhe,bmhe->bhnm", queries, key_heads, preferred_element_type=jnp.float32
    ) * HDIM ** (-0.5)


def block_forward(hidden, layer_mod, weights):
    w_qkv, w_proj, w_up, w_down = weights
    normed = modulated_norm(hidden, layer_mod[:, 0], layer_mod[:, 1]).astype(jnp.bfloat16)
    gathered = spread_rows(normed)
    queries, key_heads, values = split_heads(gathered, w_qkv)
    scores = score_block(queries, key_heads)
    row_top = jnp.max(scores, axis=-1, keepdims=True)
    logsum = row_top + jnp.log(jnp.sum(jnp.exp(scores - row_top), axis=-1, keepdims=True))
    softmax_w = jnp.exp(scores - logsum).astype(jnp.bfloat16)
    attended = jnp.einsum(
        "bhnm,bmhe->bnhe", softmax_w, values, preferred_element_type=jnp.float32
    ).astype(jnp.bfloat16)
    attended = attended.reshape(attended.shape[0], attended.shape[1], -1)
    branch = fold_rows(
        jnp.einsum("bne,de->bnd", attended, w_proj, preferred_element_type=jnp.float32)
    )
    middle = hidden + layer_mod[:, 2][:, None, :] * branch
    normed_two = modulated_norm(middle, layer_mod[:, 3], layer_mod[:, 4]).astype(jnp.bfloat16)
    gathered_two = spread_rows(normed_two)
    inner_pre = jnp.einsum("bnd,df->bnf", gathered_two, w_up, preferred_element_type=jnp.float32)
    activ = gelu_tanh(inner_pre).astype(jnp.bfloat16)
    outer_out = fold_rows(
        jnp.einsum("bnf,df->bnd", activ, w_down, preferred_element_type=jnp.float32)
    )
    output = middle + layer_mod[:, 5][:, None, :] * outer_out
    saved_state = (
        hidden,
        gathered,
        queries,
        key_heads,
        values,
        attended,
        logsum,
        branch,
        middle,
        gathered_two,
        inner_pre,
        outer_out,
    )
    return (output, saved_state)


def block_backward(grad_out, layer_mod, weights, saved_state):
    (
        hidden,
        gathered,
        queries,
        key_heads,
        values,
        attended,
        logsum,
        branch,
        middle,
        gathered_two,
        inner_pre,
        outer_out,
    ) = saved_state
    w_qkv, w_proj, w_up, w_down = weights
    grad_gate_m = jnp.sum(grad_out * outer_out, axis=1)
    grad_outer = spread_rows((layer_mod[:, 5][:, None, :] * grad_out).astype(jnp.bfloat16))
    activ = gelu_tanh(inner_pre).astype(jnp.bfloat16)
    grad_down = jnp.einsum("bnd,bnf->df", grad_outer, activ, preferred_element_type=jnp.float32)
    grad_activ = jnp.einsum("bnd,df->bnf", grad_outer, w_down, preferred_element_type=jnp.float32)
    _, gelu_back = jax.vjp(gelu_tanh, inner_pre)
    grad_inner = gelu_back(grad_activ)[0].astype(jnp.bfloat16)
    grad_up = jnp.einsum(
        "bnd,bnf->df", gathered_two, grad_inner, preferred_element_type=jnp.float32
    )
    grad_normed_two = fold_rows(
        jnp.einsum("bnf,df->bnd", grad_inner, w_up, preferred_element_type=jnp.float32)
    )
    _, norm_back = jax.vjp(modulated_norm, middle, layer_mod[:, 3], layer_mod[:, 4])
    grad_middle, grad_shift_m, grad_scale_m = norm_back(grad_normed_two)
    grad_middle = grad_middle + grad_out
    grad_gate_a = jnp.sum(grad_middle * branch, axis=1)
    grad_branch = spread_rows((layer_mod[:, 2][:, None, :] * grad_middle).astype(jnp.bfloat16))
    grad_proj = jnp.einsum("bnd,bne->de", grad_branch, attended, preferred_element_type=jnp.float32)
    grad_att = jnp.einsum(
        "bnd,de->bne", grad_branch, w_proj, preferred_element_type=jnp.float32
    ).astype(jnp.bfloat16)
    grad_att = grad_att.reshape(queries.shape)
    scores = score_block(queries, key_heads)
    soft_float = jnp.exp(scores - logsum)
    softmax_w = soft_float.astype(jnp.bfloat16)
    grad_values = jnp.einsum(
        "bhnm,bnhe->bmhe", softmax_w, grad_att, preferred_element_type=jnp.float32
    ).astype(jnp.bfloat16)
    grad_soft = jnp.einsum("bnhe,bmhe->bhnm", grad_att, values, preferred_element_type=jnp.float32)
    row_delta = jnp.sum(soft_float * grad_soft, axis=-1, keepdims=True)
    grad_scores = (soft_float * (grad_soft - row_delta)).astype(jnp.bfloat16)
    grad_queries = (
        jnp.einsum("bhnm,bmhe->bnhe", grad_scores, key_heads, preferred_element_type=jnp.float32)
        * HDIM ** (-0.5)
    ).astype(jnp.bfloat16)
    grad_keys = (
        jnp.einsum("bhnm,bnhe->bmhe", grad_scores, queries, preferred_element_type=jnp.float32)
        * HDIM ** (-0.5)
    ).astype(jnp.bfloat16)
    grad_mixed = jnp.stack([grad_queries, grad_keys, grad_values], axis=2)
    grad_mixed = grad_mixed.reshape(grad_mixed.shape[0], grad_mixed.shape[1], 3, -1)
    grad_qkv = jnp.einsum("bnd,bnte->dte", gathered, grad_mixed, preferred_element_type=jnp.float32)
    grad_normed = fold_rows(
        jnp.einsum("bnte,dte->bnd", grad_mixed, w_qkv, preferred_element_type=jnp.float32)
    )
    _, norm_back_two = jax.vjp(modulated_norm, hidden, layer_mod[:, 0], layer_mod[:, 1])
    grad_hidden, grad_shift_a, grad_scale_a = norm_back_two(grad_normed)
    grad_hidden = grad_hidden + grad_middle
    grad_layer_mod = jnp.stack(
        [grad_shift_a, grad_scale_a, grad_gate_a, grad_shift_m, grad_scale_m, grad_gate_m], axis=1
    )
    return (grad_hidden, grad_layer_mod, (grad_qkv, grad_proj, grad_up, grad_down))


ORDERS = ((0, 1, 2), (0, 2, 1))
LAG = 2
BURST_LAG = 3
MESH_ID = pl.DeviceIdType.MESH
NN = (((1,), (0,)), ((), ()))
NT = (((1,), (1,)), ((), ()))
TN = (((0,), (0,)), ((), ()))


def grid_of(dp_count):
    if dp_count == 16:
        return (4, 2, 2)
    sizes = [1, 1, 1]
    rest, prime = dp_count, 2
    while rest > 1:
        while rest % prime == 0:
            sizes[sizes.index(min(sizes))] *= prime
            rest //= prime
        prime += 1
    return tuple(sorted(sizes, reverse=True))


def place(sizes):
    index = lax.axis_index("dp")
    return (index // (sizes[1] * sizes[2]), index // sizes[2] % sizes[1], index % sizes[2])


def peer_of(sizes, spot, axis, other):
    moved = [other if a == axis else spot[a] for a in range(3)]
    return (moved[0] * sizes[1] + moved[1]) * sizes[2] + moved[2], lax.axis_index("tensor")


def dot(left, right, form):
    return lax.dot_general(left, right, form, preferred_element_type=jnp.float32)


def greet(peers):
    barrier = pltpu.get_barrier_semaphore()
    for peer in peers:
        pl.semaphore_signal(barrier, inc=1, device_id=peer, device_id_type=MESH_ID)
    pl.semaphore_wait(barrier, len(peers))


def axis_peers(sizes, spot):
    peers = []
    for axis in range(3):
        for offset in range(1, sizes[axis]):
            peers.append(peer_of(sizes, spot, axis, (spot[axis] + offset) % sizes[axis]))
    return peers


def norm_parts(x):
    centre = x - jnp.mean(x, axis=-1, keepdims=True)
    spread = jnp.mean(centre * centre, axis=-1, keepdims=True)
    rstd = lax.rsqrt(spread + EPS_LAYER)
    return centre * rstd, rstd


def norm_forward(x, shift, scale):
    return (norm_parts(x)[0] * (1.0 + scale) + shift).astype(jnp.bfloat16)


def norm_backward(x, scale, dy):
    xh, rstd = norm_parts(x)
    dxh = dy * (1.0 + scale)
    dx = (
        dxh
        - jnp.mean(dxh, axis=-1, keepdims=True)
        - xh * jnp.mean(dxh * xh, axis=-1, keepdims=True)
    ) * rstd
    return dx, jnp.sum(dy, axis=0, keepdims=True), jnp.sum(dy * xh, axis=0, keepdims=True)


GELU_C = math.sqrt(2.0 / math.pi)


def step_kernel(sizes, layers, total_count, *refs):
    (
        blob,
        hidden_in,
        timing,
        cond_cols,
        mod_rows,
        velocity,
        time_weight,
        blended,
        head_rows,
        own_grads,
        timing_all,
        cond_out,
        grad_cond_out,
        grad_mods,
        sums,
        full,
        got_one,
        got_two,
        got_three,
        gathered,
        grad_spread,
        outbox,
        inbox,
        qkv,
        attended,
        hidden,
        middle,
        branch,
        outer,
        inner,
        act,
        grad_inner,
        grad_mixed,
        resid,
        part,
        turned,
        timing_box,
        mod_part,
        mod_box,
        mod,
        mod_grads,
        mod_grads_low,
        mod_grads_box,
        ends,
        loss_row,
        ends_box,
        sum_part,
        sum_box,
        small_send,
        small_recv,
        ag_send,
        ag_recv,
        rs_send,
        rs_recv,
        pair_send,
        pair_recv,
        own_sem,
    ) = refs
    low = jnp.bfloat16
    spot = place(sizes)
    my_dp, my_core = lax.axis_index("dp"), lax.axis_index("tensor")
    partner = (my_dp, 1 - my_core)
    waves, rows, columns = blob.shape
    samples, half_rows, width = hidden_in.shape
    tokens = 2 * half_rows
    heads_wide = qkv.shape[3] // 3
    pairs = heads_wide // (2 * HDIM)
    mine = pl.ds(pl.multiple_of(my_core * half_rows, half_rows), half_rows)
    theirs = pl.ds(pl.multiple_of((1 - my_core) * half_rows, half_rows), half_rows)
    tile = 384
    per_wave = columns // tile
    chunks = waves * per_wave

    own = pltpu.make_async_copy(blob, full.at[:, spot[0], spot[1], spot[2]], own_sem)
    own.start()
    dp_peers = all_peers(sizes[0] * sizes[1] * sizes[2], False)
    greet(dp_peers + [partner])

    small_unsent = []

    def small(kind, slot, source, target, device):
        return pltpu.make_async_remote_copy(
            src_ref=source,
            dst_ref=target,
            send_sem=small_send.at[kind, slot],
            recv_sem=small_recv.at[kind, slot],
            device_id=device,
            device_id_type=MESH_ID,
        )

    def small_start(copies):
        for copy in copies:
            copy.start()
            small_unsent.append(copy)

    devices = len(dp_peers) + 1
    mod_part[...] = jnp.zeros_like(mod_part)
    mod_grads[...] = jnp.zeros_like(mod_grads)
    time_copies = [
        small(0, i, timing, timing_box.at[my_dp], peer) for i, peer in enumerate(dp_peers)
    ]
    small_start(time_copies)
    timing_box[my_dp] = timing[...]

    unsent = []

    def chunk_place(chunk):
        return chunk // per_wave, pl.ds(chunk % per_wave * tile, tile), ORDERS[chunk % 2]

    def gather_copies(chunk, phase):
        wave, lanes, order = chunk_place(chunk)
        axis = order[phase]
        pick = [spot[a] for a in range(3)]
        for earlier in order[:phase]:
            pick[earlier] = slice(None)
        target = full.at[wave, pick[0], pick[1], pick[2], :, lanes]
        source = blob.at[wave, :, lanes] if phase == 0 else target
        return [
            pltpu.make_async_remote_copy(
                src_ref=source,
                dst_ref=target,
                send_sem=ag_send.at[chunk, phase, offset],
                recv_sem=ag_recv.at[chunk, phase, offset],
                device_id=peer_of(sizes, spot, axis, (spot[axis] + offset) % sizes[axis]),
                device_id_type=MESH_ID,
            )
            for offset in range(1, sizes[axis])
        ]

    gather_state = [0]

    def gather_step():
        step = gather_state[0]
        gather_state[0] += 1
        for phase in reversed(range(4)):
            chunk = step - LAG * phase
            if not 0 <= chunk < chunks:
                continue
            if phase > 0:
                for copy in gather_copies(chunk, phase - 1):
                    copy.wait_recv()
            if chunk == 0 and phase == 1:
                own.wait()
            if phase < 3:
                for copy in gather_copies(chunk, phase):
                    copy.start()
                    unsent.append(copy)

    def gather_until(wave):
        while gather_state[0] <= per_wave * (wave + 1) - 1 + 3 * LAG:
            gather_step()

    def gather_more():
        if gather_state[0] < chunks + 3 * LAG:
            gather_step()

    inboxes = (got_one, got_two, got_three)
    rs_unsent = []

    def reduce_copies(chunk, phase):
        wave, lanes, order = chunk_place(chunk)
        order = order[::-1]
        axis = order[phase]
        made = []
        for offset in range(1, sizes[axis]):
            other = (spot[axis] + offset) % sizes[axis]
            pick = [slice(None)] * 3
            for earlier in order[:phase]:
                pick[earlier] = spot[earlier]
            pick[axis] = other
            made.append(
                pltpu.make_async_remote_copy(
                    src_ref=full.at[wave, pick[0], pick[1], pick[2], :, lanes],
                    dst_ref=inboxes[phase].at[chunk, offset - 1],
                    send_sem=rs_send.at[chunk, phase, offset],
                    recv_sem=rs_recv.at[chunk, phase, offset],
                    device_id=peer_of(sizes, spot, axis, other),
                    device_id_type=MESH_ID,
                )
            )
        return made

    def reduce_send(chunk, phase):
        for copy in reduce_copies(chunk, phase):
            copy.start()
            rs_unsent.append(copy)

    def reduce_absorb(chunk, phase):
        for copy in reduce_copies(chunk, phase):
            copy.wait_recv()
        wave, lanes, order = chunk_place(chunk)
        order = order[::-1]
        box = inboxes[phase]
        peers = sizes[order[phase]] - 1
        left = sorted(order[phase + 1 :])
        if not left:
            total = full[wave, spot[0], spot[1], spot[2], :, lanes].astype(jnp.float32)
            for p in range(peers):
                total = total + box[chunk, p].astype(jnp.float32)
            own_grads[wave, :, lanes] = total
            return
        span = math.prod(sizes[a] for a in left)

        def body(step, carry):
            index = (step,) if len(left) == 1 else (step // sizes[left[1]], step % sizes[left[1]])
            pick = list(spot)
            for a, i in zip(left, index):
                pick[a] = i
            total = full[wave, pick[0], pick[1], pick[2], :, lanes].astype(jnp.float32)
            for p in range(peers):
                total = total + box[(chunk, p) + index].astype(jnp.float32)
            full[wave, pick[0], pick[1], pick[2], :, lanes] = total.astype(low)
            return carry

        lax.fori_loop(0, span, body, 0)

    produced = []
    taken = [0, 0, 0, 0]

    def reduce_advance(phase):
        chunk = produced[taken[phase]]
        taken[phase] += 1
        reduce_absorb(chunk, phase - 1)
        if phase < 3:
            reduce_send(chunk, phase)

    def reduce_more(lag=1):
        if taken[3] + LAG <= taken[2]:
            reduce_advance(3)
        if taken[2] + LAG <= taken[1]:
            reduce_advance(2)
        if taken[1] + lag <= len(produced):
            reduce_advance(1)

    def reduce_start(chunk):
        produced.append(chunk)
        reduce_send(chunk, 0)
        reduce_more(BURST_LAG)

    def spread_copy(buffer, slot, stage, b):
        return pltpu.make_async_remote_copy(
            src_ref=buffer.at[slot, b, mine],
            dst_ref=buffer.at[slot, b, mine],
            send_sem=pair_send.at[stage, b],
            recv_sem=pair_recv.at[stage, b],
            device_id=partner,
            device_id_type=MESH_ID,
        )

    pair_unsent = []
    out_turn = {}
    out_last = {}

    def spread(buffer, slot, stage, b, value):
        buffer[slot, b, mine] = value
        copy = spread_copy(buffer, slot, stage, b)
        copy.start()
        pair_unsent.append(copy)

    def fold_copy(slot, stage, b):
        return pltpu.make_async_remote_copy(
            src_ref=outbox.at[out_turn[slot] % 2, b],
            dst_ref=inbox.at[slot, b],
            send_sem=pair_send.at[stage, b],
            recv_sem=pair_recv.at[stage, b],
            device_id=partner,
            device_id_type=MESH_ID,
        )

    def fold(slot, stage, b, value):
        turn = out_turn.setdefault(slot, len(out_turn))
        part[b] = value
        if (turn % 2, b) in out_last:
            out_last[turn % 2, b].wait_send()
        outbox[turn % 2, b] = part[b, theirs].astype(low)
        copy = fold_copy(slot, stage, b)
        copy.start()
        out_last[turn % 2, b] = copy

    def folded(slot, stage, b):
        fold_copy(slot, stage, b).wait_recv()
        return part[b, mine] + inbox[slot, b].astype(jnp.float32)

    def each_sample(body, between=lambda: None):
        for b in range(samples):
            body(b)
            between()

    def weight(wave):
        return full[wave].reshape(width, columns)

    def weight_lanes(wave, lanes, count):
        return full[wave, :, :, :, :, lanes].reshape(width, count)

    def layer_input(layer, b):
        return hidden_in[b] if layer == 0 else hidden[layer - 1, b]

    vectors = mod_rows.shape[1] // width
    per_core = vectors // 2

    def vec(b, row):
        at = b * per_core + row % per_core
        return mod[row // per_core, at : at + 1]

    lane = lax.broadcasted_iota(jnp.int32, (1, 2 * HDIM), 1)
    first_head = lane < HDIM
    keep = (
        jnp.where(first_head, 1.0, 0.0).astype(low),
        jnp.where(first_head, 0.0, 1.0).astype(low),
    )
    factor = HDIM ** (-0.5)

    def pair_lanes(kind, p):
        return pl.ds(kind * heads_wide + p * 2 * HDIM, 2 * HDIM)

    gather_more()
    gather_more()

    for copy in time_copies:
        copy.wait_recv()
    for j in range(devices):
        for b in range(samples):
            timing_all[b * devices + j : b * devices + j + 1] = timing_box[j, b : b + 1]
    everyone = samples * devices
    time_act = timing_all[:, :width]
    time_act = (time_act * jax.nn.sigmoid(time_act)).astype(low)
    classes = cond_cols.shape[1] - width
    label = timing_all[:, width + FREQ : width + FREQ + 1]
    onehot = lax.broadcasted_iota(jnp.int32, (everyone, classes), 1) == label.astype(jnp.int32)
    cond = dot(time_act, cond_cols[:, :width], NT) + dot(
        jnp.where(onehot, 1.0, 0.0).astype(low), cond_cols[:, width:], NT
    )
    cond_out[...] = cond
    cond_act = (cond * jax.nn.sigmoid(cond)).astype(low)
    for i in range(per_core):
        lanes = pl.ds(pl.multiple_of((my_core * per_core + i) * width, 128), width)
        got = dot(cond_act, mod_rows[:, lanes], NN)
        for j in range(devices):
            for b in range(samples):
                at = b * per_core + i
                mod_part[j, at : at + 1] = got[b * devices + j : b * devices + j + 1]
    mod_copies = [
        small(1, i, mod_part.at[peer[0]], mod_box.at[i], peer) for i, peer in enumerate(dp_peers)
    ]
    small_start(mod_copies)
    for _ in range(2 * LAG - 2):
        gather_more()
    total_mod = mod_part[my_dp]
    for i, copy in enumerate(mod_copies):
        copy.wait_recv()
        total_mod = total_mod + mod_box[i]
    mod[my_core] = total_mod
    mod_pair = small(2, 0, mod.at[my_core], mod.at[my_core], partner)
    small_start([mod_pair])
    gather_more()
    mod_pair.wait_recv()
    for layer in range(layers):
        row = 6 * layer
        sa, sb, sc, sd = (8 * layer + i for i in range(4))

        def first(b):
            if layer == 0:
                x = hidden_in[b]
            else:
                x = middle[layer - 1, b] + vec(b, row - 1) * outer[layer - 1, b]
            if layer > 0:
                hidden[layer - 1, b] = x
            spread(gathered, 2 * layer, sa, b, norm_forward(x, vec(b, row), vec(b, row + 1)))

        each_sample(first, gather_more)
        gather_until(3 * layer)

        def attention(b):
            spread_copy(gathered, 2 * layer, sa, b).wait_recv()
            for kind in range(3):
                lanes = pl.ds(kind * heads_wide, heads_wide)
                qkv[layer, b, :, lanes] = dot(
                    gathered[2 * layer, b], weight_lanes(3 * layer, lanes, heads_wide), NN
                ).astype(low)
            for p in range(pairs):
                q = qkv[layer, b, :, pair_lanes(0, p)]
                k = qkv[layer, b, :, pair_lanes(1, p)]
                v = qkv[layer, b, :, pair_lanes(2, p)]
                got = []
                for h in range(2):
                    s = dot(q, k * keep[h], NT) * factor
                    e = jnp.exp(s - jnp.max(s, axis=-1, keepdims=True))
                    e = e / jnp.sum(e, axis=-1, keepdims=True)
                    got.append(dot(e.astype(low), v, NN))
                attended[layer, b, :, pl.ds(p * 2 * HDIM, 2 * HDIM)] = jnp.where(
                    first_head, got[0], got[1]
                ).astype(low)
            fold(
                4 * layer,
                sb,
                b,
                dot(
                    attended[layer, b],
                    weight_lanes(3 * layer, pl.ds(3 * heads_wide, heads_wide), heads_wide),
                    NT,
                ),
            )

        each_sample(attention, gather_more)

        def second(b):
            got = folded(4 * layer, sb, b)
            branch[layer, b] = got
            x = layer_input(layer, b) + vec(b, row + 2) * got
            middle[layer, b] = x
            spread(gathered, 2 * layer + 1, sc, b, norm_forward(x, vec(b, row + 3), vec(b, row + 4)))

        each_sample(second, gather_more)
        gather_until(3 * layer + 1)

        def widen(b):
            spread_copy(gathered, 2 * layer + 1, sc, b).wait_recv()

            def body(n, carry):
                lanes = pl.ds(pl.multiple_of(n * tile, tile), tile)
                x = dot(gathered[2 * layer + 1, b], weight_lanes(3 * layer + 1, lanes, tile), NN)
                inner[b, :, lanes] = x
                t = jnp.tanh(GELU_C * (x + 0.044715 * x * x * x))
                act[b, :, lanes] = (0.5 * x * (1.0 + t)).astype(low)
                return carry

            lax.fori_loop(0, columns // tile, body, 0)

        each_sample(widen, gather_more)
        gather_until(3 * layer + 2)

        def narrow(b):
            fold(4 * layer + 1, sd, b, dot(act[b], weight(3 * layer + 2), NT))

        each_sample(narrow, gather_more)

        def third(b):
            outer[layer, b] = folded(4 * layer + 1, sd, b)

        each_sample(third)

    for copy in unsent:
        copy.wait_send()

    last = layers - 1
    loss_row[...] = jnp.zeros_like(loss_row)
    ends[...] = jnp.zeros_like(ends)
    pad = pl.ds(PATCH, PATCH)

    def head(b):
        x = middle[last, b] + vec(b, 6 * layers - 1) * outer[last, b]
        shift, scale = vec(b, 6 * layers), vec(b, 6 * layers + 1)
        xh, _ = norm_parts(x)
        normed = (xh * (1.0 + scale) + shift).astype(low)
        predicted = dot(head_rows[...], normed, NT)
        error = predicted - velocity[b]
        weighted = time_weight[b] * error
        loss_row[...] += jnp.sum(weighted * error, axis=0, keepdims=True)
        grad_pred = (2.0 * weighted / total_count).astype(low)
        ends[pad, :width] += dot(grad_pred, normed, NN)
        dx, gshift, gscale = norm_backward(x, scale, dot(grad_pred, head_rows[...], TN))
        mod_grads[b, 6 * layers : 6 * layers + 1] = gshift
        mod_grads[b, 6 * layers + 1 : 6 * layers + 2] = gscale
        resid[b] = dx

    each_sample(head)

    def weight_grad(wave, left, right_of, first_tile, count):
        turned[...] = left.reshape(samples * tokens, width).T
        for n in range(count):
            got = dot(turned[...], right_of(pl.ds(n * tile, tile)), NN)
            lanes = pl.ds((first_tile + n) * tile, tile)
            full[wave, :, :, :, :, lanes] = got.astype(low).reshape(sizes + (rows, tile))
            reduce_start(wave * per_wave + first_tile + n)

    for layer in reversed(range(layers)):
        row = 6 * layer
        se, sf, sg, sh = (8 * layer + 4 + i for i in range(4))

        def grad_first(b):
            g = resid[b]
            mod_grads[b, row + 5 : row + 6] = jnp.sum(g * outer[layer, b], axis=0, keepdims=True)
            spread(grad_spread, 2 * layer, se, b, (vec(b, row + 5) * g).astype(low))

        each_sample(grad_first, reduce_more)

        def grad_wide(b):
            spread_copy(grad_spread, 2 * layer, se, b).wait_recv()

            def body(n, carry):
                lanes = pl.ds(pl.multiple_of(n * tile, tile), tile)
                if layer == last:
                    x = inner[b, :, lanes]
                else:
                    x = dot(
                        gathered[2 * layer + 1, b], weight_lanes(3 * layer + 1, lanes, tile), NN
                    )
                g = dot(grad_spread[2 * layer, b], weight_lanes(3 * layer + 2, lanes, tile), NN)
                t = jnp.tanh(GELU_C * (x + 0.044715 * x * x * x))
                if layer != last:
                    act[b, :, lanes] = (0.5 * x * (1.0 + t)).astype(low)
                slope = 0.5 * (1.0 + t) + 0.5 * x * (1.0 - t * t) * (
                    GELU_C * (1.0 + 3.0 * 0.044715 * x * x)
                )
                grad_inner[b, :, lanes] = (g * slope).astype(low)
                return carry

            lax.fori_loop(0, columns // tile, body, 0)
            fold(4 * layer + 2, sf, b, dot(grad_inner[b], weight(3 * layer + 1), NT))

        each_sample(grad_wide, reduce_more)

        def wide_of(source):
            return lambda lanes: source[:, :, lanes].reshape(samples * tokens, tile)

        weight_grad(3 * layer + 2, grad_spread[2 * layer], wide_of(act), 0, per_wave)
        weight_grad(3 * layer + 1, gathered[2 * layer + 1], wide_of(grad_inner), 0, per_wave)

        def grad_second(b):
            dy = folded(4 * layer + 2, sf, b)
            dx, gshift, gscale = norm_backward(middle[layer, b], vec(b, row + 4), dy)
            g = dx + resid[b]
            resid[b] = g
            mod_grads[b, row + 3 : row + 4] = gshift
            mod_grads[b, row + 4 : row + 5] = gscale
            mod_grads[b, row + 2 : row + 3] = jnp.sum(g * branch[layer, b], axis=0, keepdims=True)
            spread(grad_spread, 2 * layer + 1, sg, b, (vec(b, row + 2) * g).astype(low))

        each_sample(grad_second, reduce_more)

        def grad_attention(b):
            spread_copy(grad_spread, 2 * layer + 1, sg, b).wait_recv()
            got_all = dot(
                grad_spread[2 * layer + 1, b],
                weight_lanes(3 * layer, pl.ds(3 * heads_wide, heads_wide), heads_wide),
                NN,
            ).astype(low)
            for p in range(pairs):
                ga = got_all[:, p * 2 * HDIM : (p + 1) * 2 * HDIM]
                q = qkv[layer, b, :, pair_lanes(0, p)]
                k = qkv[layer, b, :, pair_lanes(1, p)]
                v = qkv[layer, b, :, pair_lanes(2, p)]
                gq, gk, gv = [], [], []
                for h in range(2):
                    s = dot(k * keep[h], q, NT) * factor
                    e = jnp.exp(s - jnp.max(s, axis=0, keepdims=True))
                    e = e / jnp.sum(e, axis=0, keepdims=True)
                    dp = dot(v * keep[h], ga, NT)
                    ds = (e * (dp - jnp.sum(e * dp, axis=0, keepdims=True))).astype(low)
                    gv.append(dot(e.astype(low), ga, NN))
                    gk.append(dot(ds, q, NN))
                    gq.append(dot(ds, k, TN))
                for kind, got, scale in ((0, gq, factor), (1, gk, factor), (2, gv, 1.0)):
                    grad_mixed[b, :, pair_lanes(kind, p)] = (
                        jnp.where(first_head, got[0], got[1]) * scale
                    ).astype(low)
            fold(
                4 * layer + 3,
                sh,
                b,
                dot(
                    grad_mixed[b],
                    weight_lanes(3 * layer, pl.ds(0, 3 * heads_wide), 3 * heads_wide),
                    NT,
                ),
            )

        each_sample(grad_attention, reduce_more)
        weight_grad(3 * layer, gathered[2 * layer], wide_of(grad_mixed), 0, 3)
        weight_grad(3 * layer, grad_spread[2 * layer + 1], wide_of(attended.at[layer]), 3, 1)

        def grad_third(b):
            dy = folded(4 * layer + 3, sh, b)
            dx, gshift, gscale = norm_backward(layer_input(layer, b), vec(b, row + 1), dy)
            resid[b] = dx + resid[b]
            mod_grads[b, row : row + 1] = gshift
            mod_grads[b, row + 1 : row + 2] = gscale

        each_sample(grad_third, reduce_more)

    def patch(b):
        ends[pl.ds(0, PATCH), :width] += dot(blended[b], resid[b].astype(low), NN)

    each_sample(patch)
    ends[0:1, width:] = loss_row[0:1]
    for b in range(samples):
        mod_grads_low[b] = mod_grads[b].astype(low)
    first_pair = small(2, 1, mod_grads_low.at[1 - my_core], mod_grads_box, partner)
    ends_pair = small(2, 2, ends, ends_box, partner)
    small_start([first_pair, ends_pair])
    reduce_more()
    first_pair.wait_recv()
    grad_mods[my_core, my_dp] = (
        mod_grads_low[my_core].astype(jnp.float32) + mod_grads_box[...].astype(jnp.float32)
    ).astype(low)
    share_copies = [
        small(3, i, grad_mods.at[my_core, my_dp], grad_mods.at[my_core, my_dp], peer)
        for i, peer in enumerate(dp_peers)
    ]
    small_start(share_copies)
    for _ in range(3):
        reduce_more()
    for copy in share_copies:
        copy.wait_recv()
    share_pair = small(2, 3, grad_mods.at[my_core], grad_mods.at[my_core], partner)
    small_start([share_pair])
    reduce_more()
    share_pair.wait_recv()
    slots = grad_mods.shape[2]
    every_row = grad_mods[...].reshape(everyone * slots, width)
    slot = lax.broadcasted_iota(jnp.int32, (everyone * slots, 1), 0) % slots
    grad_cond_act = jnp.zeros((everyone * slots, rows), jnp.float32)
    for i in range(vectors):
        got = dot(every_row, mod_rows[:, pl.ds(i * width, width)], NT)
        grad_cond_act = grad_cond_act + jnp.where(slot == i, got, 0.0)
    grad_cond_act = jnp.sum(grad_cond_act.reshape(everyone, slots, rows), axis=1)
    reduce_more()
    cond = cond_out[...]
    gate = jax.nn.sigmoid(cond)
    grad_cond = grad_cond_act * gate * (1.0 + cond * (1.0 - gate))
    grad_cond_out[...] = grad_cond
    grad_time_act = dot(grad_cond.astype(low), cond_cols[:, :width], NN)
    ends_pair.wait_recv()
    ends_sum = ends[...] + ends_box[...]
    is_first = my_core == 0
    picked = jnp.where(is_first, ends_sum[:everyone, :width], grad_time_act)
    extra = jnp.where(is_first, ends_sum[0:1, width:], 0.0)
    for j in range(devices):
        for b in range(samples):
            sum_part[j, b : b + 1, :width] = picked[b * devices + j : b * devices + j + 1]
            sum_part[j, b : b + 1, width:] = extra
    sum_copies = [
        small(4, i, sum_part.at[peer[0]], sum_box.at[i], peer) for i, peer in enumerate(dp_peers)
    ]
    small_start(sum_copies)
    for _ in range(3):
        reduce_more()
    total_sum = sum_part[my_dp]
    for i, copy in enumerate(sum_copies):
        copy.wait_recv()
        total_sum = total_sum + sum_box[i]
    sums[my_core, my_dp] = total_sum
    back_copies = [
        small(5, i, sums.at[my_core, my_dp], sums.at[my_core, my_dp], peer)
        for i, peer in enumerate(dp_peers)
    ]
    small_start(back_copies)
    for _ in range(3):
        reduce_more()
    for copy in back_copies:
        copy.wait_recv()
    sums_pair = small(2, 4, sums.at[my_core], sums.at[my_core], partner)
    small_start([sums_pair])
    while taken[3] < chunks:
        before = list(taken)
        reduce_more()
        if taken == before:
            for phase in (3, 2):
                if taken[phase] < taken[phase - 1]:
                    reduce_advance(phase)
                    break
    sums_pair.wait_recv()
    for copy in small_unsent:
        copy.wait_send()
    for copy in rs_unsent:
        copy.wait_send()

    for copy in pair_unsent + list(out_last.values()):
        copy.wait_send()


def train_step(
    blob,
    hidden,
    timing,
    cond_cols,
    mod_rows,
    velocity,
    time_weight,
    blended,
    head_rows,
    dp_count,
    layers,
    total,
):
    sizes = grid_of(dp_count)
    waves, rows, columns = blob.shape
    samples, half_rows, width = hidden.shape
    tokens = 2 * half_rows
    tile = columns // 4
    chunks = 4 * waves
    heads_wide = columns // 4
    most = max(sizes)
    slots = 16
    low, wide = jnp.bfloat16, jnp.float32
    in_vmem = pl.BlockSpec(memory_space=pltpu.VMEM)
    stages = 8 * layers
    resid_shape = (layers, samples, half_rows, width)
    dma = pltpu.SemaphoreType.DMA
    everyone = samples * dp_count
    return pl.pallas_call(
        lambda *refs: step_kernel(sizes, layers, total, *refs),
        out_shape=(
            jax.ShapeDtypeStruct((waves, rows, columns), wide),
            jax.ShapeDtypeStruct((everyone, timing.shape[1]), wide),
            jax.ShapeDtypeStruct((everyone, rows), wide),
            jax.ShapeDtypeStruct((everyone, rows), wide),
            jax.ShapeDtypeStruct((2, dp_count, slots, width), low),
            jax.ShapeDtypeStruct((2, dp_count, samples, width + 128), wide),
        ),
        in_specs=[pl.BlockSpec(memory_space=pl.ANY)] + [in_vmem] * 8,
        out_specs=(in_vmem,) * 6,
        scratch_shapes=[
            pltpu.VMEM((waves,) + sizes + (rows, columns), low),
            pltpu.VMEM((chunks, sizes[2] - 1, sizes[0], sizes[1], rows, tile), low),
            pltpu.VMEM((chunks, sizes[1] - 1, sizes[0], rows, tile), low),
            pltpu.VMEM((chunks, sizes[0] - 1, rows, tile), low),
            pltpu.VMEM((2 * layers, samples, tokens, width), low),
            pltpu.VMEM((2 * layers, samples, tokens, width), low),
            pltpu.VMEM((2, samples, half_rows, width), low),
            pltpu.VMEM((4 * layers, samples, half_rows, width), low),
            pltpu.VMEM((layers, samples, tokens, 3 * heads_wide), low),
            pltpu.VMEM((layers, samples, tokens, heads_wide), low),
            pltpu.VMEM((max(layers - 1, 1),) + resid_shape[1:], wide),
            pltpu.VMEM(resid_shape, wide),
            pltpu.VMEM(resid_shape, wide),
            pltpu.VMEM(resid_shape, wide),
            pltpu.VMEM((samples, tokens, columns), wide),
            pltpu.VMEM((samples, tokens, columns), low),
            pltpu.VMEM((samples, tokens, columns), low),
            pltpu.VMEM((samples, tokens, 3 * heads_wide), low),
            pltpu.VMEM((samples, half_rows, width), wide),
            pltpu.VMEM((samples, tokens, width), wide),
            pltpu.VMEM((width, samples * tokens), low),
            pltpu.VMEM((dp_count,) + timing.shape, wide),
            pltpu.VMEM((dp_count, slots, width), wide),
            pltpu.VMEM((dp_count - 1, slots, width), wide),
            pltpu.VMEM((2, slots, width), wide),
            pltpu.VMEM((samples, slots, width), wide),
            pltpu.VMEM((samples, slots, width), low),
            pltpu.VMEM((slots, width), low),
            pltpu.VMEM((2 * PATCH, width + 128), wide),
            pltpu.VMEM((8, half_rows), wide),
            pltpu.VMEM((2 * PATCH, width + 128), wide),
            pltpu.VMEM((dp_count, samples, width + 128), wide),
            pltpu.VMEM((dp_count - 1, samples, width + 128), wide),
            dma((6, max(dp_count, 8))),
            dma((6, max(dp_count, 8))),
            dma((chunks, 3, most)),
            dma((chunks, 3, most)),
            dma((chunks, 3, most)),
            dma((chunks, 3, most)),
            dma((stages, samples)),
            dma((stages, samples)),
            dma,
        ],
        compiler_params=pltpu.CompilerParams(
            collective_id=0, has_side_effects=True, vmem_limit_bytes=64 * 2**20 - 2**17
        ),
    )(blob, hidden, timing, cond_cols, mod_rows, velocity, time_weight, blended, head_rows)


def all_peers(dp_count, with_cores):
    me, core = lax.axis_index("dp"), lax.axis_index("tensor")
    peers = []
    for offset in range(1, dp_count):
        peers.append(((me + offset) % dp_count, core))
    if with_cores:
        for offset in range(dp_count):
            peers.append(((me + offset) % dp_count, 1 - core))
    return peers


def push(source, target, sems, slot, device):
    return pltpu.make_async_remote_copy(
        src_ref=source,
        dst_ref=target,
        send_sem=sems[0].at[slot],
        recv_sem=sems[1].at[slot],
        device_id=device,
        device_id_type=MESH_ID,
    )


def norm_kernel(dp_count, x, out, box, send, recv):
    peers = all_peers(dp_count, True)
    greet(peers)
    copies = [push(x, box.at[i], (send, recv), i, p) for i, p in enumerate(peers)]
    for copy in copies:
        copy.start()
    total = x[...]
    for i, copy in enumerate(copies):
        copy.wait_recv()
        total = total + box[i]
    out[...] = total
    for copy in copies:
        copy.wait_send()


def sum_norms(x, dp_count):
    dma = pltpu.SemaphoreType.DMA
    count = 2 * dp_count - 1
    return pl.pallas_call(
        lambda *refs: norm_kernel(dp_count, *refs),
        out_shape=jax.ShapeDtypeStruct(x.shape, x.dtype),
        in_specs=[pl.BlockSpec(memory_space=pltpu.VMEM)],
        out_specs=pl.BlockSpec(memory_space=pltpu.VMEM),
        scratch_shapes=[pltpu.VMEM((count,) + x.shape, x.dtype), dma((count,)), dma((count,))],
        compiler_params=pltpu.CompilerParams(collective_id=5, has_side_effects=True),
    )(x)


def gather_plain(blob, dp_count):
    waves, rows, columns = blob.shape
    return lax.all_gather(blob, "dp", axis=1, tiled=True)


def reduce_plain(grads, dp_count):
    return jnp.stack(
        [
            lax.psum_scatter(g.astype(jnp.float32), "dp", scatter_dimension=0, tiled=True)
            for g in grads
        ]
    )


def local(
    latents,
    gaussian,
    velocity,
    time_ids,
    labels,
    small_w,
    small_m,
    small_v,
    cond_w,
    cond_m,
    cond_v,
    mod_w,
    mod_m,
    mod_v,
    qkv_w,
    qkv_m,
    qkv_v,
    proj_w,
    proj_m,
    proj_v,
    up_w,
    up_m,
    up_v,
    down_w,
    down_m,
    down_v,
):
    layer_count = qkv_w.shape[0]
    model_width = mod_w.shape[1] // (6 * layer_count + 2)
    dp_count = lax.axis_size("dp")
    tensor_count = lax.axis_size("tensor")
    samples = latents.shape[0]
    half_rows = latents.shape[2]
    rows = qkv_w.shape[1]
    kernels = rows % 16 == 0
    my_dp = lax.axis_index("dp")
    low = jnp.bfloat16

    parts = []
    for i in range(layer_count):
        parts.append(
            jnp.concatenate(
                [qkv_w[i, :, 0], qkv_w[i, :, 1], qkv_w[i, :, 2], proj_w[i].T], axis=1
            ).astype(low)
        )
        parts.append(up_w[i].astype(low))
        parts.append(down_w[i].T.astype(low))
    blob = jnp.stack(parts)
    heads_wide = qkv_w.shape[3]

    small_low = small_w.astype(low)
    patch_rows = small_low[:PATCH]
    time_rows = small_low[PATCH : PATCH + FREQ]
    head_rows = small_low[PATCH + FREQ :]
    mod_low = mod_w.astype(low)

    moment = (time_ids.astype(jnp.float32) + 0.5) / TSTEPS
    blended = ((1.0 - moment)[:, None, None] * latents + moment[:, None, None] * gaussian).astype(
        jnp.bfloat16
    )
    token_index = lax.axis_index("tensor") * half_rows + jnp.arange(half_rows)
    hidden = (
        jnp.einsum("bpn,pd->bnd", blended, patch_rows, preferred_element_type=jnp.float32)
        + position_table(token_index, model_width)[None]
    )
    time_weight = 0.5 + moment
    total_count = samples * dp_count * half_rows * tensor_count * PATCH
    features = time_features(moment).astype(low)
    time_pre = jnp.dot(features, time_rows, preferred_element_type=jnp.float32)
    timing = jnp.concatenate(
        [
            time_pre,
            features.astype(jnp.float32),
            jnp.broadcast_to(labels.astype(jnp.float32)[:, None], (samples, 128)),
        ],
        axis=1,
    )
    if kernels:
        spare = -cond_w.shape[0] % 128
        own_grads, timing_all, cond, grad_cond, shared, sums = train_step(
            blob,
            hidden,
            timing,
            jnp.pad(cond_w.T.astype(low), ((0, 0), (0, spare))),
            mod_low,
            velocity,
            jnp.broadcast_to(time_weight[:, None, None], velocity.shape),
            blended,
            head_rows,
            dp_count,
            layer_count,
            float(total_count),
        )
        vectors = 6 * layer_count + 2
        grad_mods = shared[:, :, :vectors].reshape(samples * dp_count, -1)
        loss_sum = jnp.sum(sums[0, 0, 0, model_width:])
        sums = sums.transpose(0, 2, 1, 3)[..., :model_width].reshape(2, -1, model_width)
        ends, grad_time_act = sums[0], sums[1]
    else:
        timing_all = lax.all_gather(timing, "dp", axis=1, tiled=False)
        timing_all = timing_all.reshape(samples * dp_count, -1)
        time_act = jax.nn.silu(timing_all[:, :model_width]).astype(low)
        all_labels = timing_all[:, model_width + FREQ].astype(jnp.int32)
        onehot = (all_labels[:, None] == jnp.arange(CLASSES)[None, :]).astype(low)
        cond_low = cond_w.astype(low)
        cond = jnp.dot(
            time_act, cond_low[:model_width], preferred_element_type=jnp.float32
        ) + jnp.dot(onehot, cond_low[model_width:], preferred_element_type=jnp.float32)
        modulation = jnp.dot(
            jax.nn.silu(cond).astype(low), mod_low, preferred_element_type=jnp.float32
        ).reshape(samples, dp_count, -1)
        modulation = lax.psum_scatter(modulation, "dp", scatter_dimension=1, tiled=True)[:, 0]
        full = gather_plain(blob, dp_count)
        saved_list = []
        fetched = []
        for layer_id in range(layer_count):
            packed = full[3 * layer_id]
            weights = (
                packed[:, : 3 * heads_wide].reshape(model_width, 3, heads_wide),
                packed[:, 3 * heads_wide :],
                full[3 * layer_id + 1],
                full[3 * layer_id + 2],
            )
            layer_mod = modulation[
                :, 6 * layer_id * model_width : (6 * layer_id + 6) * model_width
            ].reshape(samples, 6, model_width)
            hidden, saved_state = block_forward(hidden, layer_mod, weights)
            saved_list.append(saved_state)
            fetched.append(weights)
        final_mod = modulation[:, 6 * layer_count * model_width :].reshape(samples, 2, model_width)
        final_normed = modulated_norm(hidden, final_mod[:, 0], final_mod[:, 1]).astype(jnp.bfloat16)
        predicted = jnp.einsum(
            "bnd,pd->bpn", final_normed, head_rows, preferred_element_type=jnp.float32
        )
        error = predicted - velocity
        loss_part = jnp.sum(time_weight[:, None, None] * error * error)
        grad_pred = (time_weight[:, None, None] * (2.0 * error) / total_count).astype(jnp.bfloat16)
        grad_head = jnp.einsum(
            "bpn,bnd->pd", grad_pred, final_normed, preferred_element_type=jnp.float32
        )
        grad_final = jnp.einsum("bpn,pd->bnd", grad_pred, head_rows, preferred_element_type=jnp.float32)
        _, final_back = jax.vjp(modulated_norm, hidden, final_mod[:, 0], final_mod[:, 1])
        grad_hidden, grad_fshift, grad_fscale = final_back(grad_final)
        mod_grads = [None] * layer_count
        layer_grads = [None] * (3 * layer_count)
        for layer_id in reversed(range(layer_count)):
            layer_mod = modulation[
                :, 6 * layer_id * model_width : (6 * layer_id + 6) * model_width
            ].reshape(samples, 6, model_width)
            grad_hidden, grad_layer_mod, grads = block_backward(
                grad_hidden, layer_mod, fetched[layer_id], saved_list[layer_id]
            )
            layer_grads[3 * layer_id] = jnp.concatenate(
                [grads[0].reshape(model_width, 3 * heads_wide).astype(low), grads[1].astype(low)],
                axis=1,
            )
            layer_grads[3 * layer_id + 1] = grads[2].astype(low)
            layer_grads[3 * layer_id + 2] = grads[3].astype(low)
            mod_grads[layer_id] = grad_layer_mod.reshape(samples, 6 * model_width)
        own_grads = reduce_plain(layer_grads, dp_count)
        grad_patch = jnp.einsum(
            "bpn,bnd->pd", blended, grad_hidden.astype(jnp.bfloat16), preferred_element_type=jnp.float32
        )
        ends = jnp.concatenate([grad_patch, grad_head], axis=0)
        all_mods = jnp.concatenate(
            mod_grads
            + [jnp.stack([grad_fshift, grad_fscale], axis=1).reshape(samples, 2 * model_width)],
            axis=1,
        )
        grad_mods = lax.all_gather(lax.psum(all_mods.astype(low), "tensor"), "dp", axis=1)
        grad_mods = grad_mods.reshape(samples * dp_count, -1)
        grad_cond_act = jnp.einsum(
            "be,de->bd", grad_mods, mod_low, preferred_element_type=jnp.float32
        )
        _, silu_back = jax.vjp(jax.nn.silu, cond)
        grad_cond = silu_back(grad_cond_act)[0]
        grad_time_act = jnp.einsum(
            "be,de->bd",
            grad_cond.astype(low),
            cond_low[:model_width],
            preferred_element_type=jnp.float32,
        )
        ends, grad_time_act, loss_sum = lax.psum(
            (ends, grad_time_act / tensor_count, loss_part), ("dp", "tensor")
        )
    time_pre = timing_all[:, :model_width]
    features = timing_all[:, model_width : model_width + FREQ].astype(low)
    all_labels = timing_all[:, model_width + FREQ].astype(jnp.int32)
    onehot = all_labels[:, None] == jnp.arange(CLASSES)[None, :]
    time_act = jax.nn.silu(time_pre).astype(low)
    cond_act = jax.nn.silu(cond).astype(low)
    grad_temb = grad_cond.astype(low)
    grad_mod_w = jnp.einsum("bd,be->de", cond_act, grad_mods, preferred_element_type=jnp.float32)
    grad_table = jnp.einsum(
        "bc,bd->cd", onehot.astype(jnp.float32), grad_cond, precision=HIGHEST_PREC
    )
    grad_time_two = jnp.einsum("bd,be->de", time_act, grad_temb, preferred_element_type=jnp.float32)
    grad_cond_w = jnp.concatenate([grad_time_two, grad_table], axis=0)
    _, silu_back_two = jax.vjp(jax.nn.silu, time_pre)
    grad_pre = silu_back_two(grad_time_act)[0].astype(low)
    grad_time_one = jnp.einsum("bf,bd->fd", features, grad_pre, preferred_element_type=jnp.float32)
    grad_small = jnp.concatenate([ends[:PATCH], grad_time_one, ends[PATCH:]], axis=0)

    def stacked(kind):
        return jnp.stack([kind(i) for i in range(layer_count)])

    grads_list = [
        grad_small,
        grad_cond_w,
        grad_mod_w,
        stacked(lambda i: own_grads[3 * i][:, : 3 * heads_wide].reshape(rows, 3, heads_wide)),
        stacked(lambda i: own_grads[3 * i][:, 3 * heads_wide :].T),
        stacked(lambda i: own_grads[3 * i + 1]),
        stacked(lambda i: own_grads[3 * i + 2].T),
    ]
    weights_list = [small_w, cond_w, mod_w, qkv_w, proj_w, up_w, down_w]
    firsts_list = [small_m, cond_m, mod_m, qkv_m, proj_m, up_m, down_m]
    seconds_list = [small_v, cond_v, mod_v, qkv_v, proj_v, up_v, down_v]
    shares = [1.0 / (dp_count * tensor_count), 1.0 / tensor_count, 1.0 / tensor_count]
    shares = shares + [1.0] * 4

    def squares(arrays):
        sums = []
        for kind_id, a in enumerate(arrays):
            axes = None if kind_id < 3 else tuple(range(1, a.ndim))
            sums.append(jnp.sum(a * a, axis=axes).reshape(-1) * shares[kind_id])
        return jnp.concatenate(sums)

    results = [
        lamb_parts(weights_list[i], firsts_list[i], seconds_list[i], grads_list[i])
        for i in range(len(weights_list))
    ]
    updates = [r[2] for r in results]
    total_sq = jnp.stack([squares(weights_list), squares(updates)])
    if kernels:
        kinds = total_sq.shape[1]
        total_sq = sum_norms(jnp.pad(total_sq, ((0, 6), (0, 128 - kinds))), dp_count)[:2, :kinds]
    else:
        total_sq = lax.psum(total_sq, ("dp", "tensor"))
    norms = jnp.sqrt(total_sq + EPS_NORM)
    ratio = norms[0] / norms[1]
    outputs = []
    for kind_id in range(7):
        if kind_id < 3:
            factor = ratio[kind_id]
        else:
            first = 3 + (kind_id - 3) * layer_count
            factor = ratio[first : first + layer_count].reshape(
                (layer_count,) + (1,) * (weights_list[kind_id].ndim - 1)
            )
        outputs.append(weights_list[kind_id] - LEARN_RATE * factor * updates[kind_id])
        outputs.append(results[kind_id][0])
        outputs.append(results[kind_id][1])
    return tuple(outputs) + (loss_sum, norms)


def solution(mesh):
    return jax.shard_map(
        local,
        mesh=mesh,
        in_specs=(
            P("dp", None, "tensor"),
            P("dp", None, "tensor"),
            P("dp", None, "tensor"),
            P("dp"),
            P("dp"),
            P(),
            P(),
            P(),
            P(None, "dp"),
            P(None, "dp"),
            P(None, "dp"),
            P("dp", None),
            P("dp", None),
            P("dp", None),
            P(None, "dp", None, "tensor"),
            P(None, "dp", None, "tensor"),
            P(None, "dp", None, "tensor"),
            P(None, "tensor", "dp"),
            P(None, "tensor", "dp"),
            P(None, "tensor", "dp"),
            P(None, "dp", "tensor"),
            P(None, "dp", "tensor"),
            P(None, "dp", "tensor"),
            P(None, "tensor", "dp"),
            P(None, "tensor", "dp"),
            P(None, "tensor", "dp"),
        ),
        out_specs=(
            P(),
            P(),
            P(),
            P(None, "dp"),
            P(None, "dp"),
            P(None, "dp"),
            P("dp", None),
            P("dp", None),
            P("dp", None),
            P(None, "dp", None, "tensor"),
            P(None, "dp", None, "tensor"),
            P(None, "dp", None, "tensor"),
            P(None, "tensor", "dp"),
            P(None, "tensor", "dp"),
            P(None, "tensor", "dp"),
            P(None, "dp", "tensor"),
            P(None, "dp", "tensor"),
            P(None, "dp", "tensor"),
            P(None, "tensor", "dp"),
            P(None, "tensor", "dp"),
            P(None, "tensor", "dp"),
            P(),
            P(),
        ),
        check_vma=False,
    )
```

```python
import math

import jax
import jax.numpy as jnp
from jax import lax
from jax.experimental import pallas as pl
from jax.experimental.pallas import tpu as pltpu
from jax.sharding import PartitionSpec as P

HDIM = 64
PATCH = 16
GRID = 16
FREQ = 256
CLASSES = 1001
TSTEPS = 1000
STEP = 10


HIGHEST_PREC = lax.Precision.HIGHEST
BETA_ONE = 0.9
BETA_TWO = 0.999
EPS_ADAM = 1e-06
EPS_LAYER = 1e-06
EPS_NORM = 1e-12
WEIGHT_DECAY = 0.01
LEARN_RATE = 0.25


def time_features(moment):
    half_freq = FREQ // 2
    frequency = jnp.exp(-math.log(10000.0) * jnp.arange(half_freq).astype(jnp.float32) / half_freq)
    angles = (1000.0 * moment)[:, None] * frequency[None, :]
    return jnp.concatenate([jnp.cos(angles), jnp.sin(angles)], axis=1)


def position_table(token_index, model_width):
    quarter = model_width // 4
    omega_rate = 1.0 / 10000.0 ** (jnp.arange(quarter).astype(jnp.float32) / quarter)
    grid_row = (token_index // GRID).astype(jnp.float32)[:, None] * omega_rate[None, :]
    grid_col = (token_index % GRID).astype(jnp.float32)[:, None] * omega_rate[None, :]
    return jnp.concatenate(
        [jnp.sin(grid_col), jnp.cos(grid_col), jnp.sin(grid_row), jnp.cos(grid_row)], axis=1
    )


def modulated_norm(hidden_in, shift_vec, scale_vec):
    centre = hidden_in - jnp.mean(hidden_in, axis=-1, keepdims=True)
    spread = jnp.mean(centre * centre, axis=-1, keepdims=True)
    return (
        centre * lax.rsqrt(spread + EPS_LAYER) * (1.0 + scale_vec[:, None, :])
        + shift_vec[:, None, :]
    )


def lamb_parts(weight, first, second, grad):
    first_new = BETA_ONE * first + (1.0 - BETA_ONE) * grad
    second_new = BETA_TWO * second + (1.0 - BETA_TWO) * grad * grad
    update = (
        first_new
        / (1.0 - BETA_ONE**STEP)
        / (jnp.sqrt(second_new / (1.0 - BETA_TWO**STEP)) + EPS_ADAM)
        + WEIGHT_DECAY * weight
    )
    return (first_new, second_new, update)


def gelu_tanh(values_in):
    return jax.nn.gelu(values_in, approximate=True)


def spread_rows(part_rows):
    return lax.all_gather(part_rows, "tensor", axis=1, tiled=True)


def fold_rows(term_rows):
    return lax.psum_scatter(
        term_rows.astype(jnp.bfloat16), "tensor", scatter_dimension=1, tiled=True
    ).astype(jnp.float32)


def split_heads(gathered, w_qkv):
    mixed = jnp.einsum("bnd,dte->bnte", gathered, w_qkv, preferred_element_type=jnp.float32).astype(
        jnp.bfloat16
    )
    shaped = mixed.reshape(mixed.shape[0], mixed.shape[1], 3, -1, HDIM)
    return (shaped[:, :, 0], shaped[:, :, 1], shaped[:, :, 2])


def score_block(queries, key_heads):
    return jnp.einsum(
        "bnhe,bmhe->bhnm", queries, key_heads, preferred_element_type=jnp.float32
    ) * HDIM ** (-0.5)


def block_forward(hidden, layer_mod, weights):
    w_qkv, w_proj, w_up, w_down = weights
    normed = modulated_norm(hidden, layer_mod[:, 0], layer_mod[:, 1]).astype(jnp.bfloat16)
    gathered = spread_rows(normed)
    queries, key_heads, values = split_heads(gathered, w_qkv)
    scores = score_block(queries, key_heads)
    row_top = jnp.max(scores, axis=-1, keepdims=True)
    logsum = row_top + jnp.log(jnp.sum(jnp.exp(scores - row_top), axis=-1, keepdims=True))
    softmax_w = jnp.exp(scores - logsum).astype(jnp.bfloat16)
    attended = jnp.einsum(
        "bhnm,bmhe->bnhe", softmax_w, values, preferred_element_type=jnp.float32
    ).astype(jnp.bfloat16)
    attended = attended.reshape(attended.shape[0], attended.shape[1], -1)
    branch = fold_rows(
        jnp.einsum("bne,de->bnd", attended, w_proj, preferred_element_type=jnp.float32)
    )
    middle = hidden + layer_mod[:, 2][:, None, :] * branch
    normed_two = modulated_norm(middle, layer_mod[:, 3], layer_mod[:, 4]).astype(jnp.bfloat16)
    gathered_two = spread_rows(normed_two)
    inner_pre = jnp.einsum("bnd,df->bnf", gathered_two, w_up, preferred_element_type=jnp.float32)
    activ = gelu_tanh(inner_pre).astype(jnp.bfloat16)
    outer_out = fold_rows(
        jnp.einsum("bnf,df->bnd", activ, w_down, preferred_element_type=jnp.float32)
    )
    output = middle + layer_mod[:, 5][:, None, :] * outer_out
    saved_state = (
        hidden,
        gathered,
        queries,
        key_heads,
        values,
        attended,
        logsum,
        branch,
        middle,
        gathered_two,
        inner_pre,
        outer_out,
    )
    return (output, saved_state)


def block_backward(grad_out, layer_mod, weights, saved_state):
    (
        hidden,
        gathered,
        queries,
        key_heads,
        values,
        attended,
        logsum,
        branch,
        middle,
        gathered_two,
        inner_pre,
        outer_out,
    ) = saved_state
    w_qkv, w_proj, w_up, w_down = weights
    grad_gate_m = jnp.sum(grad_out * outer_out, axis=1)
    grad_outer = spread_rows((layer_mod[:, 5][:, None, :] * grad_out).astype(jnp.bfloat16))
    activ = gelu_tanh(inner_pre).astype(jnp.bfloat16)
    grad_down = jnp.einsum("bnd,bnf->df", grad_outer, activ, preferred_element_type=jnp.float32)
    grad_activ = jnp.einsum("bnd,df->bnf", grad_outer, w_down, preferred_element_type=jnp.float32)
    _, gelu_back = jax.vjp(gelu_tanh, inner_pre)
    grad_inner = gelu_back(grad_activ)[0].astype(jnp.bfloat16)
    grad_up = jnp.einsum(
        "bnd,bnf->df", gathered_two, grad_inner, preferred_element_type=jnp.float32
    )
    grad_normed_two = fold_rows(
        jnp.einsum("bnf,df->bnd", grad_inner, w_up, preferred_element_type=jnp.float32)
    )
    _, norm_back = jax.vjp(modulated_norm, middle, layer_mod[:, 3], layer_mod[:, 4])
    grad_middle, grad_shift_m, grad_scale_m = norm_back(grad_normed_two)
    grad_middle = grad_middle + grad_out
    grad_gate_a = jnp.sum(grad_middle * branch, axis=1)
    grad_branch = spread_rows((layer_mod[:, 2][:, None, :] * grad_middle).astype(jnp.bfloat16))
    grad_proj = jnp.einsum("bnd,bne->de", grad_branch, attended, preferred_element_type=jnp.float32)
    grad_att = jnp.einsum(
        "bnd,de->bne", grad_branch, w_proj, preferred_element_type=jnp.float32
    ).astype(jnp.bfloat16)
    grad_att = grad_att.reshape(queries.shape)
    scores = score_block(queries, key_heads)
    soft_float = jnp.exp(scores - logsum)
    softmax_w = soft_float.astype(jnp.bfloat16)
    grad_values = jnp.einsum(
        "bhnm,bnhe->bmhe", softmax_w, grad_att, preferred_element_type=jnp.float32
    ).astype(jnp.bfloat16)
    grad_soft = jnp.einsum("bnhe,bmhe->bhnm", grad_att, values, preferred_element_type=jnp.float32)
    row_delta = jnp.sum(soft_float * grad_soft, axis=-1, keepdims=True)
    grad_scores = (soft_float * (grad_soft - row_delta)).astype(jnp.bfloat16)
    grad_queries = (
        jnp.einsum("bhnm,bmhe->bnhe", grad_scores, key_heads, preferred_element_type=jnp.float32)
        * HDIM ** (-0.5)
    ).astype(jnp.bfloat16)
    grad_keys = (
        jnp.einsum("bhnm,bnhe->bmhe", grad_scores, queries, preferred_element_type=jnp.float32)
        * HDIM ** (-0.5)
    ).astype(jnp.bfloat16)
    grad_mixed = jnp.stack([grad_queries, grad_keys, grad_values], axis=2)
    grad_mixed = grad_mixed.reshape(grad_mixed.shape[0], grad_mixed.shape[1], 3, -1)
    grad_qkv = jnp.einsum("bnd,bnte->dte", gathered, grad_mixed, preferred_element_type=jnp.float32)
    grad_normed = fold_rows(
        jnp.einsum("bnte,dte->bnd", grad_mixed, w_qkv, preferred_element_type=jnp.float32)
    )
    _, norm_back_two = jax.vjp(modulated_norm, hidden, layer_mod[:, 0], layer_mod[:, 1])
    grad_hidden, grad_shift_a, grad_scale_a = norm_back_two(grad_normed)
    grad_hidden = grad_hidden + grad_middle
    grad_layer_mod = jnp.stack(
        [grad_shift_a, grad_scale_a, grad_gate_a, grad_shift_m, grad_scale_m, grad_gate_m], axis=1
    )
    return (grad_hidden, grad_layer_mod, (grad_qkv, grad_proj, grad_up, grad_down))


ORDERS = ((0, 1, 2), (0, 2, 1))
LAG = 2
MESH_ID = pl.DeviceIdType.MESH
NN = (((1,), (0,)), ((), ()))
NT = (((1,), (1,)), ((), ()))
TN = (((0,), (0,)), ((), ()))


def grid_of(dp_count):
    if dp_count == 16:
        return (4, 2, 2)
    sizes = [1, 1, 1]
    rest, prime = dp_count, 2
    while rest > 1:
        while rest % prime == 0:
            sizes[sizes.index(min(sizes))] *= prime
            rest //= prime
        prime += 1
    return tuple(sorted(sizes, reverse=True))


def place(sizes):
    index = lax.axis_index("dp")
    return (index // (sizes[1] * sizes[2]), index // sizes[2] % sizes[1], index % sizes[2])


def peer_of(sizes, spot, axis, other):
    moved = [other if a == axis else spot[a] for a in range(3)]
    return (moved[0] * sizes[1] + moved[1]) * sizes[2] + moved[2], lax.axis_index("tensor")


def dot(left, right, form):
    return lax.dot_general(left, right, form, preferred_element_type=jnp.float32)


def greet(peers):
    barrier = pltpu.get_barrier_semaphore()
    for peer in peers:
        pl.semaphore_signal(barrier, inc=1, device_id=peer, device_id_type=MESH_ID)
    pl.semaphore_wait(barrier, len(peers))


def axis_peers(sizes, spot):
    peers = []
    for axis in range(3):
        for offset in range(1, sizes[axis]):
            peers.append(peer_of(sizes, spot, axis, (spot[axis] + offset) % sizes[axis]))
    return peers


def norm_parts(x):
    centre = x - jnp.mean(x, axis=-1, keepdims=True)
    spread = jnp.mean(centre * centre, axis=-1, keepdims=True)
    rstd = lax.rsqrt(spread + EPS_LAYER)
    return centre * rstd, rstd


def norm_forward(x, shift, scale):
    return (norm_parts(x)[0] * (1.0 + scale) + shift).astype(jnp.bfloat16)


def norm_backward(x, scale, dy):
    xh, rstd = norm_parts(x)
    dxh = dy * (1.0 + scale)
    dx = (
        dxh
        - jnp.mean(dxh, axis=-1, keepdims=True)
        - xh * jnp.mean(dxh * xh, axis=-1, keepdims=True)
    ) * rstd
    return dx, jnp.sum(dy, axis=0, keepdims=True), jnp.sum(dy * xh, axis=0, keepdims=True)


GELU_C = math.sqrt(2.0 / math.pi)


def step_kernel(sizes, layers, total_count, *refs):
    (
        qkv_own,
        proj_own,
        up_own,
        down_own,
        hidden_in,
        timing,
        cond_cols,
        mod_rows,
        velocity,
        time_weight,
        blended,
        head_rows,
        own_grads,
        timing_all,
        cond_out,
        grad_cond_out,
        grad_mod_out,
        sums_out,
        full,
        got_one,
        got_two,
        got_three,
        gathered,
        grad_spread,
        outbox,
        inbox,
        qkv,
        attended,
        hidden,
        middle,
        branch,
        outer,
        inner,
        act,
        grad_inner,
        grad_mixed,
        resid,
        part,
        turned,
        timing_box,
        mod_part,
        mod_low,
        mod_box,
        mod,
        mod_grads,
        mod_grads_low,
        mod_grads_box,
        ends,
        loss_row,
        ends_box,
        sum_part,
        sum_box,
        grad_mods,
        sums,
        small_send,
        small_recv,
        ag_send,
        ag_recv,
        rs_send,
        rs_recv,
        pair_send,
        pair_recv,
        load_sem,
    ) = refs
    low = jnp.bfloat16
    spot = place(sizes)
    my_dp, my_core = lax.axis_index("dp"), lax.axis_index("tensor")
    partner = (my_dp, 1 - my_core)
    waves, rows, columns = 3 * layers, up_own.shape[1], up_own.shape[2]
    samples, half_rows, width = hidden_in.shape
    tokens = 2 * half_rows
    heads_wide = qkv.shape[3] // 3
    pairs = heads_wide // (2 * HDIM)
    mine = pl.ds(pl.multiple_of(my_core * half_rows, half_rows), half_rows)
    theirs = pl.ds(pl.multiple_of((1 - my_core) * half_rows, half_rows), half_rows)
    tile = 384
    per_wave = columns // tile
    chunks = waves * per_wave

    loads = []

    def load(source, row, start, count, where):
        copy = pltpu.make_async_copy(
            source,
            inner.at[where, pl.ds(row * rows, rows), pl.ds(start, count)],
            load_sem.at[len(loads)],
        )
        copy.start()
        loads.append(copy)

    narrow_wide = qkv_own.shape[3]
    for layer in range(layers):
        for kind in range(3):
            load(qkv_own.at[layer, kind], layer, kind * narrow_wide, narrow_wide, 1)
        load(proj_own.at[layer], layer, 3 * narrow_wide, narrow_wide, 1)
        load(up_own.at[layer], 2 * layer, 0, columns, 0)
        load(down_own.at[layer], 2 * layer + 1, 0, columns, 0)
    dp_peers = all_peers(sizes[0] * sizes[1] * sizes[2], False)
    greet(dp_peers + [partner])

    small_unsent = []

    def small(kind, slot, source, target, device):
        return pltpu.make_async_remote_copy(
            src_ref=source,
            dst_ref=target,
            send_sem=small_send.at[kind, slot],
            recv_sem=small_recv.at[kind, slot],
            device_id=device,
            device_id_type=MESH_ID,
        )

    def small_start(copies):
        for copy in copies:
            copy.start()
            small_unsent.append(copy)

    devices = len(dp_peers) + 1
    mod_part[...] = jnp.zeros_like(mod_part)
    mod_grads[...] = jnp.zeros_like(mod_grads)
    time_copies = [
        small(0, i, timing, timing_box.at[my_dp], peer) for i, peer in enumerate(dp_peers)
    ]
    small_start(time_copies)
    timing_box[my_dp] = timing[...]

    for copy in loads:
        copy.wait()
    for wave in range(waves):
        layer, which = wave // 3, wave % 3
        start = layer * rows if which == 0 else (2 * layer + which - 1) * rows
        got = inner[1 if which == 0 else 0, start : start + rows]
        full[wave, spot[0], spot[1], spot[2]] = got.astype(low)

    unsent = []

    def chunk_place(chunk):
        return chunk // per_wave, pl.ds(chunk % per_wave * tile, tile), ORDERS[chunk % 2]

    def gather_copies(chunk, phase):
        wave, lanes, order = chunk_place(chunk)
        axis = order[phase]
        pick = [spot[a] for a in range(3)]
        for earlier in order[:phase]:
            pick[earlier] = slice(None)
        target = full.at[wave, pick[0], pick[1], pick[2], :, lanes]
        return [
            pltpu.make_async_remote_copy(
                src_ref=target,
                dst_ref=target,
                send_sem=ag_send.at[chunk, phase, offset],
                recv_sem=ag_recv.at[chunk, phase, offset],
                device_id=peer_of(sizes, spot, axis, (spot[axis] + offset) % sizes[axis]),
                device_id_type=MESH_ID,
            )
            for offset in range(1, sizes[axis])
        ]

    gather_state = [0]

    def gather_step():
        step = gather_state[0]
        gather_state[0] += 1
        for phase in reversed(range(4)):
            chunk = step - LAG * phase
            if not 0 <= chunk < chunks:
                continue
            if phase > 0:
                for copy in gather_copies(chunk, phase - 1):
                    copy.wait_recv()
            if phase < 3:
                for copy in gather_copies(chunk, phase):
                    copy.start()
                    unsent.append(copy)

    def gather_until(wave):
        while gather_state[0] <= per_wave * (wave + 1) - 1 + 3 * LAG:
            gather_step()

    def gather_more():
        if gather_state[0] < chunks + 3 * LAG:
            gather_step()

    inboxes = (got_one, got_two, got_three)
    rs_unsent = []

    def reduce_copies(chunk, phase):
        wave, lanes, order = chunk_place(chunk)
        order = order[::-1]
        axis = order[phase]
        made = []
        for offset in range(1, sizes[axis]):
            other = (spot[axis] + offset) % sizes[axis]
            pick = [slice(None)] * 3
            for earlier in order[:phase]:
                pick[earlier] = spot[earlier]
            pick[axis] = other
            made.append(
                pltpu.make_async_remote_copy(
                    src_ref=full.at[wave, pick[0], pick[1], pick[2], :, lanes],
                    dst_ref=inboxes[phase].at[chunk, offset - 1],
                    send_sem=rs_send.at[chunk, phase, offset],
                    recv_sem=rs_recv.at[chunk, phase, offset],
                    device_id=peer_of(sizes, spot, axis, other),
                    device_id_type=MESH_ID,
                )
            )
        return made

    def reduce_send(chunk, phase):
        for copy in reduce_copies(chunk, phase):
            copy.start()
            rs_unsent.append(copy)

    def reduce_absorb(chunk, phase):
        for copy in reduce_copies(chunk, phase):
            copy.wait_recv()
        wave, lanes, order = chunk_place(chunk)
        order = order[::-1]
        box = inboxes[phase]
        peers = sizes[order[phase]] - 1
        left = sorted(order[phase + 1 :])
        if not left:
            total = full[wave, spot[0], spot[1], spot[2], :, lanes].astype(jnp.float32)
            for p in range(peers):
                total = total + box[chunk, p].astype(jnp.float32)
            own_grads[wave, :, lanes] = total
            return
        span = math.prod(sizes[a] for a in left)

        def body(step, carry):
            index = (step,) if len(left) == 1 else (step // sizes[left[1]], step % sizes[left[1]])
            pick = list(spot)
            for a, i in zip(left, index):
                pick[a] = i
            total = full[wave, pick[0], pick[1], pick[2], :, lanes].astype(jnp.float32)
            for p in range(peers):
                total = total + box[(chunk, p) + index].astype(jnp.float32)
            full[wave, pick[0], pick[1], pick[2], :, lanes] = total.astype(low)
            return carry

        lax.fori_loop(0, span, body, 0)

    produced = []
    reduce_state = [0]

    def reduce_step():
        step = reduce_state[0]
        if step >= chunks + 3 * LAG or (step < chunks and step >= len(produced)):
            return False
        reduce_state[0] += 1
        for phase in (3, 2, 1):
            at = step - phase * LAG
            if 0 <= at < chunks:
                reduce_absorb(produced[at], phase - 1)
                if phase < 3:
                    reduce_send(produced[at], phase)
        if step < chunks:
            reduce_send(produced[step], 0)
        return True

    def reduce_more(count=1):
        for _ in range(count):
            reduce_step()

    def spread_copy(buffer, slot, stage, b):
        return pltpu.make_async_remote_copy(
            src_ref=buffer.at[slot, b, mine],
            dst_ref=buffer.at[slot, b, mine],
            send_sem=pair_send.at[stage, b],
            recv_sem=pair_recv.at[stage, b],
            device_id=partner,
            device_id_type=MESH_ID,
        )

    pair_unsent = []
    out_turn = {}
    out_last = {}

    def spread(buffer, slot, stage, b, value):
        buffer[slot, b, mine] = value
        copy = spread_copy(buffer, slot, stage, b)
        copy.start()
        pair_unsent.append(copy)

    def fold_copy(slot, stage, b):
        return pltpu.make_async_remote_copy(
            src_ref=outbox.at[out_turn[slot] % 2, b],
            dst_ref=inbox.at[slot, b],
            send_sem=pair_send.at[stage, b],
            recv_sem=pair_recv.at[stage, b],
            device_id=partner,
            device_id_type=MESH_ID,
        )

    def fold(slot, stage, b, value):
        turn = out_turn.setdefault(slot, len(out_turn))
        part[b] = value
        if (turn % 2, b) in out_last:
            out_last[turn % 2, b].wait_send()
        outbox[turn % 2, b] = part[b, theirs].astype(low)
        copy = fold_copy(slot, stage, b)
        copy.start()
        out_last[turn % 2, b] = copy

    def folded(slot, stage, b):
        fold_copy(slot, stage, b).wait_recv()
        return part[b, mine] + inbox[slot, b].astype(jnp.float32)

    def each_sample(body, between=lambda: None):
        for b in range(samples):
            body(b)
            between()

    def weight(wave):
        return full[wave].reshape(width, columns)

    def weight_lanes(wave, lanes, count):
        return full[wave, :, :, :, :, lanes].reshape(width, count)

    def layer_input(layer, b):
        return hidden_in[b] if layer == 0 else hidden[layer - 1, b]

    vectors = mod_rows.shape[1] // width
    per_core = vectors // 2

    def vec(b, row):
        at = b * per_core + row % per_core
        return mod[row // per_core, at : at + 1]

    lane = lax.broadcasted_iota(jnp.int32, (1, 2 * HDIM), 1)
    first_head = lane < HDIM
    keep = (
        jnp.where(first_head, 1.0, 0.0).astype(low),
        jnp.where(first_head, 0.0, 1.0).astype(low),
    )
    factor = HDIM ** (-0.5)

    def pair_lanes(kind, p):
        return pl.ds(kind * heads_wide + p * 2 * HDIM, 2 * HDIM)

    gather_more()
    gather_more()

    for copy in time_copies:
        copy.wait_recv()
    for j in range(devices):
        for b in range(samples):
            timing_all[b * devices + j : b * devices + j + 1] = timing_box[j, b : b + 1]
    everyone = samples * devices
    time_act = timing_all[:, :width]
    time_act = (time_act * jax.nn.sigmoid(time_act)).astype(low)
    classes = cond_cols.shape[1] - width
    label = timing_all[:, width + FREQ : width + FREQ + 1]
    onehot = lax.broadcasted_iota(jnp.int32, (everyone, classes), 1) == label.astype(jnp.int32)
    cond = dot(time_act, cond_cols[:, :width], NT) + dot(
        jnp.where(onehot, 1.0, 0.0).astype(low), cond_cols[:, width:], NT
    )
    cond_out[...] = cond
    cond_act = (cond * jax.nn.sigmoid(cond)).astype(low)
    for i in range(per_core):
        lanes = pl.ds(pl.multiple_of((my_core * per_core + i) * width, 128), width)
        got = dot(cond_act, mod_rows[:, lanes], NN)
        for j in range(devices):
            for b in range(samples):
                at = b * per_core + i
                mod_part[j, at : at + 1] = got[b * devices + j : b * devices + j + 1]
        if i == per_core // 2:
            gather_more()
    gather_more()
    mod_low[...] = mod_part[...].astype(low)
    mod_copies = [
        small(1, i, mod_low.at[peer[0]], mod_box.at[i], peer) for i, peer in enumerate(dp_peers)
    ]
    small_start(mod_copies)
    for _ in range(4):
        gather_more()
    total_mod = mod_part[my_dp]
    for i, copy in enumerate(mod_copies):
        copy.wait_recv()
        total_mod = total_mod + mod_box[i].astype(jnp.float32)
    mod[my_core] = total_mod
    mod_pair = small(2, 0, mod.at[my_core], mod.at[my_core], partner)
    small_start([mod_pair])
    gather_more()
    mod_pair.wait_recv()
    for layer in range(layers):
        row = 6 * layer
        sa, sb, sc, sd = (8 * layer + i for i in range(4))

        def first(b):
            if layer == 0:
                x = hidden_in[b]
            else:
                x = middle[layer - 1, b] + vec(b, row - 1) * outer[layer - 1, b]
            if layer > 0:
                hidden[layer - 1, b] = x
            spread(gathered, 2 * layer, sa, b, norm_forward(x, vec(b, row), vec(b, row + 1)))

        each_sample(first, gather_more)
        gather_until(3 * layer)

        def attention(b):
            spread_copy(gathered, 2 * layer, sa, b).wait_recv()
            for kind in range(3):
                lanes = pl.ds(kind * heads_wide, heads_wide)
                qkv[layer, b, :, lanes] = dot(
                    gathered[2 * layer, b], weight_lanes(3 * layer, lanes, heads_wide), NN
                ).astype(low)
            for p in range(pairs):
                q = qkv[layer, b, :, pair_lanes(0, p)]
                k = qkv[layer, b, :, pair_lanes(1, p)]
                v = qkv[layer, b, :, pair_lanes(2, p)]
                got = []
                for h in range(2):
                    s = dot(q, k * keep[h], NT) * factor
                    e = jnp.exp(s - jnp.max(s, axis=-1, keepdims=True))
                    e = e / jnp.sum(e, axis=-1, keepdims=True)
                    got.append(dot(e.astype(low), v, NN))
                attended[layer, b, :, pl.ds(p * 2 * HDIM, 2 * HDIM)] = jnp.where(
                    first_head, got[0], got[1]
                ).astype(low)
            fold(
                4 * layer,
                sb,
                b,
                dot(
                    attended[layer, b],
                    weight_lanes(3 * layer, pl.ds(3 * heads_wide, heads_wide), heads_wide),
                    NT,
                ),
            )

        each_sample(attention, gather_more)

        def second(b):
            got = folded(4 * layer, sb, b)
            branch[layer, b] = got
            x = layer_input(layer, b) + vec(b, row + 2) * got
            middle[layer, b] = x
            spread(gathered, 2 * layer + 1, sc, b, norm_forward(x, vec(b, row + 3), vec(b, row + 4)))

        each_sample(second, gather_more)
        gather_until(3 * layer + 1)

        def widen(b):
            spread_copy(gathered, 2 * layer + 1, sc, b).wait_recv()

            def body(n, carry):
                lanes = pl.ds(pl.multiple_of(n * tile, tile), tile)
                x = dot(gathered[2 * layer + 1, b], weight_lanes(3 * layer + 1, lanes, tile), NN)
                inner[b, :, lanes] = x
                t = jnp.tanh(GELU_C * (x + 0.044715 * x * x * x))
                act[b, :, lanes] = (0.5 * x * (1.0 + t)).astype(low)
                return carry

            lax.fori_loop(0, columns // tile, body, 0)

        each_sample(widen, gather_more)
        gather_until(3 * layer + 2)

        def narrow(b):
            fold(4 * layer + 1, sd, b, dot(act[b], weight(3 * layer + 2), NT))

        each_sample(narrow, gather_more)

        def third(b):
            outer[layer, b] = folded(4 * layer + 1, sd, b)

        each_sample(third)

    for copy in unsent:
        copy.wait_send()

    last = layers - 1
    loss_row[...] = jnp.zeros_like(loss_row)
    ends[...] = jnp.zeros_like(ends)
    pad = pl.ds(PATCH, PATCH)

    def head(b):
        x = middle[last, b] + vec(b, 6 * layers - 1) * outer[last, b]
        shift, scale = vec(b, 6 * layers), vec(b, 6 * layers + 1)
        xh, _ = norm_parts(x)
        normed = (xh * (1.0 + scale) + shift).astype(low)
        predicted = dot(head_rows[...], normed, NT)
        error = predicted - velocity[b]
        weighted = time_weight[b] * error
        loss_row[...] += jnp.sum(weighted * error, axis=0, keepdims=True)
        grad_pred = (2.0 * weighted / total_count).astype(low)
        ends[pad, :width] += dot(grad_pred, normed, NN)
        dx, gshift, gscale = norm_backward(x, scale, dot(grad_pred, head_rows[...], TN))
        mod_grads[b, 6 * layers : 6 * layers + 1] = gshift
        mod_grads[b, 6 * layers + 1 : 6 * layers + 2] = gscale
        resid[b] = dx

    each_sample(head)

    def weight_grad(wave, left, right_of, first_tile, count):
        turned[...] = left.reshape(samples * tokens, width).T
        for n in range(count):
            got = dot(turned[...], right_of(pl.ds(n * tile, tile)), NN)
            lanes = pl.ds((first_tile + n) * tile, tile)
            full[wave, :, :, :, :, lanes] = got.astype(low).reshape(sizes + (rows, tile))
            produced.append(wave * per_wave + first_tile + n)
            if len(produced) <= LAG:
                reduce_step()

    for layer in reversed(range(layers)):
        row = 6 * layer
        se, sf, sg, sh = (8 * layer + 4 + i for i in range(4))

        def grad_first(b):
            g = resid[b]
            mod_grads[b, row + 5 : row + 6] = jnp.sum(g * outer[layer, b], axis=0, keepdims=True)
            spread(grad_spread, 2 * layer, se, b, (vec(b, row + 5) * g).astype(low))

        each_sample(grad_first)

        def grad_wide(b):
            spread_copy(grad_spread, 2 * layer, se, b).wait_recv()

            def body(n, carry):
                lanes = pl.ds(pl.multiple_of(n * tile, tile), tile)
                if layer == last:
                    x = inner[b, :, lanes]
                else:
                    x = dot(
                        gathered[2 * layer + 1, b], weight_lanes(3 * layer + 1, lanes, tile), NN
                    )
                g = dot(grad_spread[2 * layer, b], weight_lanes(3 * layer + 2, lanes, tile), NN)
                t = jnp.tanh(GELU_C * (x + 0.044715 * x * x * x))
                if layer != last:
                    act[b, :, lanes] = (0.5 * x * (1.0 + t)).astype(low)
                slope = 0.5 * (1.0 + t) + 0.5 * x * (1.0 - t * t) * (
                    GELU_C * (1.0 + 3.0 * 0.044715 * x * x)
                )
                grad_inner[b, :, lanes] = (g * slope).astype(low)
                return carry

            lax.fori_loop(0, columns // tile, body, 0)
            fold(4 * layer + 2, sf, b, dot(grad_inner[b], weight(3 * layer + 1), NT))

        each_sample(grad_wide, reduce_more)

        def wide_of(source):
            return lambda lanes: source[:, :, lanes].reshape(samples * tokens, tile)

        weight_grad(3 * layer + 2, grad_spread[2 * layer], wide_of(act), 0, per_wave)
        reduce_more()
        weight_grad(3 * layer + 1, gathered[2 * layer + 1], wide_of(grad_inner), 0, per_wave)
        reduce_more()

        def grad_second(b):
            dy = folded(4 * layer + 2, sf, b)
            dx, gshift, gscale = norm_backward(middle[layer, b], vec(b, row + 4), dy)
            g = dx + resid[b]
            resid[b] = g
            mod_grads[b, row + 3 : row + 4] = gshift
            mod_grads[b, row + 4 : row + 5] = gscale
            mod_grads[b, row + 2 : row + 3] = jnp.sum(g * branch[layer, b], axis=0, keepdims=True)
            spread(grad_spread, 2 * layer + 1, sg, b, (vec(b, row + 2) * g).astype(low))

        each_sample(grad_second)

        def grad_attention(b):
            spread_copy(grad_spread, 2 * layer + 1, sg, b).wait_recv()
            got_all = dot(
                grad_spread[2 * layer + 1, b],
                weight_lanes(3 * layer, pl.ds(3 * heads_wide, heads_wide), heads_wide),
                NN,
            ).astype(low)
            for p in range(pairs):
                ga = got_all[:, p * 2 * HDIM : (p + 1) * 2 * HDIM]
                q = qkv[layer, b, :, pair_lanes(0, p)]
                k = qkv[layer, b, :, pair_lanes(1, p)]
                v = qkv[layer, b, :, pair_lanes(2, p)]
                gq, gk, gv = [], [], []
                for h in range(2):
                    s = dot(k * keep[h], q, NT) * factor
                    e = jnp.exp(s - jnp.max(s, axis=0, keepdims=True))
                    e = e / jnp.sum(e, axis=0, keepdims=True)
                    dp = dot(v * keep[h], ga, NT)
                    ds = (e * (dp - jnp.sum(e * dp, axis=0, keepdims=True))).astype(low)
                    gv.append(dot(e.astype(low), ga, NN))
                    gk.append(dot(ds, q, NN))
                    gq.append(dot(ds, k, TN))
                for kind, got, scale in ((0, gq, factor), (1, gk, factor), (2, gv, 1.0)):
                    grad_mixed[b, :, pair_lanes(kind, p)] = (
                        jnp.where(first_head, got[0], got[1]) * scale
                    ).astype(low)
            fold(
                4 * layer + 3,
                sh,
                b,
                dot(
                    grad_mixed[b],
                    weight_lanes(3 * layer, pl.ds(0, 3 * heads_wide), 3 * heads_wide),
                    NT,
                ),
            )

        each_sample(grad_attention, reduce_more)
        weight_grad(3 * layer, gathered[2 * layer], wide_of(grad_mixed), 0, 3)
        weight_grad(3 * layer, grad_spread[2 * layer + 1], wide_of(attended.at[layer]), 3, 1)

        def grad_third(b):
            dy = folded(4 * layer + 3, sh, b)
            dx, gshift, gscale = norm_backward(layer_input(layer, b), vec(b, row + 1), dy)
            resid[b] = dx + resid[b]
            mod_grads[b, row : row + 1] = gshift
            mod_grads[b, row + 1 : row + 2] = gscale

        reduce_more()
        each_sample(grad_third)

    def patch(b):
        ends[pl.ds(0, PATCH), :width] += dot(blended[b], resid[b].astype(low), NN)

    each_sample(patch)
    ends[0:1, width:] = loss_row[0:1]
    for b in range(samples):
        mod_grads_low[b] = mod_grads[b].astype(low)
    first_pair = small(2, 1, mod_grads_low.at[1 - my_core], mod_grads_box, partner)
    ends_pair = small(2, 2, ends, ends_box, partner)
    small_start([first_pair, ends_pair])
    reduce_more()
    first_pair.wait_recv()
    grad_mods[my_core, my_dp] = (
        mod_grads_low[my_core].astype(jnp.float32) + mod_grads_box[...].astype(jnp.float32)
    ).astype(low)
    share_copies = [
        small(3, i, grad_mods.at[my_core, my_dp], grad_mods.at[my_core, my_dp], peer)
        for i, peer in enumerate(dp_peers)
    ]
    small_start(share_copies)
    reduce_more(2)
    for copy in share_copies:
        copy.wait_recv()
    share_pair = small(2, 3, grad_mods.at[my_core], grad_mods.at[my_core], partner)
    small_start([share_pair])
    reduce_more()
    share_pair.wait_recv()
    slots = grad_mods.shape[2]
    every_row = grad_mods[...].reshape(everyone * slots, width)
    slot = lax.broadcasted_iota(jnp.int32, (everyone * slots, 1), 0) % slots
    grad_cond_act = jnp.zeros((everyone * slots, rows), jnp.float32)
    for i in range(vectors):
        got = dot(every_row, mod_rows[:, pl.ds(i * width, width)], NT)
        grad_cond_act = grad_cond_act + jnp.where(slot == i, got, 0.0)
    grad_cond_act = jnp.sum(grad_cond_act.reshape(everyone, slots, rows), axis=1)
    reduce_more()
    cond = cond_out[...]
    gate = jax.nn.sigmoid(cond)
    grad_cond = grad_cond_act * gate * (1.0 + cond * (1.0 - gate))
    grad_cond_out[...] = grad_cond
    grad_time_act = dot(grad_cond.astype(low), cond_cols[:, :width], NN)
    ends_pair.wait_recv()
    ends_sum = ends[...] + ends_box[...]
    is_first = my_core == 0
    picked = jnp.where(is_first, ends_sum[:everyone, :width], grad_time_act)
    extra = jnp.where(is_first, ends_sum[0:1, width:], 0.0)
    for j in range(devices):
        for b in range(samples):
            sum_part[j, b : b + 1, :width] = picked[b * devices + j : b * devices + j + 1]
            sum_part[j, b : b + 1, width:] = extra
    sum_copies = [
        small(4, i, sum_part.at[peer[0]], sum_box.at[i], peer) for i, peer in enumerate(dp_peers)
    ]
    small_start(sum_copies)
    reduce_more(2)
    total_sum = sum_part[my_dp]
    for i, copy in enumerate(sum_copies):
        copy.wait_recv()
        total_sum = total_sum + sum_box[i]
    sums[my_core, my_dp] = total_sum
    back_copies = [
        small(5, i, sums.at[my_core, my_dp], sums.at[my_core, my_dp], peer)
        for i, peer in enumerate(dp_peers)
    ]
    small_start(back_copies)
    reduce_more(2)
    for copy in back_copies:
        copy.wait_recv()
    sums_pair = small(2, 4, sums.at[my_core], sums.at[my_core], partner)
    small_start([sums_pair])
    spread_act = jnp.broadcast_to(
        (cond * gate)[:, None, :], (everyone, slots, rows)
    ).reshape(everyone * slots, rows)
    stores = []
    per_line = columns // width
    for i in range(vectors):
        left = jnp.where(slot == i, spread_act, 0.0).astype(low)
        line, at = i // per_line, i % per_line * width
        where, start = line % 2, line // 2 * rows
        inner[where, start : start + rows, at : at + width] = dot(left, every_row, TN)
    for line in range(vectors // per_line):
        where, start = line % 2, line // 2 * rows
        copy = pltpu.make_async_copy(
            inner.at[where, pl.ds(start, rows)],
            grad_mod_out.at[:, pl.ds(line * columns, columns)],
            load_sem.at[line],
        )
        copy.start()
        stores.append(copy)
    reduce_more(2)
    sums_pair.wait_recv()
    for core in range(2):
        for j in range(devices):
            for b in range(samples):
                at = b * devices + j
                sums_out[core, at : at + 1] = sums[core, j, b : b + 1]
    while reduce_step():
        pass
    for copy in stores:
        copy.wait()
    for copy in small_unsent:
        copy.wait_send()
    for copy in rs_unsent:
        copy.wait_send()

    for copy in pair_unsent + list(out_last.values()):
        copy.wait_send()


def train_step(
    own_weights,
    hidden,
    timing,
    cond_cols,
    mod_rows,
    velocity,
    time_weight,
    blended,
    head_rows,
    dp_count,
    layers,
    total,
):
    sizes = grid_of(dp_count)
    rows, columns = own_weights[2].shape[1:]
    waves = 3 * layers
    samples, half_rows, width = hidden.shape
    tokens = 2 * half_rows
    tile = columns // 4
    chunks = 4 * waves
    heads_wide = columns // 4
    most = max(sizes)
    slots = 16
    low, wide = jnp.bfloat16, jnp.float32
    in_vmem = pl.BlockSpec(memory_space=pltpu.VMEM)
    in_hbm = pl.BlockSpec(memory_space=pl.ANY)
    stages = 8 * layers
    resid_shape = (layers, samples, half_rows, width)
    dma = pltpu.SemaphoreType.DMA
    everyone = samples * dp_count
    return pl.pallas_call(
        lambda *refs: step_kernel(sizes, layers, total, *refs),
        out_shape=(
            jax.ShapeDtypeStruct((waves, rows, columns), wide),
            jax.ShapeDtypeStruct((everyone, timing.shape[1]), wide),
            jax.ShapeDtypeStruct((everyone, rows), wide),
            jax.ShapeDtypeStruct((everyone, rows), wide),
            jax.ShapeDtypeStruct((rows, mod_rows.shape[1]), wide),
            jax.ShapeDtypeStruct((2, everyone, width + 128), wide),
        ),
        in_specs=[in_hbm] * 4 + [in_vmem] * 8,
        out_specs=(in_vmem,) * 4 + (in_hbm, in_vmem),
        scratch_shapes=[
            pltpu.VMEM((waves,) + sizes + (rows, columns), low),
            pltpu.VMEM((chunks, sizes[2] - 1, sizes[0], sizes[1], rows, tile), low),
            pltpu.VMEM((chunks, sizes[1] - 1, sizes[0], rows, tile), low),
            pltpu.VMEM((chunks, sizes[0] - 1, rows, tile), low),
            pltpu.VMEM((2 * layers, samples, tokens, width), low),
            pltpu.VMEM((2 * layers, samples, tokens, width), low),
            pltpu.VMEM((2, samples, half_rows, width), low),
            pltpu.VMEM((4 * layers, samples, half_rows, width), low),
            pltpu.VMEM((layers, samples, tokens, 3 * heads_wide), low),
            pltpu.VMEM((layers, samples, tokens, heads_wide), low),
            pltpu.VMEM((max(layers - 1, 1),) + resid_shape[1:], wide),
            pltpu.VMEM(resid_shape, wide),
            pltpu.VMEM(resid_shape, wide),
            pltpu.VMEM(resid_shape, wide),
            pltpu.VMEM((samples, tokens, columns), wide),
            pltpu.VMEM((samples, tokens, columns), low),
            pltpu.VMEM((samples, tokens, columns), low),
            pltpu.VMEM((samples, tokens, 3 * heads_wide), low),
            pltpu.VMEM((samples, half_rows, width), wide),
            pltpu.VMEM((samples, tokens, width), wide),
            pltpu.VMEM((width, samples * tokens), low),
            pltpu.VMEM((dp_count,) + timing.shape, wide),
            pltpu.VMEM((dp_count, slots, width), wide),
            pltpu.VMEM((dp_count, slots, width), low),
            pltpu.VMEM((dp_count - 1, slots, width), low),
            pltpu.VMEM((2, slots, width), wide),
            pltpu.VMEM((samples, slots, width), wide),
            pltpu.VMEM((samples, slots, width), low),
            pltpu.VMEM((slots, width), low),
            pltpu.VMEM((2 * PATCH, width + 128), wide),
            pltpu.VMEM((8, half_rows), wide),
            pltpu.VMEM((2 * PATCH, width + 128), wide),
            pltpu.VMEM((dp_count, samples, width + 128), wide),
            pltpu.VMEM((dp_count - 1, samples, width + 128), wide),
            pltpu.VMEM((2, dp_count, slots, width), low),
            pltpu.VMEM((2, dp_count, samples, width + 128), wide),
            dma((6, max(dp_count, 8))),
            dma((6, max(dp_count, 8))),
            dma((chunks, 3, most)),
            dma((chunks, 3, most)),
            dma((chunks, 3, most)),
            dma((chunks, 3, most)),
            dma((stages, samples)),
            dma((stages, samples)),
            dma((6 * layers,)),
        ],
        compiler_params=pltpu.CompilerParams(
            collective_id=0, has_side_effects=True, vmem_limit_bytes=64 * 2**20 - 2**17
        ),
    )(
        *own_weights,
        hidden,
        timing,
        cond_cols,
        mod_rows,
        velocity,
        time_weight,
        blended,
        head_rows,
    )


def all_peers(dp_count, with_cores):
    me, core = lax.axis_index("dp"), lax.axis_index("tensor")
    peers = []
    for offset in range(1, dp_count):
        peers.append(((me + offset) % dp_count, core))
    if with_cores:
        for offset in range(dp_count):
            peers.append(((me + offset) % dp_count, 1 - core))
    return peers


def push(source, target, sems, slot, device):
    return pltpu.make_async_remote_copy(
        src_ref=source,
        dst_ref=target,
        send_sem=sems[0].at[slot],
        recv_sem=sems[1].at[slot],
        device_id=device,
        device_id_type=MESH_ID,
    )


def norm_kernel(dp_count, x, out, box, send, recv):
    peers = all_peers(dp_count, True)
    greet(peers)
    copies = [push(x, box.at[i], (send, recv), i, p) for i, p in enumerate(peers)]
    for copy in copies:
        copy.start()
    total = x[...]
    for i, copy in enumerate(copies):
        copy.wait_recv()
        total = total + box[i]
    out[...] = total
    for copy in copies:
        copy.wait_send()


def sum_norms(x, dp_count):
    dma = pltpu.SemaphoreType.DMA
    count = 2 * dp_count - 1
    return pl.pallas_call(
        lambda *refs: norm_kernel(dp_count, *refs),
        out_shape=jax.ShapeDtypeStruct(x.shape, x.dtype),
        in_specs=[pl.BlockSpec(memory_space=pltpu.VMEM)],
        out_specs=pl.BlockSpec(memory_space=pltpu.VMEM),
        scratch_shapes=[pltpu.VMEM((count,) + x.shape, x.dtype), dma((count,)), dma((count,))],
        compiler_params=pltpu.CompilerParams(collective_id=5, has_side_effects=True),
    )(x)


def gather_plain(blob, dp_count):
    waves, rows, columns = blob.shape
    return lax.all_gather(blob, "dp", axis=1, tiled=True)


def reduce_plain(grads, dp_count):
    return jnp.stack(
        [
            lax.psum_scatter(g.astype(jnp.float32), "dp", scatter_dimension=0, tiled=True)
            for g in grads
        ]
    )


def local(
    latents,
    gaussian,
    velocity,
    time_ids,
    labels,
    small_w,
    small_m,
    small_v,
    cond_w,
    cond_m,
    cond_v,
    mod_w,
    mod_m,
    mod_v,
    qkv_w,
    qkv_m,
    qkv_v,
    proj_w,
    proj_m,
    proj_v,
    up_w,
    up_m,
    up_v,
    down_w,
    down_m,
    down_v,
):
    layer_count = qkv_w.shape[0]
    model_width = mod_w.shape[1] // (6 * layer_count + 2)
    dp_count = lax.axis_size("dp")
    tensor_count = lax.axis_size("tensor")
    samples = latents.shape[0]
    half_rows = latents.shape[2]
    rows = qkv_w.shape[1]
    kernels = rows % 16 == 0 and 2 * layer_count * rows <= 2 * half_rows
    my_dp = lax.axis_index("dp")
    low = jnp.bfloat16

    heads_wide = qkv_w.shape[3]

    small_low = small_w.astype(low)
    patch_rows = small_low[:PATCH]
    time_rows = small_low[PATCH : PATCH + FREQ]
    head_rows = small_low[PATCH + FREQ :]
    mod_low = mod_w.astype(low)

    moment = (time_ids.astype(jnp.float32) + 0.5) / TSTEPS
    blended = ((1.0 - moment)[:, None, None] * latents + moment[:, None, None] * gaussian).astype(
        jnp.bfloat16
    )
    token_index = lax.axis_index("tensor") * half_rows + jnp.arange(half_rows)
    hidden = (
        jnp.einsum("bpn,pd->bnd", blended, patch_rows, preferred_element_type=jnp.float32)
        + position_table(token_index, model_width)[None]
    )
    time_weight = 0.5 + moment
    total_count = samples * dp_count * half_rows * tensor_count * PATCH
    features = time_features(moment).astype(low)
    time_pre = jnp.dot(features, time_rows, preferred_element_type=jnp.float32)
    timing = jnp.concatenate(
        [
            time_pre,
            features.astype(jnp.float32),
            jnp.broadcast_to(labels.astype(jnp.float32)[:, None], (samples, 128)),
        ],
        axis=1,
    )
    if kernels:
        spare = -cond_w.shape[0] % 128
        own_grads, timing_all, cond, grad_cond, grad_mod_w, sums = train_step(
            (
                qkv_w.transpose(0, 2, 1, 3),
                proj_w.transpose(0, 2, 1),
                up_w,
                down_w.transpose(0, 2, 1),
            ),
            hidden,
            timing,
            jnp.pad(cond_w.T.astype(low), ((0, 0), (0, spare))),
            mod_low,
            velocity,
            jnp.broadcast_to(time_weight[:, None, None], velocity.shape),
            blended,
            head_rows,
            dp_count,
            layer_count,
            float(total_count),
        )
        loss_sum = jnp.sum(sums[0, 0, model_width:])
        ends, grad_time_act = sums[0, :, :model_width], sums[1, :, :model_width]
    else:
        timing_all = lax.all_gather(timing, "dp", axis=1, tiled=False)
        timing_all = timing_all.reshape(samples * dp_count, -1)
        time_act = jax.nn.silu(timing_all[:, :model_width]).astype(low)
        all_labels = timing_all[:, model_width + FREQ].astype(jnp.int32)
        onehot = (all_labels[:, None] == jnp.arange(CLASSES)[None, :]).astype(low)
        cond_low = cond_w.astype(low)
        cond = jnp.dot(
            time_act, cond_low[:model_width], preferred_element_type=jnp.float32
        ) + jnp.dot(onehot, cond_low[model_width:], preferred_element_type=jnp.float32)
        modulation = jnp.dot(
            jax.nn.silu(cond).astype(low), mod_low, preferred_element_type=jnp.float32
        ).reshape(samples, dp_count, -1)
        modulation = lax.psum_scatter(modulation, "dp", scatter_dimension=1, tiled=True)[:, 0]
        parts = []
        for i in range(layer_count):
            parts.append(
                jnp.concatenate(
                    [qkv_w[i, :, 0], qkv_w[i, :, 1], qkv_w[i, :, 2], proj_w[i].T], axis=1
                ).astype(low)
            )
            parts.append(up_w[i].astype(low))
            parts.append(down_w[i].T.astype(low))
        blob = jnp.stack(parts)
        full = gather_plain(blob, dp_count)
        saved_list = []
        fetched = []
        for layer_id in range(layer_count):
            packed = full[3 * layer_id]
            weights = (
                packed[:, : 3 * heads_wide].reshape(model_width, 3, heads_wide),
                packed[:, 3 * heads_wide :],
                full[3 * layer_id + 1],
                full[3 * layer_id + 2],
            )
            layer_mod = modulation[
                :, 6 * layer_id * model_width : (6 * layer_id + 6) * model_width
            ].reshape(samples, 6, model_width)
            hidden, saved_state = block_forward(hidden, layer_mod, weights)
            saved_list.append(saved_state)
            fetched.append(weights)
        final_mod = modulation[:, 6 * layer_count * model_width :].reshape(samples, 2, model_width)
        final_normed = modulated_norm(hidden, final_mod[:, 0], final_mod[:, 1]).astype(jnp.bfloat16)
        predicted = jnp.einsum(
            "bnd,pd->bpn", final_normed, head_rows, preferred_element_type=jnp.float32
        )
        error = predicted - velocity
        loss_part = jnp.sum(time_weight[:, None, None] * error * error)
        grad_pred = (time_weight[:, None, None] * (2.0 * error) / total_count).astype(jnp.bfloat16)
        grad_head = jnp.einsum(
            "bpn,bnd->pd", grad_pred, final_normed, preferred_element_type=jnp.float32
        )
        grad_final = jnp.einsum("bpn,pd->bnd", grad_pred, head_rows, preferred_element_type=jnp.float32)
        _, final_back = jax.vjp(modulated_norm, hidden, final_mod[:, 0], final_mod[:, 1])
        grad_hidden, grad_fshift, grad_fscale = final_back(grad_final)
        mod_grads = [None] * layer_count
        layer_grads = [None] * (3 * layer_count)
        for layer_id in reversed(range(layer_count)):
            layer_mod = modulation[
                :, 6 * layer_id * model_width : (6 * layer_id + 6) * model_width
            ].reshape(samples, 6, model_width)
            grad_hidden, grad_layer_mod, grads = block_backward(
                grad_hidden, layer_mod, fetched[layer_id], saved_list[layer_id]
            )
            layer_grads[3 * layer_id] = jnp.concatenate(
                [grads[0].reshape(model_width, 3 * heads_wide).astype(low), grads[1].astype(low)],
                axis=1,
            )
            layer_grads[3 * layer_id + 1] = grads[2].astype(low)
            layer_grads[3 * layer_id + 2] = grads[3].astype(low)
            mod_grads[layer_id] = grad_layer_mod.reshape(samples, 6 * model_width)
        own_grads = reduce_plain(layer_grads, dp_count)
        grad_patch = jnp.einsum(
            "bpn,bnd->pd", blended, grad_hidden.astype(jnp.bfloat16), preferred_element_type=jnp.float32
        )
        ends = jnp.concatenate([grad_patch, grad_head], axis=0)
        all_mods = jnp.concatenate(
            mod_grads
            + [jnp.stack([grad_fshift, grad_fscale], axis=1).reshape(samples, 2 * model_width)],
            axis=1,
        )
        grad_mods = lax.all_gather(lax.psum(all_mods.astype(low), "tensor"), "dp", axis=1)
        grad_mods = grad_mods.reshape(samples * dp_count, -1)
        grad_cond_act = jnp.einsum(
            "be,de->bd", grad_mods, mod_low, preferred_element_type=jnp.float32
        )
        cond_act, silu_back = jax.vjp(jax.nn.silu, cond)
        grad_mod_w = jnp.einsum(
            "bd,be->de", cond_act.astype(low), grad_mods, preferred_element_type=jnp.float32
        )
        grad_cond = silu_back(grad_cond_act)[0]
        grad_time_act = jnp.einsum(
            "be,de->bd",
            grad_cond.astype(low),
            cond_low[:model_width],
            preferred_element_type=jnp.float32,
        )
        ends, grad_time_act, loss_sum = lax.psum(
            (ends, grad_time_act / tensor_count, loss_part), ("dp", "tensor")
        )
    time_pre = timing_all[:, :model_width]
    features = timing_all[:, model_width : model_width + FREQ].astype(low)
    all_labels = timing_all[:, model_width + FREQ].astype(jnp.int32)
    onehot = all_labels[:, None] == jnp.arange(CLASSES)[None, :]
    time_act = jax.nn.silu(time_pre).astype(low)
    grad_temb = grad_cond.astype(low)
    grad_table = jnp.einsum(
        "bc,bd->cd", onehot.astype(jnp.float32), grad_cond, precision=HIGHEST_PREC
    )
    grad_time_two = jnp.einsum("bd,be->de", time_act, grad_temb, preferred_element_type=jnp.float32)
    grad_cond_w = jnp.concatenate([grad_time_two, grad_table], axis=0)
    _, silu_back_two = jax.vjp(jax.nn.silu, time_pre)
    grad_pre = silu_back_two(grad_time_act)[0].astype(low)
    grad_time_one = jnp.einsum("bf,bd->fd", features, grad_pre, preferred_element_type=jnp.float32)
    grad_small = jnp.concatenate([ends[:PATCH], grad_time_one, ends[PATCH:]], axis=0)

    def stacked(kind):
        return jnp.stack([kind(i) for i in range(layer_count)])

    grads_list = [
        grad_small,
        grad_cond_w,
        grad_mod_w,
        stacked(lambda i: own_grads[3 * i][:, : 3 * heads_wide].reshape(rows, 3, heads_wide)),
        stacked(lambda i: own_grads[3 * i][:, 3 * heads_wide :].T),
        stacked(lambda i: own_grads[3 * i + 1]),
        stacked(lambda i: own_grads[3 * i + 2].T),
    ]
    weights_list = [small_w, cond_w, mod_w, qkv_w, proj_w, up_w, down_w]
    firsts_list = [small_m, cond_m, mod_m, qkv_m, proj_m, up_m, down_m]
    seconds_list = [small_v, cond_v, mod_v, qkv_v, proj_v, up_v, down_v]
    shares = [1.0 / (dp_count * tensor_count), 1.0 / tensor_count, 1.0 / tensor_count]
    shares = shares + [1.0] * 4

    def squares(arrays):
        sums = []
        for kind_id, a in enumerate(arrays):
            axes = None if kind_id < 3 else tuple(range(1, a.ndim))
            sums.append(jnp.sum(a * a, axis=axes).reshape(-1) * shares[kind_id])
        return jnp.concatenate(sums)

    results = [
        lamb_parts(weights_list[i], firsts_list[i], seconds_list[i], grads_list[i])
        for i in range(len(weights_list))
    ]
    updates = [r[2] for r in results]
    total_sq = jnp.stack([squares(weights_list), squares(updates)])
    if kernels:
        kinds = total_sq.shape[1]
        total_sq = sum_norms(jnp.pad(total_sq, ((0, 6), (0, 128 - kinds))), dp_count)[:2, :kinds]
    else:
        total_sq = lax.psum(total_sq, ("dp", "tensor"))
    norms = jnp.sqrt(total_sq + EPS_NORM)
    ratio = norms[0] / norms[1]
    outputs = []
    for kind_id in range(7):
        if kind_id < 3:
            factor = ratio[kind_id]
        else:
            first = 3 + (kind_id - 3) * layer_count
            factor = ratio[first : first + layer_count].reshape(
                (layer_count,) + (1,) * (weights_list[kind_id].ndim - 1)
            )
        outputs.append(weights_list[kind_id] - LEARN_RATE * factor * updates[kind_id])
        outputs.append(results[kind_id][0])
        outputs.append(results[kind_id][1])
    return tuple(outputs) + (loss_sum, norms)


def solution(mesh):
    return jax.shard_map(
        local,
        mesh=mesh,
        in_specs=(
            P("dp", None, "tensor"),
            P("dp", None, "tensor"),
            P("dp", None, "tensor"),
            P("dp"),
            P("dp"),
            P(),
            P(),
            P(),
            P(None, "dp"),
            P(None, "dp"),
            P(None, "dp"),
            P("dp", None),
            P("dp", None),
            P("dp", None),
            P(None, "dp", None, "tensor"),
            P(None, "dp", None, "tensor"),
            P(None, "dp", None, "tensor"),
            P(None, "tensor", "dp"),
            P(None, "tensor", "dp"),
            P(None, "tensor", "dp"),
            P(None, "dp", "tensor"),
            P(None, "dp", "tensor"),
            P(None, "dp", "tensor"),
            P(None, "tensor", "dp"),
            P(None, "tensor", "dp"),
            P(None, "tensor", "dp"),
        ),
        out_specs=(
            P(),
            P(),
            P(),
            P(None, "dp"),
            P(None, "dp"),
            P(None, "dp"),
            P("dp", None),
            P("dp", None),
            P("dp", None),
            P(None, "dp", None, "tensor"),
            P(None, "dp", None, "tensor"),
            P(None, "dp", None, "tensor"),
            P(None, "tensor", "dp"),
            P(None, "tensor", "dp"),
            P(None, "tensor", "dp"),
            P(None, "dp", "tensor"),
            P(None, "dp", "tensor"),
            P(None, "dp", "tensor"),
            P(None, "tensor", "dp"),
            P(None, "tensor", "dp"),
            P(None, "tensor", "dp"),
            P(),
            P(),
        ),
        check_vma=False,
    )
```

```python
import math

import jax
import jax.numpy as jnp
from jax import lax
from jax.experimental import pallas as pl
from jax.experimental.pallas import tpu as pltpu
from jax.sharding import PartitionSpec as P

HDIM = 64
PATCH = 16
GRID = 16
FREQ = 256
CLASSES = 1001
TSTEPS = 1000
STEP = 10


HIGHEST_PREC = lax.Precision.HIGHEST
BETA_ONE = 0.9
BETA_TWO = 0.999
EPS_ADAM = 1e-06
EPS_LAYER = 1e-06
EPS_NORM = 1e-12
WEIGHT_DECAY = 0.01
LEARN_RATE = 0.25


def time_features(moment):
    half_freq = FREQ // 2
    frequency = jnp.exp(-math.log(10000.0) * jnp.arange(half_freq).astype(jnp.float32) / half_freq)
    angles = (1000.0 * moment)[:, None] * frequency[None, :]
    return jnp.concatenate([jnp.cos(angles), jnp.sin(angles)], axis=1)


def position_table(token_index, model_width):
    quarter = model_width // 4
    omega_rate = 1.0 / 10000.0 ** (jnp.arange(quarter).astype(jnp.float32) / quarter)
    grid_row = (token_index // GRID).astype(jnp.float32)[:, None] * omega_rate[None, :]
    grid_col = (token_index % GRID).astype(jnp.float32)[:, None] * omega_rate[None, :]
    return jnp.concatenate(
        [jnp.sin(grid_col), jnp.cos(grid_col), jnp.sin(grid_row), jnp.cos(grid_row)], axis=1
    )


def modulated_norm(hidden_in, shift_vec, scale_vec):
    centre = hidden_in - jnp.mean(hidden_in, axis=-1, keepdims=True)
    spread = jnp.mean(centre * centre, axis=-1, keepdims=True)
    return (
        centre * lax.rsqrt(spread + EPS_LAYER) * (1.0 + scale_vec[:, None, :])
        + shift_vec[:, None, :]
    )


def lamb_parts(weight, first, second, grad):
    first_new = BETA_ONE * first + (1.0 - BETA_ONE) * grad
    second_new = BETA_TWO * second + (1.0 - BETA_TWO) * grad * grad
    update = (
        first_new
        / (1.0 - BETA_ONE**STEP)
        / (jnp.sqrt(second_new / (1.0 - BETA_TWO**STEP)) + EPS_ADAM)
        + WEIGHT_DECAY * weight
    )
    return (first_new, second_new, update)


def gelu_tanh(values_in):
    return jax.nn.gelu(values_in, approximate=True)


def spread_rows(part_rows):
    return lax.all_gather(part_rows, "tensor", axis=1, tiled=True)


def fold_rows(term_rows):
    return lax.psum_scatter(
        term_rows.astype(jnp.bfloat16), "tensor", scatter_dimension=1, tiled=True
    ).astype(jnp.float32)


def split_heads(gathered, w_qkv):
    mixed = jnp.einsum("bnd,dte->bnte", gathered, w_qkv, preferred_element_type=jnp.float32).astype(
        jnp.bfloat16
    )
    shaped = mixed.reshape(mixed.shape[0], mixed.shape[1], 3, -1, HDIM)
    return (shaped[:, :, 0], shaped[:, :, 1], shaped[:, :, 2])


def score_block(queries, key_heads):
    return jnp.einsum(
        "bnhe,bmhe->bhnm", queries, key_heads, preferred_element_type=jnp.float32
    ) * HDIM ** (-0.5)


def block_forward(hidden, layer_mod, weights):
    w_qkv, w_proj, w_up, w_down = weights
    normed = modulated_norm(hidden, layer_mod[:, 0], layer_mod[:, 1]).astype(jnp.bfloat16)
    gathered = spread_rows(normed)
    queries, key_heads, values = split_heads(gathered, w_qkv)
    scores = score_block(queries, key_heads)
    row_top = jnp.max(scores, axis=-1, keepdims=True)
    logsum = row_top + jnp.log(jnp.sum(jnp.exp(scores - row_top), axis=-1, keepdims=True))
    softmax_w = jnp.exp(scores - logsum).astype(jnp.bfloat16)
    attended = jnp.einsum(
        "bhnm,bmhe->bnhe", softmax_w, values, preferred_element_type=jnp.float32
    ).astype(jnp.bfloat16)
    attended = attended.reshape(attended.shape[0], attended.shape[1], -1)
    branch = fold_rows(
        jnp.einsum("bne,de->bnd", attended, w_proj, preferred_element_type=jnp.float32)
    )
    middle = hidden + layer_mod[:, 2][:, None, :] * branch
    normed_two = modulated_norm(middle, layer_mod[:, 3], layer_mod[:, 4]).astype(jnp.bfloat16)
    gathered_two = spread_rows(normed_two)
    inner_pre = jnp.einsum("bnd,df->bnf", gathered_two, w_up, preferred_element_type=jnp.float32)
    activ = gelu_tanh(inner_pre).astype(jnp.bfloat16)
    outer_out = fold_rows(
        jnp.einsum("bnf,df->bnd", activ, w_down, preferred_element_type=jnp.float32)
    )
    output = middle + layer_mod[:, 5][:, None, :] * outer_out
    saved_state = (
        hidden,
        gathered,
        queries,
        key_heads,
        values,
        attended,
        logsum,
        branch,
        middle,
        gathered_two,
        inner_pre,
        outer_out,
    )
    return (output, saved_state)


def block_backward(grad_out, layer_mod, weights, saved_state):
    (
        hidden,
        gathered,
        queries,
        key_heads,
        values,
        attended,
        logsum,
        branch,
        middle,
        gathered_two,
        inner_pre,
        outer_out,
    ) = saved_state
    w_qkv, w_proj, w_up, w_down = weights
    grad_gate_m = jnp.sum(grad_out * outer_out, axis=1)
    grad_outer = spread_rows((layer_mod[:, 5][:, None, :] * grad_out).astype(jnp.bfloat16))
    activ = gelu_tanh(inner_pre).astype(jnp.bfloat16)
    grad_down = jnp.einsum("bnd,bnf->df", grad_outer, activ, preferred_element_type=jnp.float32)
    grad_activ = jnp.einsum("bnd,df->bnf", grad_outer, w_down, preferred_element_type=jnp.float32)
    _, gelu_back = jax.vjp(gelu_tanh, inner_pre)
    grad_inner = gelu_back(grad_activ)[0].astype(jnp.bfloat16)
    grad_up = jnp.einsum(
        "bnd,bnf->df", gathered_two, grad_inner, preferred_element_type=jnp.float32
    )
    grad_normed_two = fold_rows(
        jnp.einsum("bnf,df->bnd", grad_inner, w_up, preferred_element_type=jnp.float32)
    )
    _, norm_back = jax.vjp(modulated_norm, middle, layer_mod[:, 3], layer_mod[:, 4])
    grad_middle, grad_shift_m, grad_scale_m = norm_back(grad_normed_two)
    grad_middle = grad_middle + grad_out
    grad_gate_a = jnp.sum(grad_middle * branch, axis=1)
    grad_branch = spread_rows((layer_mod[:, 2][:, None, :] * grad_middle).astype(jnp.bfloat16))
    grad_proj = jnp.einsum("bnd,bne->de", grad_branch, attended, preferred_element_type=jnp.float32)
    grad_att = jnp.einsum(
        "bnd,de->bne", grad_branch, w_proj, preferred_element_type=jnp.float32
    ).astype(jnp.bfloat16)
    grad_att = grad_att.reshape(queries.shape)
    scores = score_block(queries, key_heads)
    soft_float = jnp.exp(scores - logsum)
    softmax_w = soft_float.astype(jnp.bfloat16)
    grad_values = jnp.einsum(
        "bhnm,bnhe->bmhe", softmax_w, grad_att, preferred_element_type=jnp.float32
    ).astype(jnp.bfloat16)
    grad_soft = jnp.einsum("bnhe,bmhe->bhnm", grad_att, values, preferred_element_type=jnp.float32)
    row_delta = jnp.sum(soft_float * grad_soft, axis=-1, keepdims=True)
    grad_scores = (soft_float * (grad_soft - row_delta)).astype(jnp.bfloat16)
    grad_queries = (
        jnp.einsum("bhnm,bmhe->bnhe", grad_scores, key_heads, preferred_element_type=jnp.float32)
        * HDIM ** (-0.5)
    ).astype(jnp.bfloat16)
    grad_keys = (
        jnp.einsum("bhnm,bnhe->bmhe", grad_scores, queries, preferred_element_type=jnp.float32)
        * HDIM ** (-0.5)
    ).astype(jnp.bfloat16)
    grad_mixed = jnp.stack([grad_queries, grad_keys, grad_values], axis=2)
    grad_mixed = grad_mixed.reshape(grad_mixed.shape[0], grad_mixed.shape[1], 3, -1)
    grad_qkv = jnp.einsum("bnd,bnte->dte", gathered, grad_mixed, preferred_element_type=jnp.float32)
    grad_normed = fold_rows(
        jnp.einsum("bnte,dte->bnd", grad_mixed, w_qkv, preferred_element_type=jnp.float32)
    )
    _, norm_back_two = jax.vjp(modulated_norm, hidden, layer_mod[:, 0], layer_mod[:, 1])
    grad_hidden, grad_shift_a, grad_scale_a = norm_back_two(grad_normed)
    grad_hidden = grad_hidden + grad_middle
    grad_layer_mod = jnp.stack(
        [grad_shift_a, grad_scale_a, grad_gate_a, grad_shift_m, grad_scale_m, grad_gate_m], axis=1
    )
    return (grad_hidden, grad_layer_mod, (grad_qkv, grad_proj, grad_up, grad_down))


ORDERS = ((0, 1, 2), (0, 2, 1))
LAG = 2
MESH_ID = pl.DeviceIdType.MESH
NN = (((1,), (0,)), ((), ()))
NT = (((1,), (1,)), ((), ()))
TN = (((0,), (0,)), ((), ()))


def grid_of(dp_count):
    if dp_count == 16:
        return (4, 2, 2)
    sizes = [1, 1, 1]
    rest, prime = dp_count, 2
    while rest > 1:
        while rest % prime == 0:
            sizes[sizes.index(min(sizes))] *= prime
            rest //= prime
        prime += 1
    return tuple(sorted(sizes, reverse=True))


def place(sizes):
    index = lax.axis_index("dp")
    return (index // (sizes[1] * sizes[2]), index // sizes[2] % sizes[1], index % sizes[2])


def peer_of(sizes, spot, axis, other):
    moved = [other if a == axis else spot[a] for a in range(3)]
    return (moved[0] * sizes[1] + moved[1]) * sizes[2] + moved[2], lax.axis_index("tensor")


def dot(left, right, form):
    return lax.dot_general(left, right, form, preferred_element_type=jnp.float32)


def greet(peers):
    barrier = pltpu.get_barrier_semaphore()
    for peer in peers:
        pl.semaphore_signal(barrier, inc=1, device_id=peer, device_id_type=MESH_ID)
    pl.semaphore_wait(barrier, len(peers))


def axis_peers(sizes, spot):
    peers = []
    for axis in range(3):
        for offset in range(1, sizes[axis]):
            peers.append(peer_of(sizes, spot, axis, (spot[axis] + offset) % sizes[axis]))
    return peers


def norm_parts(x):
    centre = x - jnp.mean(x, axis=-1, keepdims=True)
    spread = jnp.mean(centre * centre, axis=-1, keepdims=True)
    rstd = lax.rsqrt(spread + EPS_LAYER)
    return centre * rstd, rstd


def norm_forward(x, shift, scale):
    return (norm_parts(x)[0] * (1.0 + scale) + shift).astype(jnp.bfloat16)


def norm_backward(x, scale, dy):
    xh, rstd = norm_parts(x)
    dxh = dy * (1.0 + scale)
    dx = (
        dxh
        - jnp.mean(dxh, axis=-1, keepdims=True)
        - xh * jnp.mean(dxh * xh, axis=-1, keepdims=True)
    ) * rstd
    return dx, jnp.sum(dy, axis=0, keepdims=True), jnp.sum(dy * xh, axis=0, keepdims=True)


GELU_C = math.sqrt(2.0 / math.pi)


def step_kernel(sizes, layers, total_count, *refs):
    (
        qkv_own,
        proj_own,
        up_own,
        down_own,
        hidden_in,
        timing,
        cond_cols,
        mod_rows,
        velocity,
        time_weight,
        blended,
        head_rows,
        own_grads,
        timing_all,
        cond_out,
        grad_cond_out,
        grad_mod_out,
        sums_out,
        full,
        got_one,
        got_two,
        got_three,
        gathered,
        grad_spread,
        outbox,
        inbox,
        qkv,
        attended,
        hidden,
        middle,
        branch,
        outer,
        inner,
        act,
        grad_inner,
        grad_mixed,
        resid,
        part,
        turned,
        timing_box,
        mod_part,
        mod_low,
        mod_box,
        mod,
        mod_grads,
        mod_grads_low,
        mod_grads_box,
        ends,
        loss_row,
        ends_box,
        sum_part,
        sum_box,
        grad_mods,
        sums,
        small_send,
        small_recv,
        ag_send,
        ag_recv,
        rs_send,
        rs_recv,
        pair_send,
        pair_recv,
        load_sem,
    ) = refs
    low = jnp.bfloat16
    spot = place(sizes)
    my_dp, my_core = lax.axis_index("dp"), lax.axis_index("tensor")
    partner = (my_dp, 1 - my_core)
    waves, rows, columns = 3 * layers, up_own.shape[1], up_own.shape[2]
    samples, half_rows, width = hidden_in.shape
    tokens = 2 * half_rows
    heads_wide = qkv.shape[3] // 3
    pairs = heads_wide // (2 * HDIM)
    mine = pl.ds(pl.multiple_of(my_core * half_rows, half_rows), half_rows)
    theirs = pl.ds(pl.multiple_of((1 - my_core) * half_rows, half_rows), half_rows)
    tile = 384
    per_wave = columns // tile
    chunks = waves * per_wave

    loads = []

    def load(source, row, start, count, where):
        copy = pltpu.make_async_copy(
            source,
            inner.at[where, pl.ds(row * rows, rows), pl.ds(start, count)],
            load_sem.at[len(loads)],
        )
        copy.start()
        loads.append(copy)

    narrow_wide = qkv_own.shape[3]
    for layer in range(layers):
        for kind in range(3):
            load(qkv_own.at[layer, kind], layer, kind * narrow_wide, narrow_wide, 1)
        load(proj_own.at[layer], layer, 3 * narrow_wide, narrow_wide, 1)
        load(up_own.at[layer], 2 * layer, 0, columns, 0)
        load(down_own.at[layer], 2 * layer + 1, 0, columns, 0)
    dp_peers = all_peers(sizes[0] * sizes[1] * sizes[2], False)
    greet(dp_peers + [partner])

    small_unsent = []

    def small(kind, slot, source, target, device):
        return pltpu.make_async_remote_copy(
            src_ref=source,
            dst_ref=target,
            send_sem=small_send.at[kind, slot],
            recv_sem=small_recv.at[kind, slot],
            device_id=device,
            device_id_type=MESH_ID,
        )

    def small_start(copies):
        for copy in copies:
            copy.start()
            small_unsent.append(copy)

    devices = len(dp_peers) + 1
    mod_part[...] = jnp.zeros_like(mod_part)
    mod_grads[...] = jnp.zeros_like(mod_grads)
    time_copies = [
        small(0, i, timing, timing_box.at[my_dp], peer) for i, peer in enumerate(dp_peers)
    ]
    small_start(time_copies)
    timing_box[my_dp] = timing[...]

    for copy in loads:
        copy.wait()
    for wave in range(waves):
        layer, which = wave // 3, wave % 3
        start = layer * rows if which == 0 else (2 * layer + which - 1) * rows
        got = inner[1 if which == 0 else 0, start : start + rows]
        full[wave, spot[0], spot[1], spot[2]] = got.astype(low)

    unsent = []

    def chunk_place(chunk):
        return chunk // per_wave, pl.ds(chunk % per_wave * tile, tile), ORDERS[chunk % 2]

    def gather_copies(chunk, phase):
        wave, lanes, order = chunk_place(chunk)
        axis = order[phase]
        pick = [spot[a] for a in range(3)]
        for earlier in order[:phase]:
            pick[earlier] = slice(None)
        target = full.at[wave, pick[0], pick[1], pick[2], :, lanes]
        return [
            pltpu.make_async_remote_copy(
                src_ref=target,
                dst_ref=target,
                send_sem=ag_send.at[chunk, phase, offset],
                recv_sem=ag_recv.at[chunk, phase, offset],
                device_id=peer_of(sizes, spot, axis, (spot[axis] + offset) % sizes[axis]),
                device_id_type=MESH_ID,
            )
            for offset in range(1, sizes[axis])
        ]

    gather_state = [0]

    def gather_step():
        step = gather_state[0]
        gather_state[0] += 1
        for phase in reversed(range(4)):
            chunk = step - LAG * phase
            if not 0 <= chunk < chunks:
                continue
            if phase > 0:
                for copy in gather_copies(chunk, phase - 1):
                    copy.wait_recv()
            if phase < 3:
                for copy in gather_copies(chunk, phase):
                    copy.start()
                    unsent.append(copy)

    def gather_until(wave):
        while gather_state[0] <= per_wave * (wave + 1) - 1 + 3 * LAG:
            gather_step()

    def gather_more():
        if gather_state[0] < chunks + 3 * LAG:
            gather_step()

    inboxes = (got_one, got_two, got_three)
    rs_unsent = []

    def reduce_copies(chunk, phase):
        wave, lanes, order = chunk_place(chunk)
        order = order[::-1]
        axis = order[phase]
        made = []
        for offset in range(1, sizes[axis]):
            other = (spot[axis] + offset) % sizes[axis]
            pick = [slice(None)] * 3
            for earlier in order[:phase]:
                pick[earlier] = spot[earlier]
            pick[axis] = other
            made.append(
                pltpu.make_async_remote_copy(
                    src_ref=full.at[wave, pick[0], pick[1], pick[2], :, lanes],
                    dst_ref=inboxes[phase].at[chunk, offset - 1],
                    send_sem=rs_send.at[chunk, phase, offset],
                    recv_sem=rs_recv.at[chunk, phase, offset],
                    device_id=peer_of(sizes, spot, axis, other),
                    device_id_type=MESH_ID,
                )
            )
        return made

    def reduce_send(chunk, phase):
        for copy in reduce_copies(chunk, phase):
            copy.start()
            rs_unsent.append(copy)

    def reduce_absorb(chunk, phase):
        for copy in reduce_copies(chunk, phase):
            copy.wait_recv()
        wave, lanes, order = chunk_place(chunk)
        order = order[::-1]
        box = inboxes[phase]
        peers = sizes[order[phase]] - 1
        left = sorted(order[phase + 1 :])
        if not left:
            total = full[wave, spot[0], spot[1], spot[2], :, lanes].astype(jnp.float32)
            for p in range(peers):
                total = total + box[chunk, p].astype(jnp.float32)
            own_grads[wave, :, lanes] = total
            return
        span = math.prod(sizes[a] for a in left)

        def body(step, carry):
            index = (step,) if len(left) == 1 else (step // sizes[left[1]], step % sizes[left[1]])
            pick = list(spot)
            for a, i in zip(left, index):
                pick[a] = i
            total = full[wave, pick[0], pick[1], pick[2], :, lanes].astype(jnp.float32)
            for p in range(peers):
                total = total + box[(chunk, p) + index].astype(jnp.float32)
            full[wave, pick[0], pick[1], pick[2], :, lanes] = total.astype(low)
            return carry

        lax.fori_loop(0, span, body, 0)

    produced = []
    reduce_state = [0]

    def reduce_step():
        step = reduce_state[0]
        if step >= chunks + 3 * LAG or (step < chunks and step >= len(produced)):
            return False
        reduce_state[0] += 1
        for phase in (3, 2, 1):
            at = step - phase * LAG
            if 0 <= at < chunks:
                reduce_absorb(produced[at], phase - 1)
                if phase < 3:
                    reduce_send(produced[at], phase)
        if step < chunks:
            reduce_send(produced[step], 0)
        return True

    def reduce_more(count=1):
        for _ in range(count):
            reduce_step()

    def spread_copy(buffer, slot, stage, b):
        return pltpu.make_async_remote_copy(
            src_ref=buffer.at[slot, b, mine],
            dst_ref=buffer.at[slot, b, mine],
            send_sem=pair_send.at[stage, b],
            recv_sem=pair_recv.at[stage, b],
            device_id=partner,
            device_id_type=MESH_ID,
        )

    pair_unsent = []
    out_turn = {}
    out_last = {}

    def spread(buffer, slot, stage, b, value):
        buffer[slot, b, mine] = value
        copy = spread_copy(buffer, slot, stage, b)
        copy.start()
        pair_unsent.append(copy)

    def fold_copy(slot, stage, b):
        return pltpu.make_async_remote_copy(
            src_ref=outbox.at[out_turn[slot] % 2, b],
            dst_ref=inbox.at[slot, b],
            send_sem=pair_send.at[stage, b],
            recv_sem=pair_recv.at[stage, b],
            device_id=partner,
            device_id_type=MESH_ID,
        )

    def fold(slot, stage, b, value):
        turn = out_turn.setdefault(slot, len(out_turn))
        part[b] = value
        if (turn % 2, b) in out_last:
            out_last[turn % 2, b].wait_send()
        outbox[turn % 2, b] = part[b, theirs].astype(low)
        copy = fold_copy(slot, stage, b)
        copy.start()
        out_last[turn % 2, b] = copy

    def folded(slot, stage, b):
        fold_copy(slot, stage, b).wait_recv()
        return part[b, mine] + inbox[slot, b].astype(jnp.float32)

    def each_sample(body, between=lambda: None):
        for b in range(samples):
            body(b)
            between()

    def weight(wave):
        return full[wave].reshape(width, columns)

    def weight_lanes(wave, lanes, count):
        return full[wave, :, :, :, :, lanes].reshape(width, count)

    def layer_input(layer, b):
        return hidden_in[b] if layer == 0 else hidden[layer - 1, b]

    vectors = mod_rows.shape[1] // width
    per_core = vectors // 2

    def vec(b, row):
        at = b * per_core + row % per_core
        return mod[row // per_core, at : at + 1]

    lane = lax.broadcasted_iota(jnp.int32, (1, 2 * HDIM), 1)
    first_head = lane < HDIM
    keep = (
        jnp.where(first_head, 1.0, 0.0).astype(low),
        jnp.where(first_head, 0.0, 1.0).astype(low),
    )
    factor = HDIM ** (-0.5)

    def pair_lanes(kind, p):
        return pl.ds(kind * heads_wide + p * 2 * HDIM, 2 * HDIM)

    gather_more()
    gather_more()

    for copy in time_copies:
        copy.wait_recv()
    for j in range(devices):
        for b in range(samples):
            timing_all[b * devices + j : b * devices + j + 1] = timing_box[j, b : b + 1]
    everyone = samples * devices
    time_act = timing_all[:, :width]
    time_act = (time_act * jax.nn.sigmoid(time_act)).astype(low)
    classes = cond_cols.shape[1] - width
    label = timing_all[:, width + FREQ : width + FREQ + 1]
    onehot = lax.broadcasted_iota(jnp.int32, (everyone, classes), 1) == label.astype(jnp.int32)
    cond = dot(time_act, cond_cols[:, :width], NT) + dot(
        jnp.where(onehot, 1.0, 0.0).astype(low), cond_cols[:, width:], NT
    )
    cond_out[...] = cond
    cond_act = (cond * jax.nn.sigmoid(cond)).astype(low)
    for i in range(per_core):
        lanes = pl.ds(pl.multiple_of((my_core * per_core + i) * width, 128), width)
        got = dot(cond_act, mod_rows[:, lanes], NN)
        for j in range(devices):
            for b in range(samples):
                at = b * per_core + i
                mod_part[j, at : at + 1] = got[b * devices + j : b * devices + j + 1]
        if i == per_core // 2:
            gather_more()
    gather_more()
    mod_low[...] = mod_part[...].astype(low)
    mod_copies = [
        small(1, i, mod_low.at[peer[0]], mod_box.at[i], peer) for i, peer in enumerate(dp_peers)
    ]
    small_start(mod_copies)
    for _ in range(4):
        gather_more()
    total_mod = mod_part[my_dp]
    for i, copy in enumerate(mod_copies):
        copy.wait_recv()
        total_mod = total_mod + mod_box[i].astype(jnp.float32)
    mod[my_core] = total_mod
    mod_pair = small(2, 0, mod.at[my_core], mod.at[my_core], partner)
    small_start([mod_pair])
    gather_more()
    mod_pair.wait_recv()
    for layer in range(layers):
        row = 6 * layer
        sa, sb, sc, sd = (8 * layer + i for i in range(4))

        def first(b):
            if layer == 0:
                x = hidden_in[b]
            else:
                x = middle[layer - 1, b] + vec(b, row - 1) * outer[layer - 1, b]
            if layer > 0:
                hidden[layer - 1, b] = x
            spread(gathered, 2 * layer, sa, b, norm_forward(x, vec(b, row), vec(b, row + 1)))

        each_sample(first, gather_more)
        gather_until(3 * layer)

        def attention(b):
            spread_copy(gathered, 2 * layer, sa, b).wait_recv()
            for kind in range(3):
                lanes = pl.ds(kind * heads_wide, heads_wide)
                qkv[layer, b, :, lanes] = dot(
                    gathered[2 * layer, b], weight_lanes(3 * layer, lanes, heads_wide), NN
                ).astype(low)
            for p in range(pairs):
                q = qkv[layer, b, :, pair_lanes(0, p)]
                k = qkv[layer, b, :, pair_lanes(1, p)]
                v = qkv[layer, b, :, pair_lanes(2, p)]
                got = []
                for h in range(2):
                    s = dot(q, k * keep[h], NT) * factor
                    e = jnp.exp(s - jnp.max(s, axis=-1, keepdims=True))
                    e = e / jnp.sum(e, axis=-1, keepdims=True)
                    got.append(dot(e.astype(low), v, NN))
                attended[layer, b, :, pl.ds(p * 2 * HDIM, 2 * HDIM)] = jnp.where(
                    first_head, got[0], got[1]
                ).astype(low)
            fold(
                4 * layer,
                sb,
                b,
                dot(
                    attended[layer, b],
                    weight_lanes(3 * layer, pl.ds(3 * heads_wide, heads_wide), heads_wide),
                    NT,
                ),
            )

        each_sample(attention, gather_more)

        def second(b):
            got = folded(4 * layer, sb, b)
            branch[layer, b] = got
            x = layer_input(layer, b) + vec(b, row + 2) * got
            middle[layer, b] = x
            spread(gathered, 2 * layer + 1, sc, b, norm_forward(x, vec(b, row + 3), vec(b, row + 4)))

        each_sample(second, gather_more)
        gather_until(3 * layer + 1)

        def widen(b):
            spread_copy(gathered, 2 * layer + 1, sc, b).wait_recv()

            def body(n, carry):
                lanes = pl.ds(pl.multiple_of(n * tile, tile), tile)
                x = dot(gathered[2 * layer + 1, b], weight_lanes(3 * layer + 1, lanes, tile), NN)
                inner[b, :, lanes] = x
                t = jnp.tanh(GELU_C * (x + 0.044715 * x * x * x))
                act[b, :, lanes] = (0.5 * x * (1.0 + t)).astype(low)
                return carry

            lax.fori_loop(0, columns // tile, body, 0)

        each_sample(widen, gather_more)
        gather_until(3 * layer + 2)

        def narrow(b):
            fold(4 * layer + 1, sd, b, dot(act[b], weight(3 * layer + 2), NT))

        each_sample(narrow, gather_more)

        def third(b):
            outer[layer, b] = folded(4 * layer + 1, sd, b)

        each_sample(third)

    for copy in unsent:
        copy.wait_send()

    last = layers - 1
    loss_row[...] = jnp.zeros_like(loss_row)
    ends[...] = jnp.zeros_like(ends)
    pad = pl.ds(PATCH, PATCH)

    def head(b):
        x = middle[last, b] + vec(b, 6 * layers - 1) * outer[last, b]
        shift, scale = vec(b, 6 * layers), vec(b, 6 * layers + 1)
        xh, _ = norm_parts(x)
        normed = (xh * (1.0 + scale) + shift).astype(low)
        predicted = dot(head_rows[...], normed, NT)
        error = predicted - velocity[b]
        weighted = time_weight[b] * error
        loss_row[...] += jnp.sum(weighted * error, axis=0, keepdims=True)
        grad_pred = (2.0 * weighted / total_count).astype(low)
        ends[pad, :width] += dot(grad_pred, normed, NN)
        dx, gshift, gscale = norm_backward(x, scale, dot(grad_pred, head_rows[...], TN))
        mod_grads[b, 6 * layers : 6 * layers + 1] = gshift
        mod_grads[b, 6 * layers + 1 : 6 * layers + 2] = gscale
        resid[b] = dx

    each_sample(head)

    def weight_grad(wave, left, right_of, first_tile, count):
        turned[...] = left.reshape(samples * tokens, width).T
        for n in range(count):
            got = dot(turned[...], right_of(pl.ds(n * tile, tile)), NN)
            lanes = pl.ds((first_tile + n) * tile, tile)
            full[wave, :, :, :, :, lanes] = got.astype(low).reshape(sizes + (rows, tile))
            produced.append(wave * per_wave + first_tile + n)
            if len(produced) <= LAG:
                reduce_step()

    for layer in reversed(range(layers)):
        row = 6 * layer
        se, sf, sg, sh = (8 * layer + 4 + i for i in range(4))

        def grad_first(b):
            g = resid[b]
            mod_grads[b, row + 5 : row + 6] = jnp.sum(g * outer[layer, b], axis=0, keepdims=True)
            spread(grad_spread, 2 * layer, se, b, (vec(b, row + 5) * g).astype(low))

        each_sample(grad_first)

        def grad_wide(b):
            spread_copy(grad_spread, 2 * layer, se, b).wait_recv()

            def body(n, carry):
                lanes = pl.ds(pl.multiple_of(n * tile, tile), tile)
                if layer == last:
                    x = inner[b, :, lanes]
                else:
                    x = dot(
                        gathered[2 * layer + 1, b], weight_lanes(3 * layer + 1, lanes, tile), NN
                    )
                g = dot(grad_spread[2 * layer, b], weight_lanes(3 * layer + 2, lanes, tile), NN)
                t = jnp.tanh(GELU_C * (x + 0.044715 * x * x * x))
                if layer != last:
                    act[b, :, lanes] = (0.5 * x * (1.0 + t)).astype(low)
                slope = 0.5 * (1.0 + t) + 0.5 * x * (1.0 - t * t) * (
                    GELU_C * (1.0 + 3.0 * 0.044715 * x * x)
                )
                grad_inner[b, :, lanes] = (g * slope).astype(low)
                return carry

            lax.fori_loop(0, columns // tile, body, 0)
            fold(4 * layer + 2, sf, b, dot(grad_inner[b], weight(3 * layer + 1), NT))

        each_sample(grad_wide, reduce_more)

        def wide_of(source):
            return lambda lanes: source[:, :, lanes].reshape(samples * tokens, tile)

        weight_grad(3 * layer + 2, grad_spread[2 * layer], wide_of(act), 0, per_wave)
        reduce_more()
        weight_grad(3 * layer + 1, gathered[2 * layer + 1], wide_of(grad_inner), 0, per_wave)
        reduce_more()

        def grad_second(b):
            dy = folded(4 * layer + 2, sf, b)
            dx, gshift, gscale = norm_backward(middle[layer, b], vec(b, row + 4), dy)
            g = dx + resid[b]
            resid[b] = g
            mod_grads[b, row + 3 : row + 4] = gshift
            mod_grads[b, row + 4 : row + 5] = gscale
            mod_grads[b, row + 2 : row + 3] = jnp.sum(g * branch[layer, b], axis=0, keepdims=True)
            spread(grad_spread, 2 * layer + 1, sg, b, (vec(b, row + 2) * g).astype(low))

        each_sample(grad_second)

        def grad_attention(b):
            spread_copy(grad_spread, 2 * layer + 1, sg, b).wait_recv()
            got_all = dot(
                grad_spread[2 * layer + 1, b],
                weight_lanes(3 * layer, pl.ds(3 * heads_wide, heads_wide), heads_wide),
                NN,
            ).astype(low)
            for p in range(pairs):
                ga = got_all[:, p * 2 * HDIM : (p + 1) * 2 * HDIM]
                q = qkv[layer, b, :, pair_lanes(0, p)]
                k = qkv[layer, b, :, pair_lanes(1, p)]
                v = qkv[layer, b, :, pair_lanes(2, p)]
                gq, gk, gv = [], [], []
                for h in range(2):
                    s = dot(k * keep[h], q, NT) * factor
                    e = jnp.exp(s - jnp.max(s, axis=0, keepdims=True))
                    e = e / jnp.sum(e, axis=0, keepdims=True)
                    dp = dot(v * keep[h], ga, NT)
                    ds = (e * (dp - jnp.sum(e * dp, axis=0, keepdims=True))).astype(low)
                    gv.append(dot(e.astype(low), ga, NN))
                    gk.append(dot(ds, q, NN))
                    gq.append(dot(ds, k, TN))
                for kind, got, scale in ((0, gq, factor), (1, gk, factor), (2, gv, 1.0)):
                    grad_mixed[b, :, pair_lanes(kind, p)] = (
                        jnp.where(first_head, got[0], got[1]) * scale
                    ).astype(low)
            fold(
                4 * layer + 3,
                sh,
                b,
                dot(
                    grad_mixed[b],
                    weight_lanes(3 * layer, pl.ds(0, 3 * heads_wide), 3 * heads_wide),
                    NT,
                ),
            )

        each_sample(grad_attention, reduce_more)
        weight_grad(3 * layer, gathered[2 * layer], wide_of(grad_mixed), 0, 3)
        weight_grad(3 * layer, grad_spread[2 * layer + 1], wide_of(attended.at[layer]), 3, 1)

        def grad_third(b):
            dy = folded(4 * layer + 3, sh, b)
            dx, gshift, gscale = norm_backward(layer_input(layer, b), vec(b, row + 1), dy)
            resid[b] = dx + resid[b]
            mod_grads[b, row : row + 1] = gshift
            mod_grads[b, row + 1 : row + 2] = gscale

        reduce_more()
        each_sample(grad_third)

    def patch(b):
        ends[pl.ds(0, PATCH), :width] += dot(blended[b], resid[b].astype(low), NN)

    each_sample(patch)
    ends[0:1, width:] = loss_row[0:1]
    for b in range(samples):
        mod_grads_low[b] = mod_grads[b].astype(low)
    first_pair = small(2, 1, mod_grads_low.at[1 - my_core], mod_grads_box, partner)
    ends_pair = small(2, 2, ends, ends_box, partner)
    small_start([first_pair, ends_pair])
    reduce_more()
    first_pair.wait_recv()
    grad_mods[my_core, my_dp] = (
        mod_grads_low[my_core].astype(jnp.float32) + mod_grads_box[...].astype(jnp.float32)
    ).astype(low)
    share_copies = [
        small(3, i, grad_mods.at[my_core, my_dp], grad_mods.at[my_core, my_dp], peer)
        for i, peer in enumerate(dp_peers)
    ]
    small_start(share_copies)
    reduce_more(2)
    for copy in share_copies:
        copy.wait_recv()
    share_pair = small(2, 3, grad_mods.at[my_core], grad_mods.at[my_core], partner)
    small_start([share_pair])
    reduce_more()
    share_pair.wait_recv()
    slots = grad_mods.shape[2]
    every_row = grad_mods[...].reshape(everyone * slots, width)
    slot = lax.broadcasted_iota(jnp.int32, (everyone * slots, 1), 0) % slots
    grad_cond_act = jnp.zeros((everyone * slots, rows), jnp.float32)
    for i in range(vectors):
        got = dot(every_row, mod_rows[:, pl.ds(i * width, width)], NT)
        grad_cond_act = grad_cond_act + jnp.where(slot == i, got, 0.0)
    grad_cond_act = jnp.sum(grad_cond_act.reshape(everyone, slots, rows), axis=1)
    reduce_more()
    cond = cond_out[...]
    gate = jax.nn.sigmoid(cond)
    grad_cond = grad_cond_act * gate * (1.0 + cond * (1.0 - gate))
    grad_cond_out[...] = grad_cond
    grad_time_act = dot(grad_cond.astype(low), cond_cols[:, :width], NN)
    ends_pair.wait_recv()
    ends_sum = ends[...] + ends_box[...]
    is_first = my_core == 0
    picked = jnp.where(is_first, ends_sum[:everyone, :width], grad_time_act)
    extra = jnp.where(is_first, ends_sum[0:1, width:], 0.0)
    for j in range(devices):
        for b in range(samples):
            sum_part[j, b : b + 1, :width] = picked[b * devices + j : b * devices + j + 1]
            sum_part[j, b : b + 1, width:] = extra
    sum_copies = [
        small(4, i, sum_part.at[peer[0]], sum_box.at[i], peer) for i, peer in enumerate(dp_peers)
    ]
    small_start(sum_copies)
    reduce_more(2)
    total_sum = sum_part[my_dp]
    for i, copy in enumerate(sum_copies):
        copy.wait_recv()
        total_sum = total_sum + sum_box[i]
    sums[my_core, my_dp] = total_sum
    back_copies = [
        small(5, i, sums.at[my_core, my_dp], sums.at[my_core, my_dp], peer)
        for i, peer in enumerate(dp_peers)
    ]
    small_start(back_copies)
    reduce_more(2)
    for copy in back_copies:
        copy.wait_recv()
    sums_pair = small(2, 4, sums.at[my_core], sums.at[my_core], partner)
    small_start([sums_pair])
    spread_act = jnp.broadcast_to(
        (cond * gate)[:, None, :], (everyone, slots, rows)
    ).reshape(everyone * slots, rows)
    stores = []
    per_line = columns // width
    for i in range(vectors):
        left = jnp.where(slot == i, spread_act, 0.0).astype(low)
        line, at = i // per_line, i % per_line * width
        where, start = line % 2, line // 2 * rows
        inner[where, start : start + rows, at : at + width] = dot(left, every_row, TN)
    for line in range(vectors // per_line):
        where, start = line % 2, line // 2 * rows
        copy = pltpu.make_async_copy(
            inner.at[where, pl.ds(start, rows)],
            grad_mod_out.at[:, pl.ds(line * columns, columns)],
            load_sem.at[line],
        )
        copy.start()
        stores.append(copy)
    reduce_more(2)
    sums_pair.wait_recv()
    for core in range(2):
        for j in range(devices):
            for b in range(samples):
                at = b * devices + j
                sums_out[core, at : at + 1] = sums[core, j, b : b + 1]
    while reduce_step():
        pass
    for copy in stores:
        copy.wait()
    for copy in small_unsent:
        copy.wait_send()
    for copy in rs_unsent:
        copy.wait_send()

    for copy in pair_unsent + list(out_last.values()):
        copy.wait_send()


def train_step(
    own_weights,
    hidden,
    timing,
    cond_cols,
    mod_rows,
    velocity,
    time_weight,
    blended,
    head_rows,
    dp_count,
    layers,
    total,
):
    sizes = grid_of(dp_count)
    rows, columns = own_weights[2].shape[1:]
    waves = 3 * layers
    samples, half_rows, width = hidden.shape
    tokens = 2 * half_rows
    tile = columns // 4
    chunks = 4 * waves
    heads_wide = columns // 4
    most = max(sizes)
    slots = 16
    low, wide = jnp.bfloat16, jnp.float32
    in_vmem = pl.BlockSpec(memory_space=pltpu.VMEM)
    in_hbm = pl.BlockSpec(memory_space=pl.ANY)
    stages = 8 * layers
    resid_shape = (layers, samples, half_rows, width)
    dma = pltpu.SemaphoreType.DMA
    everyone = samples * dp_count
    return pl.pallas_call(
        lambda *refs: step_kernel(sizes, layers, total, *refs),
        out_shape=(
            jax.ShapeDtypeStruct((waves, rows, columns), wide),
            jax.ShapeDtypeStruct((everyone, timing.shape[1]), wide),
            jax.ShapeDtypeStruct((everyone, rows), wide),
            jax.ShapeDtypeStruct((everyone, rows), wide),
            jax.ShapeDtypeStruct((rows, mod_rows.shape[1]), wide),
            jax.ShapeDtypeStruct((2, everyone, width + 128), wide),
        ),
        in_specs=[in_hbm] * 4 + [in_vmem] * 8,
        out_specs=(in_vmem,) * 4 + (in_hbm, in_vmem),
        scratch_shapes=[
            pltpu.VMEM((waves,) + sizes + (rows, columns), low),
            pltpu.VMEM((chunks, sizes[2] - 1, sizes[0], sizes[1], rows, tile), low),
            pltpu.VMEM((chunks, sizes[1] - 1, sizes[0], rows, tile), low),
            pltpu.VMEM((chunks, sizes[0] - 1, rows, tile), low),
            pltpu.VMEM((2 * layers, samples, tokens, width), low),
            pltpu.VMEM((2 * layers, samples, tokens, width), low),
            pltpu.VMEM((2, samples, half_rows, width), low),
            pltpu.VMEM((4 * layers, samples, half_rows, width), low),
            pltpu.VMEM((layers, samples, tokens, 3 * heads_wide), low),
            pltpu.VMEM((layers, samples, tokens, heads_wide), low),
            pltpu.VMEM((max(layers - 1, 1),) + resid_shape[1:], wide),
            pltpu.VMEM(resid_shape, wide),
            pltpu.VMEM(resid_shape, wide),
            pltpu.VMEM(resid_shape, wide),
            pltpu.VMEM((samples, tokens, columns), wide),
            pltpu.VMEM((samples, tokens, columns), low),
            pltpu.VMEM((samples, tokens, columns), low),
            pltpu.VMEM((samples, tokens, 3 * heads_wide), low),
            pltpu.VMEM((samples, half_rows, width), wide),
            pltpu.VMEM((samples, tokens, width), wide),
            pltpu.VMEM((width, samples * tokens), low),
            pltpu.VMEM((dp_count,) + timing.shape, wide),
            pltpu.VMEM((dp_count, slots, width), wide),
            pltpu.VMEM((dp_count, slots, width), low),
            pltpu.VMEM((dp_count - 1, slots, width), low),
            pltpu.VMEM((2, slots, width), wide),
            pltpu.VMEM((samples, slots, width), wide),
            pltpu.VMEM((samples, slots, width), low),
            pltpu.VMEM((slots, width), low),
            pltpu.VMEM((2 * PATCH, width + 128), wide),
            pltpu.VMEM((8, half_rows), wide),
            pltpu.VMEM((2 * PATCH, width + 128), wide),
            pltpu.VMEM((dp_count, samples, width + 128), wide),
            pltpu.VMEM((dp_count - 1, samples, width + 128), wide),
            pltpu.VMEM((2, dp_count, slots, width), low),
            pltpu.VMEM((2, dp_count, samples, width + 128), wide),
            dma((6, max(dp_count, 8))),
            dma((6, max(dp_count, 8))),
            dma((chunks, 3, most)),
            dma((chunks, 3, most)),
            dma((chunks, 3, most)),
            dma((chunks, 3, most)),
            dma((stages, samples)),
            dma((stages, samples)),
            dma((6 * layers,)),
        ],
        compiler_params=pltpu.CompilerParams(
            collective_id=0, has_side_effects=True, vmem_limit_bytes=64 * 2**20 - 2**17
        ),
    )(
        *own_weights,
        hidden,
        timing,
        cond_cols,
        mod_rows,
        velocity,
        time_weight,
        blended,
        head_rows,
    )


def all_peers(dp_count, with_cores):
    me, core = lax.axis_index("dp"), lax.axis_index("tensor")
    peers = []
    for offset in range(1, dp_count):
        peers.append(((me + offset) % dp_count, core))
    if with_cores:
        for offset in range(dp_count):
            peers.append(((me + offset) % dp_count, 1 - core))
    return peers


def push(source, target, sems, slot, device):
    return pltpu.make_async_remote_copy(
        src_ref=source,
        dst_ref=target,
        send_sem=sems[0].at[slot],
        recv_sem=sems[1].at[slot],
        device_id=device,
        device_id_type=MESH_ID,
    )


def norm_kernel(dp_count, x, out, box, send, recv):
    peers = all_peers(dp_count, True)
    greet(peers)
    copies = [push(x, box.at[i], (send, recv), i, p) for i, p in enumerate(peers)]
    for copy in copies:
        copy.start()
    total = x[...]
    for i, copy in enumerate(copies):
        copy.wait_recv()
        total = total + box[i]
    out[...] = total
    for copy in copies:
        copy.wait_send()


def sum_norms(x, dp_count):
    dma = pltpu.SemaphoreType.DMA
    count = 2 * dp_count - 1
    return pl.pallas_call(
        lambda *refs: norm_kernel(dp_count, *refs),
        out_shape=jax.ShapeDtypeStruct(x.shape, x.dtype),
        in_specs=[pl.BlockSpec(memory_space=pltpu.VMEM)],
        out_specs=pl.BlockSpec(memory_space=pltpu.VMEM),
        scratch_shapes=[pltpu.VMEM((count,) + x.shape, x.dtype), dma((count,)), dma((count,))],
        compiler_params=pltpu.CompilerParams(collective_id=5, has_side_effects=True),
    )(x)


def gather_plain(blob, dp_count):
    waves, rows, columns = blob.shape
    return lax.all_gather(blob, "dp", axis=1, tiled=True)


def reduce_plain(grads, dp_count):
    return jnp.stack(
        [
            lax.psum_scatter(g.astype(jnp.float32), "dp", scatter_dimension=0, tiled=True)
            for g in grads
        ]
    )


KINDS = 7


def pieces_of(kind, shape, layers):
    if kind == 0:
        return [((pl.ds(r, 48), slice(None)), 0) for r in range(0, shape[0], 48)]
    if kind == 1:
        split = [0] + list(range(768, shape[1], 512)) + [shape[1]]
        return [((slice(None), pl.ds(a, b - a)), 1) for a, b in zip(split, split[1:])]
    if kind == 2:
        return [((slice(None), pl.ds(c, 768)), 2) for c in range(0, shape[1], 768)]
    found = []
    for layer in range(layers):
        column = 3 + (kind - 3) * layers + layer
        if kind == 3:
            found += [((layer, part), column) for part in range(3)]
        else:
            found.append(((layer,), column))
    return found


def lamb_kernel(layers, shares, *refs):
    weights, firsts, seconds = refs[:7], refs[7:14], refs[14:21]
    own_grads, grad_mod, timing_all, grad_cond, sums = refs[21:26]
    first_out, second_out, update_out = refs[26:33], refs[33:40], refs[40:47]
    norms_out = refs[47]
    w_buf, m_buf, v_buf = refs[48:55], refs[55:62], refs[62:69]
    block_grads, mod_buf, small_buf, cond_buf, in_sem, out_sem, grad_sem = refs[69:]
    low = jnp.bfloat16
    width = small_buf.shape[1]
    heads_wide = w_buf[3].shape[3]
    sequence = (5, 6, 3, 4, 2, 1, 0)
    loads = {}
    block_load = pltpu.make_async_copy(own_grads, block_grads, grad_sem.at[0])
    block_load.start()
    mod_load = pltpu.make_async_copy(grad_mod, mod_buf, grad_sem.at[1])
    for kind in sequence:
        loads[kind] = [
            pltpu.make_async_copy(source[kind], target[kind], in_sem.at[kind, i])
            for i, (source, target) in enumerate(
                ((weights, w_buf), (firsts, m_buf), (seconds, v_buf))
            )
        ]
        for copy in loads[kind]:
            copy.start()
        if kind == 2:
            mod_load.start()

    time_pre = timing_all[:, :width]
    gate = jax.nn.sigmoid(time_pre)
    time_act = (time_pre * gate).astype(low)
    grad_time_act = sums[1, :, :width]
    grad_pre = (grad_time_act * gate * (1.0 + time_pre * (1.0 - gate))).astype(low)
    small_buf[:PATCH] = sums[0, :PATCH, :width]
    small_buf[PATCH : PATCH + FREQ] = dot(
        timing_all[:, width : width + FREQ].astype(low), grad_pre, TN
    )
    small_buf[PATCH + FREQ :] = sums[0, PATCH:, :width]
    label = timing_all[:, width + FREQ : width + FREQ + 1].astype(jnp.int32)
    classes = cond_buf.shape[1] - width
    onehot = lax.broadcasted_iota(jnp.int32, (timing_all.shape[0], classes), 1) == label
    cond_buf[:, :width] = dot(grad_cond[...].astype(low), time_act, TN)
    cond_buf[:, width:] = lax.dot_general(
        grad_cond[...],
        jnp.where(onehot, 1.0, 0.0),
        TN,
        precision=HIGHEST_PREC,
        preferred_element_type=jnp.float32,
    )

    def gradient(kind, index):
        if kind < 3:
            return (small_buf, cond_buf, mod_buf)[kind][index]
        layer = index[0]
        if kind == 3:
            return block_grads[3 * layer, :, pl.ds(index[1] * heads_wide, heads_wide)]
        if kind == 4:
            return block_grads[3 * layer, :, pl.ds(3 * heads_wide, heads_wide)]
        return block_grads[3 * layer + kind - 4]

    lane = lax.broadcasted_iota(jnp.int32, (1, 128), 1)
    norm_rows = [jnp.zeros((1, 128), jnp.float32), jnp.zeros((1, 128), jnp.float32)]
    stores = []
    block_load.wait()
    for kind in sequence:
        for copy in loads[kind]:
            copy.wait()
        if kind == 2:
            mod_load.wait()
        share = shares[kind]
        for index, column in pieces_of(kind, w_buf[kind].shape, layers):
            g = gradient(kind, index)
            weight = w_buf[kind][index]
            first, second, update = lamb_parts(weight, m_buf[kind][index], v_buf[kind][index], g)
            m_buf[kind][index] = first
            v_buf[kind][index] = second
            w_buf[kind][index] = update
            for row, value in enumerate((weight, update)):
                norm_rows[row] = norm_rows[row] + jnp.where(
                    lane == column, share * jnp.sum(value * value), 0.0
                )
        for i, (source, target) in enumerate(
            ((m_buf, first_out), (v_buf, second_out), (w_buf, update_out))
        ):
            copy = pltpu.make_async_copy(source[kind], target[kind], out_sem.at[kind, i])
            copy.start()
            stores.append(copy)
    norms_out[...] = jnp.zeros_like(norms_out)
    norms_out[0:1] = norm_rows[0]
    norms_out[1:2] = norm_rows[1]
    for copy in stores:
        copy.wait()


def lamb_first(weights, firsts, seconds, own_grads, grad_mod, timing_all, grad_cond, sums, shares):
    layers = weights[3].shape[0]
    in_hbm = pl.BlockSpec(memory_space=pl.ANY)
    in_vmem = pl.BlockSpec(memory_space=pltpu.VMEM)
    wide = jnp.float32
    like = [jax.ShapeDtypeStruct(w.shape, wide) for w in weights]
    held = [pltpu.VMEM(w.shape, wide) for w in weights]
    dma = pltpu.SemaphoreType.DMA
    out = pl.pallas_call(
        lambda *refs: lamb_kernel(layers, shares, *refs),
        out_shape=tuple(like * 3 + [jax.ShapeDtypeStruct((8, 128), wide)]),
        in_specs=[in_hbm] * 23 + [in_vmem] * 3,
        out_specs=tuple([in_hbm] * 21 + [in_vmem]),
        scratch_shapes=held * 3
        + [
            pltpu.VMEM(own_grads.shape, wide),
            pltpu.VMEM(grad_mod.shape, wide),
            held[0],
            held[1],
            dma((KINDS, 3)),
            dma((KINDS, 3)),
            dma((2,)),
        ],
        compiler_params=pltpu.CompilerParams(vmem_limit_bytes=64 * 2**20 - 2**17),
    )(*weights, *firsts, *seconds, own_grads, grad_mod, timing_all, grad_cond, sums)
    return out[:7], out[7:14], out[14:21], out[21]


def apply_kernel(layers, *refs):
    norms, weights, updates = refs[0], refs[1:8], refs[8:15]
    outs, w_buf, u_buf, in_sem, out_sem = refs[15:22], refs[22:29], refs[29:36], refs[36], refs[37]
    sequence = (5, 6, 3, 4, 1, 0, 2)
    loads = {}
    for kind in sequence:
        loads[kind] = [
            pltpu.make_async_copy(source[kind], target[kind], in_sem.at[kind, i])
            for i, (source, target) in enumerate(((weights, w_buf), (updates, u_buf)))
        ]
        for copy in loads[kind]:
            copy.start()
    lane = lax.broadcasted_iota(jnp.int32, (1, 128), 1)
    ratio = jnp.sqrt(norms[0:1] + EPS_NORM) / jnp.sqrt(norms[1:2] + EPS_NORM)
    stores = []
    for kind in sequence:
        for copy in loads[kind]:
            copy.wait()
        for index, column in pieces_of(kind, w_buf[kind].shape, layers):
            factor = LEARN_RATE * jnp.sum(jnp.where(lane == column, ratio, 0.0))
            w_buf[kind][index] = w_buf[kind][index] - factor * u_buf[kind][index]
        copy = pltpu.make_async_copy(w_buf[kind], outs[kind], out_sem.at[kind])
        copy.start()
        stores.append(copy)
    for copy in stores:
        copy.wait()


def lamb_last(norms, weights, updates):
    layers = weights[3].shape[0]
    in_hbm = pl.BlockSpec(memory_space=pl.ANY)
    wide = jnp.float32
    held = [pltpu.VMEM(w.shape, wide) for w in weights]
    dma = pltpu.SemaphoreType.DMA
    return pl.pallas_call(
        lambda *refs: apply_kernel(layers, *refs),
        out_shape=tuple(jax.ShapeDtypeStruct(w.shape, wide) for w in weights),
        in_specs=[pl.BlockSpec(memory_space=pltpu.VMEM)] + [in_hbm] * 14,
        out_specs=(in_hbm,) * 7,
        scratch_shapes=held * 2 + [dma((KINDS, 2)), dma((KINDS,))],
        compiler_params=pltpu.CompilerParams(vmem_limit_bytes=64 * 2**20 - 2**17),
    )(norms, *weights, *updates)


def turned_views(small, cond, mod, qkv, proj, up, down):
    return [
        small,
        cond.T,
        mod,
        qkv.transpose(0, 2, 1, 3),
        proj.transpose(0, 2, 1),
        up,
        down.transpose(0, 2, 1),
    ]


def local(
    latents,
    gaussian,
    velocity,
    time_ids,
    labels,
    small_w,
    small_m,
    small_v,
    cond_w,
    cond_m,
    cond_v,
    mod_w,
    mod_m,
    mod_v,
    qkv_w,
    qkv_m,
    qkv_v,
    proj_w,
    proj_m,
    proj_v,
    up_w,
    up_m,
    up_v,
    down_w,
    down_m,
    down_v,
):
    layer_count = qkv_w.shape[0]
    model_width = mod_w.shape[1] // (6 * layer_count + 2)
    dp_count = lax.axis_size("dp")
    tensor_count = lax.axis_size("tensor")
    samples = latents.shape[0]
    half_rows = latents.shape[2]
    rows = qkv_w.shape[1]
    kernels = rows % 16 == 0 and 2 * layer_count * rows <= 2 * half_rows
    my_dp = lax.axis_index("dp")
    low = jnp.bfloat16

    heads_wide = qkv_w.shape[3]

    small_low = small_w.astype(low)
    patch_rows = small_low[:PATCH]
    time_rows = small_low[PATCH : PATCH + FREQ]
    head_rows = small_low[PATCH + FREQ :]
    mod_low = mod_w.astype(low)

    moment = (time_ids.astype(jnp.float32) + 0.5) / TSTEPS
    blended = ((1.0 - moment)[:, None, None] * latents + moment[:, None, None] * gaussian).astype(
        jnp.bfloat16
    )
    token_index = lax.axis_index("tensor") * half_rows + jnp.arange(half_rows)
    hidden = (
        jnp.einsum("bpn,pd->bnd", blended, patch_rows, preferred_element_type=jnp.float32)
        + position_table(token_index, model_width)[None]
    )
    time_weight = 0.5 + moment
    total_count = samples * dp_count * half_rows * tensor_count * PATCH
    features = time_features(moment).astype(low)
    time_pre = jnp.dot(features, time_rows, preferred_element_type=jnp.float32)
    timing = jnp.concatenate(
        [
            time_pre,
            features.astype(jnp.float32),
            jnp.broadcast_to(labels.astype(jnp.float32)[:, None], (samples, 128)),
        ],
        axis=1,
    )
    if kernels:
        spare = -cond_w.shape[0] % 128
        own_grads, timing_all, cond, grad_cond, grad_mod_w, sums = train_step(
            (
                qkv_w.transpose(0, 2, 1, 3),
                proj_w.transpose(0, 2, 1),
                up_w,
                down_w.transpose(0, 2, 1),
            ),
            hidden,
            timing,
            jnp.pad(cond_w.T.astype(low), ((0, 0), (0, spare))),
            mod_low,
            velocity,
            jnp.broadcast_to(time_weight[:, None, None], velocity.shape),
            blended,
            head_rows,
            dp_count,
            layer_count,
            float(total_count),
        )
        loss_sum = jnp.sum(sums[0, 0, model_width:])
        shares = [1.0 / (dp_count * tensor_count), 1.0 / tensor_count, 1.0 / tensor_count]
        weights = turned_views(small_w, cond_w, mod_w, qkv_w, proj_w, up_w, down_w)
        firsts, seconds, updates, squares_sum = lamb_first(
            weights,
            turned_views(small_m, cond_m, mod_m, qkv_m, proj_m, up_m, down_m),
            turned_views(small_v, cond_v, mod_v, qkv_v, proj_v, up_v, down_v),
            own_grads,
            grad_mod_w,
            timing_all,
            grad_cond,
            sums,
            shares + [1.0] * 4,
        )
        squares_sum = sum_norms(squares_sum, dp_count)
        renewed = lamb_last(squares_sum, weights, updates)
        outputs = []
        for triple in zip(*(turned_views(*kind) for kind in (renewed, firsts, seconds))):
            outputs += list(triple)
        norms = jnp.sqrt(squares_sum[:2, : 3 + 4 * layer_count] + EPS_NORM)
        return tuple(outputs) + (loss_sum, norms)
    else:
        timing_all = lax.all_gather(timing, "dp", axis=1, tiled=False)
        timing_all = timing_all.reshape(samples * dp_count, -1)
        time_act = jax.nn.silu(timing_all[:, :model_width]).astype(low)
        all_labels = timing_all[:, model_width + FREQ].astype(jnp.int32)
        onehot = (all_labels[:, None] == jnp.arange(CLASSES)[None, :]).astype(low)
        cond_low = cond_w.astype(low)
        cond = jnp.dot(
            time_act, cond_low[:model_width], preferred_element_type=jnp.float32
        ) + jnp.dot(onehot, cond_low[model_width:], preferred_element_type=jnp.float32)
        modulation = jnp.dot(
            jax.nn.silu(cond).astype(low), mod_low, preferred_element_type=jnp.float32
        ).reshape(samples, dp_count, -1)
        modulation = lax.psum_scatter(modulation, "dp", scatter_dimension=1, tiled=True)[:, 0]
        parts = []
        for i in range(layer_count):
            parts.append(
                jnp.concatenate(
                    [qkv_w[i, :, 0], qkv_w[i, :, 1], qkv_w[i, :, 2], proj_w[i].T], axis=1
                ).astype(low)
            )
            parts.append(up_w[i].astype(low))
            parts.append(down_w[i].T.astype(low))
        blob = jnp.stack(parts)
        full = gather_plain(blob, dp_count)
        saved_list = []
        fetched = []
        for layer_id in range(layer_count):
            packed = full[3 * layer_id]
            weights = (
                packed[:, : 3 * heads_wide].reshape(model_width, 3, heads_wide),
                packed[:, 3 * heads_wide :],
                full[3 * layer_id + 1],
                full[3 * layer_id + 2],
            )
            layer_mod = modulation[
                :, 6 * layer_id * model_width : (6 * layer_id + 6) * model_width
            ].reshape(samples, 6, model_width)
            hidden, saved_state = block_forward(hidden, layer_mod, weights)
            saved_list.append(saved_state)
            fetched.append(weights)
        final_mod = modulation[:, 6 * layer_count * model_width :].reshape(samples, 2, model_width)
        final_normed = modulated_norm(hidden, final_mod[:, 0], final_mod[:, 1]).astype(jnp.bfloat16)
        predicted = jnp.einsum(
            "bnd,pd->bpn", final_normed, head_rows, preferred_element_type=jnp.float32
        )
        error = predicted - velocity
        loss_part = jnp.sum(time_weight[:, None, None] * error * error)
        grad_pred = (time_weight[:, None, None] * (2.0 * error) / total_count).astype(jnp.bfloat16)
        grad_head = jnp.einsum(
            "bpn,bnd->pd", grad_pred, final_normed, preferred_element_type=jnp.float32
        )
        grad_final = jnp.einsum("bpn,pd->bnd", grad_pred, head_rows, preferred_element_type=jnp.float32)
        _, final_back = jax.vjp(modulated_norm, hidden, final_mod[:, 0], final_mod[:, 1])
        grad_hidden, grad_fshift, grad_fscale = final_back(grad_final)
        mod_grads = [None] * layer_count
        layer_grads = [None] * (3 * layer_count)
        for layer_id in reversed(range(layer_count)):
            layer_mod = modulation[
                :, 6 * layer_id * model_width : (6 * layer_id + 6) * model_width
            ].reshape(samples, 6, model_width)
            grad_hidden, grad_layer_mod, grads = block_backward(
                grad_hidden, layer_mod, fetched[layer_id], saved_list[layer_id]
            )
            layer_grads[3 * layer_id] = jnp.concatenate(
                [grads[0].reshape(model_width, 3 * heads_wide).astype(low), grads[1].astype(low)],
                axis=1,
            )
            layer_grads[3 * layer_id + 1] = grads[2].astype(low)
            layer_grads[3 * layer_id + 2] = grads[3].astype(low)
            mod_grads[layer_id] = grad_layer_mod.reshape(samples, 6 * model_width)
        own_grads = reduce_plain(layer_grads, dp_count)
        grad_patch = jnp.einsum(
            "bpn,bnd->pd", blended, grad_hidden.astype(jnp.bfloat16), preferred_element_type=jnp.float32
        )
        ends = jnp.concatenate([grad_patch, grad_head], axis=0)
        all_mods = jnp.concatenate(
            mod_grads
            + [jnp.stack([grad_fshift, grad_fscale], axis=1).reshape(samples, 2 * model_width)],
            axis=1,
        )
        grad_mods = lax.all_gather(lax.psum(all_mods.astype(low), "tensor"), "dp", axis=1)
        grad_mods = grad_mods.reshape(samples * dp_count, -1)
        grad_cond_act = jnp.einsum(
            "be,de->bd", grad_mods, mod_low, preferred_element_type=jnp.float32
        )
        cond_act, silu_back = jax.vjp(jax.nn.silu, cond)
        grad_mod_w = jnp.einsum(
            "bd,be->de", cond_act.astype(low), grad_mods, preferred_element_type=jnp.float32
        )
        grad_cond = silu_back(grad_cond_act)[0]
        grad_time_act = jnp.einsum(
            "be,de->bd",
            grad_cond.astype(low),
            cond_low[:model_width],
            preferred_element_type=jnp.float32,
        )
        ends, grad_time_act, loss_sum = lax.psum(
            (ends, grad_time_act / tensor_count, loss_part), ("dp", "tensor")
        )
    time_pre = timing_all[:, :model_width]
    features = timing_all[:, model_width : model_width + FREQ].astype(low)
    all_labels = timing_all[:, model_width + FREQ].astype(jnp.int32)
    onehot = all_labels[:, None] == jnp.arange(CLASSES)[None, :]
    time_act = jax.nn.silu(time_pre).astype(low)
    grad_temb = grad_cond.astype(low)
    grad_table = jnp.einsum(
        "bc,bd->cd", onehot.astype(jnp.float32), grad_cond, precision=HIGHEST_PREC
    )
    grad_time_two = jnp.einsum("bd,be->de", time_act, grad_temb, preferred_element_type=jnp.float32)
    grad_cond_w = jnp.concatenate([grad_time_two, grad_table], axis=0)
    _, silu_back_two = jax.vjp(jax.nn.silu, time_pre)
    grad_pre = silu_back_two(grad_time_act)[0].astype(low)
    grad_time_one = jnp.einsum("bf,bd->fd", features, grad_pre, preferred_element_type=jnp.float32)
    grad_small = jnp.concatenate([ends[:PATCH], grad_time_one, ends[PATCH:]], axis=0)

    def stacked(kind):
        return jnp.stack([kind(i) for i in range(layer_count)])

    grads_list = [
        grad_small,
        grad_cond_w,
        grad_mod_w,
        stacked(lambda i: own_grads[3 * i][:, : 3 * heads_wide].reshape(rows, 3, heads_wide)),
        stacked(lambda i: own_grads[3 * i][:, 3 * heads_wide :].T),
        stacked(lambda i: own_grads[3 * i + 1]),
        stacked(lambda i: own_grads[3 * i + 2].T),
    ]
    weights_list = [small_w, cond_w, mod_w, qkv_w, proj_w, up_w, down_w]
    firsts_list = [small_m, cond_m, mod_m, qkv_m, proj_m, up_m, down_m]
    seconds_list = [small_v, cond_v, mod_v, qkv_v, proj_v, up_v, down_v]
    shares = [1.0 / (dp_count * tensor_count), 1.0 / tensor_count, 1.0 / tensor_count]
    shares = shares + [1.0] * 4

    def squares(arrays):
        sums = []
        for kind_id, a in enumerate(arrays):
            axes = None if kind_id < 3 else tuple(range(1, a.ndim))
            sums.append(jnp.sum(a * a, axis=axes).reshape(-1) * shares[kind_id])
        return jnp.concatenate(sums)

    results = [
        lamb_parts(weights_list[i], firsts_list[i], seconds_list[i], grads_list[i])
        for i in range(len(weights_list))
    ]
    updates = [r[2] for r in results]
    total_sq = jnp.stack([squares(weights_list), squares(updates)])
    total_sq = lax.psum(total_sq, ("dp", "tensor"))
    norms = jnp.sqrt(total_sq + EPS_NORM)
    ratio = norms[0] / norms[1]
    outputs = []
    for kind_id in range(7):
        if kind_id < 3:
            factor = ratio[kind_id]
        else:
            first = 3 + (kind_id - 3) * layer_count
            factor = ratio[first : first + layer_count].reshape(
                (layer_count,) + (1,) * (weights_list[kind_id].ndim - 1)
            )
        outputs.append(weights_list[kind_id] - LEARN_RATE * factor * updates[kind_id])
        outputs.append(results[kind_id][0])
        outputs.append(results[kind_id][1])
    return tuple(outputs) + (loss_sum, norms)


def solution(mesh):
    return jax.shard_map(
        local,
        mesh=mesh,
        in_specs=(
            P("dp", None, "tensor"),
            P("dp", None, "tensor"),
            P("dp", None, "tensor"),
            P("dp"),
            P("dp"),
            P(),
            P(),
            P(),
            P(None, "dp"),
            P(None, "dp"),
            P(None, "dp"),
            P("dp", None),
            P("dp", None),
            P("dp", None),
            P(None, "dp", None, "tensor"),
            P(None, "dp", None, "tensor"),
            P(None, "dp", None, "tensor"),
            P(None, "tensor", "dp"),
            P(None, "tensor", "dp"),
            P(None, "tensor", "dp"),
            P(None, "dp", "tensor"),
            P(None, "dp", "tensor"),
            P(None, "dp", "tensor"),
            P(None, "tensor", "dp"),
            P(None, "tensor", "dp"),
            P(None, "tensor", "dp"),
        ),
        out_specs=(
            P(),
            P(),
            P(),
            P(None, "dp"),
            P(None, "dp"),
            P(None, "dp"),
            P("dp", None),
            P("dp", None),
            P("dp", None),
            P(None, "dp", None, "tensor"),
            P(None, "dp", None, "tensor"),
            P(None, "dp", None, "tensor"),
            P(None, "tensor", "dp"),
            P(None, "tensor", "dp"),
            P(None, "tensor", "dp"),
            P(None, "dp", "tensor"),
            P(None, "dp", "tensor"),
            P(None, "dp", "tensor"),
            P(None, "tensor", "dp"),
            P(None, "tensor", "dp"),
            P(None, "tensor", "dp"),
            P(),
            P(),
        ),
        check_vma=False,
    )
```

```python
import math

import jax
import jax.numpy as jnp
from jax import lax
from jax.experimental import pallas as pl
from jax.experimental.pallas import tpu as pltpu
from jax.sharding import PartitionSpec as P

HDIM = 64
PATCH = 16
GRID = 16
FREQ = 256
CLASSES = 1001
TSTEPS = 1000
STEP = 10


HIGHEST_PREC = lax.Precision.HIGHEST
BETA_ONE = 0.9
BETA_TWO = 0.999
EPS_ADAM = 1e-06
EPS_LAYER = 1e-06
EPS_NORM = 1e-12
WEIGHT_DECAY = 0.01
LEARN_RATE = 0.25


def time_features(moment):
    half_freq = FREQ // 2
    frequency = jnp.exp(-math.log(10000.0) * jnp.arange(half_freq).astype(jnp.float32) / half_freq)
    angles = (1000.0 * moment)[:, None] * frequency[None, :]
    return jnp.concatenate([jnp.cos(angles), jnp.sin(angles)], axis=1)


def position_table(token_index, model_width):
    quarter = model_width // 4
    omega_rate = 1.0 / 10000.0 ** (jnp.arange(quarter).astype(jnp.float32) / quarter)
    grid_row = (token_index // GRID).astype(jnp.float32)[:, None] * omega_rate[None, :]
    grid_col = (token_index % GRID).astype(jnp.float32)[:, None] * omega_rate[None, :]
    return jnp.concatenate(
        [jnp.sin(grid_col), jnp.cos(grid_col), jnp.sin(grid_row), jnp.cos(grid_row)], axis=1
    )


def modulated_norm(hidden_in, shift_vec, scale_vec):
    centre = hidden_in - jnp.mean(hidden_in, axis=-1, keepdims=True)
    spread = jnp.mean(centre * centre, axis=-1, keepdims=True)
    return (
        centre * lax.rsqrt(spread + EPS_LAYER) * (1.0 + scale_vec[:, None, :])
        + shift_vec[:, None, :]
    )


def lamb_parts(weight, first, second, grad):
    first_new = BETA_ONE * first + (1.0 - BETA_ONE) * grad
    second_new = BETA_TWO * second + (1.0 - BETA_TWO) * grad * grad
    update = (
        first_new
        / (1.0 - BETA_ONE**STEP)
        / (jnp.sqrt(second_new / (1.0 - BETA_TWO**STEP)) + EPS_ADAM)
        + WEIGHT_DECAY * weight
    )
    return (first_new, second_new, update)


def gelu_tanh(values_in):
    return jax.nn.gelu(values_in, approximate=True)


def spread_rows(part_rows):
    return lax.all_gather(part_rows, "tensor", axis=1, tiled=True)


def fold_rows(term_rows):
    return lax.psum_scatter(
        term_rows.astype(jnp.bfloat16), "tensor", scatter_dimension=1, tiled=True
    ).astype(jnp.float32)


def split_heads(gathered, w_qkv):
    mixed = jnp.einsum("bnd,dte->bnte", gathered, w_qkv, preferred_element_type=jnp.float32).astype(
        jnp.bfloat16
    )
    shaped = mixed.reshape(mixed.shape[0], mixed.shape[1], 3, -1, HDIM)
    return (shaped[:, :, 0], shaped[:, :, 1], shaped[:, :, 2])


def score_block(queries, key_heads):
    return jnp.einsum(
        "bnhe,bmhe->bhnm", queries, key_heads, preferred_element_type=jnp.float32
    ) * HDIM ** (-0.5)


def block_forward(hidden, layer_mod, weights):
    w_qkv, w_proj, w_up, w_down = weights
    normed = modulated_norm(hidden, layer_mod[:, 0], layer_mod[:, 1]).astype(jnp.bfloat16)
    gathered = spread_rows(normed)
    queries, key_heads, values = split_heads(gathered, w_qkv)
    scores = score_block(queries, key_heads)
    row_top = jnp.max(scores, axis=-1, keepdims=True)
    logsum = row_top + jnp.log(jnp.sum(jnp.exp(scores - row_top), axis=-1, keepdims=True))
    softmax_w = jnp.exp(scores - logsum).astype(jnp.bfloat16)
    attended = jnp.einsum(
        "bhnm,bmhe->bnhe", softmax_w, values, preferred_element_type=jnp.float32
    ).astype(jnp.bfloat16)
    attended = attended.reshape(attended.shape[0], attended.shape[1], -1)
    branch = fold_rows(
        jnp.einsum("bne,de->bnd", attended, w_proj, preferred_element_type=jnp.float32)
    )
    middle = hidden + layer_mod[:, 2][:, None, :] * branch
    normed_two = modulated_norm(middle, layer_mod[:, 3], layer_mod[:, 4]).astype(jnp.bfloat16)
    gathered_two = spread_rows(normed_two)
    inner_pre = jnp.einsum("bnd,df->bnf", gathered_two, w_up, preferred_element_type=jnp.float32)
    activ = gelu_tanh(inner_pre).astype(jnp.bfloat16)
    outer_out = fold_rows(
        jnp.einsum("bnf,df->bnd", activ, w_down, preferred_element_type=jnp.float32)
    )
    output = middle + layer_mod[:, 5][:, None, :] * outer_out
    saved_state = (
        hidden,
        gathered,
        queries,
        key_heads,
        values,
        attended,
        logsum,
        branch,
        middle,
        gathered_two,
        inner_pre,
        outer_out,
    )
    return (output, saved_state)


def block_backward(grad_out, layer_mod, weights, saved_state):
    (
        hidden,
        gathered,
        queries,
        key_heads,
        values,
        attended,
        logsum,
        branch,
        middle,
        gathered_two,
        inner_pre,
        outer_out,
    ) = saved_state
    w_qkv, w_proj, w_up, w_down = weights
    grad_gate_m = jnp.sum(grad_out * outer_out, axis=1)
    grad_outer = spread_rows((layer_mod[:, 5][:, None, :] * grad_out).astype(jnp.bfloat16))
    activ = gelu_tanh(inner_pre).astype(jnp.bfloat16)
    grad_down = jnp.einsum("bnd,bnf->df", grad_outer, activ, preferred_element_type=jnp.float32)
    grad_activ = jnp.einsum("bnd,df->bnf", grad_outer, w_down, preferred_element_type=jnp.float32)
    _, gelu_back = jax.vjp(gelu_tanh, inner_pre)
    grad_inner = gelu_back(grad_activ)[0].astype(jnp.bfloat16)
    grad_up = jnp.einsum(
        "bnd,bnf->df", gathered_two, grad_inner, preferred_element_type=jnp.float32
    )
    grad_normed_two = fold_rows(
        jnp.einsum("bnf,df->bnd", grad_inner, w_up, preferred_element_type=jnp.float32)
    )
    _, norm_back = jax.vjp(modulated_norm, middle, layer_mod[:, 3], layer_mod[:, 4])
    grad_middle, grad_shift_m, grad_scale_m = norm_back(grad_normed_two)
    grad_middle = grad_middle + grad_out
    grad_gate_a = jnp.sum(grad_middle * branch, axis=1)
    grad_branch = spread_rows((layer_mod[:, 2][:, None, :] * grad_middle).astype(jnp.bfloat16))
    grad_proj = jnp.einsum("bnd,bne->de", grad_branch, attended, preferred_element_type=jnp.float32)
    grad_att = jnp.einsum(
        "bnd,de->bne", grad_branch, w_proj, preferred_element_type=jnp.float32
    ).astype(jnp.bfloat16)
    grad_att = grad_att.reshape(queries.shape)
    scores = score_block(queries, key_heads)
    soft_float = jnp.exp(scores - logsum)
    softmax_w = soft_float.astype(jnp.bfloat16)
    grad_values = jnp.einsum(
        "bhnm,bnhe->bmhe", softmax_w, grad_att, preferred_element_type=jnp.float32
    ).astype(jnp.bfloat16)
    grad_soft = jnp.einsum("bnhe,bmhe->bhnm", grad_att, values, preferred_element_type=jnp.float32)
    row_delta = jnp.sum(soft_float * grad_soft, axis=-1, keepdims=True)
    grad_scores = (soft_float * (grad_soft - row_delta)).astype(jnp.bfloat16)
    grad_queries = (
        jnp.einsum("bhnm,bmhe->bnhe", grad_scores, key_heads, preferred_element_type=jnp.float32)
        * HDIM ** (-0.5)
    ).astype(jnp.bfloat16)
    grad_keys = (
        jnp.einsum("bhnm,bnhe->bmhe", grad_scores, queries, preferred_element_type=jnp.float32)
        * HDIM ** (-0.5)
    ).astype(jnp.bfloat16)
    grad_mixed = jnp.stack([grad_queries, grad_keys, grad_values], axis=2)
    grad_mixed = grad_mixed.reshape(grad_mixed.shape[0], grad_mixed.shape[1], 3, -1)
    grad_qkv = jnp.einsum("bnd,bnte->dte", gathered, grad_mixed, preferred_element_type=jnp.float32)
    grad_normed = fold_rows(
        jnp.einsum("bnte,dte->bnd", grad_mixed, w_qkv, preferred_element_type=jnp.float32)
    )
    _, norm_back_two = jax.vjp(modulated_norm, hidden, layer_mod[:, 0], layer_mod[:, 1])
    grad_hidden, grad_shift_a, grad_scale_a = norm_back_two(grad_normed)
    grad_hidden = grad_hidden + grad_middle
    grad_layer_mod = jnp.stack(
        [grad_shift_a, grad_scale_a, grad_gate_a, grad_shift_m, grad_scale_m, grad_gate_m], axis=1
    )
    return (grad_hidden, grad_layer_mod, (grad_qkv, grad_proj, grad_up, grad_down))


ORDERS = ((0, 1, 2), (0, 2, 1))
LAG = 2
GATHER_PLAN = (
    (3, (0, 1, 2)),
    (3, (0, 2, 1)),
    (1, (2, 1, 0)),
    (2, (0, 1, 2)),
    (2, (0, 2, 1)),
    (1, (1, 2, 0)),
)
GATHER_LAG = 3
MESH_ID = pl.DeviceIdType.MESH
NN = (((1,), (0,)), ((), ()))
NT = (((1,), (1,)), ((), ()))
TN = (((0,), (0,)), ((), ()))


def grid_of(dp_count):
    if dp_count == 16:
        return (4, 2, 2)
    sizes = [1, 1, 1]
    rest, prime = dp_count, 2
    while rest > 1:
        while rest % prime == 0:
            sizes[sizes.index(min(sizes))] *= prime
            rest //= prime
        prime += 1
    return tuple(sorted(sizes, reverse=True))


def place(sizes):
    index = lax.axis_index("dp")
    return (index // (sizes[1] * sizes[2]), index // sizes[2] % sizes[1], index % sizes[2])


def peer_of(sizes, spot, axis, other):
    moved = [other if a == axis else spot[a] for a in range(3)]
    return (moved[0] * sizes[1] + moved[1]) * sizes[2] + moved[2], lax.axis_index("tensor")


def dot(left, right, form):
    return lax.dot_general(left, right, form, preferred_element_type=jnp.float32)


def greet(peers):
    barrier = pltpu.get_barrier_semaphore()
    for peer in peers:
        pl.semaphore_signal(barrier, inc=1, device_id=peer, device_id_type=MESH_ID)
    pl.semaphore_wait(barrier, len(peers))


def axis_peers(sizes, spot):
    peers = []
    for axis in range(3):
        for offset in range(1, sizes[axis]):
            peers.append(peer_of(sizes, spot, axis, (spot[axis] + offset) % sizes[axis]))
    return peers


def norm_parts(x):
    centre = x - jnp.mean(x, axis=-1, keepdims=True)
    spread = jnp.mean(centre * centre, axis=-1, keepdims=True)
    rstd = lax.rsqrt(spread + EPS_LAYER)
    return centre * rstd, rstd


def norm_forward(x, shift, scale):
    return (norm_parts(x)[0] * (1.0 + scale) + shift).astype(jnp.bfloat16)


def norm_backward(x, scale, dy):
    xh, rstd = norm_parts(x)
    dxh = dy * (1.0 + scale)
    dx = (
        dxh
        - jnp.mean(dxh, axis=-1, keepdims=True)
        - xh * jnp.mean(dxh * xh, axis=-1, keepdims=True)
    ) * rstd
    return dx, jnp.sum(dy, axis=0, keepdims=True), jnp.sum(dy * xh, axis=0, keepdims=True)


GELU_C = math.sqrt(2.0 / math.pi)


def step_kernel(sizes, layers, total_count, *refs):
    (
        qkv_own,
        proj_own,
        up_own,
        down_own,
        small_own,
        places,
        latents,
        gaussian,
        moments,
        timing,
        cond_own,
        mod_rows,
        velocity,
        own_grads,
        timing_all,
        cond_out,
        grad_cond_out,
        grad_mod_out,
        sums_out,
        full,
        got_one,
        got_two,
        got_three,
        gathered,
        grad_spread,
        outbox,
        inbox,
        qkv,
        attended,
        hidden,
        middle,
        branch,
        outer,
        inner,
        act,
        grad_inner,
        grad_mixed,
        resid,
        part,
        turned,
        cond_cols,
        end_rows,
        blended,
        timing_box,
        mod_low,
        mod_box,
        mod,
        mod_grads,
        mod_grads_low,
        mod_grads_box,
        ends,
        loss_row,
        ends_box,
        sum_part,
        sum_box,
        grad_mods,
        sums,
        small_send,
        small_recv,
        ag_send,
        ag_recv,
        rs_send,
        rs_recv,
        pair_send,
        pair_recv,
        load_sem,
    ) = refs
    low = jnp.bfloat16
    spot = place(sizes)
    my_dp, my_core = lax.axis_index("dp"), lax.axis_index("tensor")
    partner = (my_dp, 1 - my_core)
    waves, rows, columns = 3 * layers, up_own.shape[1], up_own.shape[2]
    samples, half_rows, width = latents.shape[0], places.shape[0], places.shape[1]
    tokens = 2 * half_rows
    heads_wide = qkv.shape[3] // 3
    pairs = heads_wide // (2 * HDIM)
    mine = pl.ds(pl.multiple_of(my_core * half_rows, half_rows), half_rows)
    theirs = pl.ds(pl.multiple_of((1 - my_core) * half_rows, half_rows), half_rows)
    tile = 384
    per_wave = columns // tile
    chunks = waves * per_wave

    loads = []

    def load(source, row, start, count, where):
        copy = pltpu.make_async_copy(
            source,
            inner.at[where, pl.ds(row * rows, rows), pl.ds(start, count)],
            load_sem.at[len(loads)],
        )
        copy.start()
        loads.append(copy)

    narrow_wide = qkv_own.shape[3]
    for layer in range(layers):
        for kind in range(3):
            load(qkv_own.at[layer, kind], layer, kind * narrow_wide, narrow_wide, 1)
        load(proj_own.at[layer], layer, 3 * narrow_wide, narrow_wide, 1)
        load(up_own.at[layer], 2 * layer, 0, columns, 0)
        load(down_own.at[layer], 2 * layer + 1, 0, columns, 0)
    for row, source in ((0, 0), (PATCH, PATCH + FREQ)):
        copy = pltpu.make_async_copy(
            small_own.at[pl.ds(source, PATCH)],
            end_rows.at[pl.ds(row, PATCH)],
            load_sem.at[len(loads)],
        )
        copy.start()
        loads.append(copy)
    dp_peers = all_peers(sizes[0] * sizes[1] * sizes[2], False)
    greet(dp_peers + [partner])

    small_unsent = []

    def small(kind, slot, source, target, device):
        return pltpu.make_async_remote_copy(
            src_ref=source,
            dst_ref=target,
            send_sem=small_send.at[kind, slot],
            recv_sem=small_recv.at[kind, slot],
            device_id=device,
            device_id_type=MESH_ID,
        )

    def small_start(copies):
        for copy in copies:
            copy.start()
            small_unsent.append(copy)

    devices = len(dp_peers) + 1
    mod_slots = mod_low.shape[1]
    part[0] = jnp.zeros((devices * mod_slots, width), jnp.float32)
    mod_grads[...] = jnp.zeros_like(mod_grads)
    time_copies = [
        small(0, i, timing, timing_box.at[my_dp], peer) for i, peer in enumerate(dp_peers)
    ]
    small_start(time_copies)
    timing_box[my_dp] = timing[...]

    for copy in loads:
        copy.wait()
    for wave in range(waves):
        layer, which = wave // 3, wave % 3
        start = layer * rows if which == 0 else (2 * layer + which - 1) * rows
        got = inner[1 if which == 0 else 0, start : start + rows]
        full[wave, spot[0], spot[1], spot[2]] = got.astype(low)

    unsent = []

    def chunk_place(chunk):
        return chunk // per_wave, pl.ds(chunk % per_wave * tile, tile), ORDERS[chunk % 2]

    plan = []
    for wave in range(waves):
        start = 0
        for count, order in GATHER_PLAN:
            plan.append((wave, start, count * (columns // 12), order))
            start += count * (columns // 12)
    relay = sizes[0] == 4
    stage_count = 4 if relay else 3

    def gather_stages(chunk):
        found = []
        for position, axis in enumerate(plan[chunk][3]):
            if axis == 0 and relay:
                found += [(position, axis, "direct"), (position, axis, "passed")]
            else:
                found.append((position, axis, "all"))
        return found

    def gather_copies(chunk, stage):
        wave, start, count, order = plan[chunk]
        position, axis, how = gather_stages(chunk)[stage]
        line = spot[0]

        def made(slot, source, device):
            pick = [spot[a] for a in range(3)]
            for earlier in order[:position]:
                pick[earlier] = slice(None)
            pick[axis] = source
            target = full.at[wave, pick[0], pick[1], pick[2], :, pl.ds(start, count)]
            return pltpu.make_async_remote_copy(
                src_ref=target,
                dst_ref=target,
                send_sem=ag_send.at[chunk, position, slot],
                recv_sem=ag_recv.at[chunk, position, slot],
                device_id=peer_of(sizes, spot, axis, device),
                device_id_type=MESH_ID,
            )

        if how == "passed":
            end = jnp.where(line >= 2, 3, 0)
            inside = (line == 1) | (line == 2)
            return [(made(0, 3 - end, end), inside, (line == 0) | (line == 3))]
        found = []
        for offset in range(1, sizes[axis]):
            copy = made(offset, spot[axis], (spot[axis] + offset) % sizes[axis])
            if how == "direct" and offset == 1:
                found.append((copy, line < 3, line > 0))
            elif how == "direct" and offset == 3:
                found.append((copy, line > 0, line < 3))
            else:
                found.append((copy, None, None))
        return found

    def when(condition, action):
        if condition is None:
            action()
        else:
            pl.when(condition)(action)

    gather_state = [0]
    gather_end = len(plan) + stage_count * GATHER_LAG

    def gather_step():
        step = gather_state[0]
        gather_state[0] += 1
        for stage in reversed(range(stage_count + 1)):
            chunk = step - GATHER_LAG * stage
            if not 0 <= chunk < len(plan):
                continue
            if stage > 0:
                for copy, _, here in gather_copies(chunk, stage - 1):
                    when(here, copy.wait_recv)
            if stage < stage_count:
                for copy, there, _ in gather_copies(chunk, stage):
                    when(there, copy.start)
                    unsent.append((copy, there))

    def gather_until(wave):
        last_chunk = len(GATHER_PLAN) * (wave + 1) - 1
        while gather_state[0] <= last_chunk + stage_count * GATHER_LAG:
            gather_step()

    def gather_more(count=1):
        for _ in range(count):
            if gather_state[0] < gather_end:
                gather_step()

    inboxes = (got_one, got_two, got_three)
    rs_unsent = []

    def reduce_copies(chunk, phase):
        wave, lanes, order = chunk_place(chunk)
        order = order[::-1]
        axis = order[phase]
        made = []
        for offset in range(1, sizes[axis]):
            other = (spot[axis] + offset) % sizes[axis]
            pick = [slice(None)] * 3
            for earlier in order[:phase]:
                pick[earlier] = spot[earlier]
            pick[axis] = other
            made.append(
                pltpu.make_async_remote_copy(
                    src_ref=full.at[wave, pick[0], pick[1], pick[2], :, lanes],
                    dst_ref=inboxes[phase].at[chunk, offset - 1],
                    send_sem=rs_send.at[chunk, phase, offset],
                    recv_sem=rs_recv.at[chunk, phase, offset],
                    device_id=peer_of(sizes, spot, axis, other),
                    device_id_type=MESH_ID,
                )
            )
        return made

    def reduce_send(chunk, phase):
        for copy in reduce_copies(chunk, phase):
            copy.start()
            rs_unsent.append(copy)

    def reduce_absorb(chunk, phase):
        for copy in reduce_copies(chunk, phase):
            copy.wait_recv()
        wave, lanes, order = chunk_place(chunk)
        order = order[::-1]
        box = inboxes[phase]
        peers = sizes[order[phase]] - 1
        left = sorted(order[phase + 1 :])
        if not left:
            total = full[wave, spot[0], spot[1], spot[2], :, lanes].astype(jnp.float32)
            for p in range(peers):
                total = total + box[chunk, p].astype(jnp.float32)
            own_grads[wave, :, lanes] = total
            return
        span = math.prod(sizes[a] for a in left)

        def body(step, carry):
            index = (step,) if len(left) == 1 else (step // sizes[left[1]], step % sizes[left[1]])
            pick = list(spot)
            for a, i in zip(left, index):
                pick[a] = i
            total = full[wave, pick[0], pick[1], pick[2], :, lanes].astype(jnp.float32)
            for p in range(peers):
                total = total + box[(chunk, p) + index].astype(jnp.float32)
            full[wave, pick[0], pick[1], pick[2], :, lanes] = total.astype(low)
            return carry

        lax.fori_loop(0, span, body, 0)

    produced = []
    reduce_state = [0]

    def reduce_step():
        step = reduce_state[0]
        if step >= chunks + 3 * LAG or (step < chunks and step >= len(produced)):
            return False
        reduce_state[0] += 1
        for phase in (3, 2, 1):
            at = step - phase * LAG
            if 0 <= at < chunks:
                reduce_absorb(produced[at], phase - 1)
                if phase < 3:
                    reduce_send(produced[at], phase)
        if step < chunks:
            reduce_send(produced[step], 0)
        return True

    def reduce_more(count=1):
        for _ in range(count):
            reduce_step()

    def spread_copy(buffer, slot, stage, b):
        return pltpu.make_async_remote_copy(
            src_ref=buffer.at[slot, b, mine],
            dst_ref=buffer.at[slot, b, mine],
            send_sem=pair_send.at[stage, b],
            recv_sem=pair_recv.at[stage, b],
            device_id=partner,
            device_id_type=MESH_ID,
        )

    pair_unsent = []
    out_turn = {}
    out_last = {}

    def spread(buffer, slot, stage, b, value):
        buffer[slot, b, mine] = value
        copy = spread_copy(buffer, slot, stage, b)
        copy.start()
        pair_unsent.append(copy)

    def fold_copy(slot, stage, b):
        return pltpu.make_async_remote_copy(
            src_ref=outbox.at[out_turn[slot] % 2, b],
            dst_ref=inbox.at[slot, b],
            send_sem=pair_send.at[stage, b],
            recv_sem=pair_recv.at[stage, b],
            device_id=partner,
            device_id_type=MESH_ID,
        )

    def fold(slot, stage, b, value):
        turn = out_turn.setdefault(slot, len(out_turn))
        part[b] = value
        if (turn % 2, b) in out_last:
            out_last[turn % 2, b].wait_send()
        outbox[turn % 2, b] = part[b, theirs].astype(low)
        copy = fold_copy(slot, stage, b)
        copy.start()
        out_last[turn % 2, b] = copy

    def folded(slot, stage, b):
        fold_copy(slot, stage, b).wait_recv()
        return part[b, mine] + inbox[slot, b].astype(jnp.float32)

    def each_sample(body, between=lambda: None):
        for b in range(samples):
            body(b)
            between()

    def weight(wave):
        return full[wave].reshape(width, columns)

    def weight_lanes(wave, lanes, count):
        return full[wave, :, :, :, :, lanes].reshape(width, count)

    def layer_input(layer, b):
        return hidden[layer, b]

    vectors = mod_rows.shape[1] // width
    per_core = vectors // 2

    def vec(b, row):
        at = b * per_core + row % per_core
        return mod[row // per_core, at : at + 1]

    lane = lax.broadcasted_iota(jnp.int32, (1, 2 * HDIM), 1)
    first_head = lane < HDIM
    keep = (
        jnp.where(first_head, 1.0, 0.0).astype(low),
        jnp.where(first_head, 0.0, 1.0).astype(low),
    )
    factor = HDIM ** (-0.5)

    def pair_lanes(kind, p):
        return pl.ds(kind * heads_wide + p * 2 * HDIM, 2 * HDIM)

    gather_more(GATHER_LAG)

    patch_rows = end_rows[:PATCH].astype(low)
    head_rows = end_rows[PATCH:].astype(low)
    for b in range(samples):
        moment = moments[b]
        blended[b] = ((1.0 - moment) * latents[b] + moment * gaussian[b]).astype(low)
        hidden[0, b] = dot(blended[b], patch_rows, TN) + places[...]
    cond_count = cond_own.shape[1]
    cond_cols[...] = jnp.zeros_like(cond_cols)
    cond_cols[:, :cond_count] = cond_own[...].astype(low)

    for copy in time_copies:
        copy.wait_recv()
    for j in range(devices):
        for b in range(samples):
            timing_all[b * devices + j : b * devices + j + 1] = timing_box[j, b : b + 1]
    everyone = samples * devices
    time_act = timing_all[:, :width]
    time_act = (time_act * jax.nn.sigmoid(time_act)).astype(low)
    classes = cond_cols.shape[1] - width
    label = timing_all[:, width + FREQ : width + FREQ + 1]
    onehot = lax.broadcasted_iota(jnp.int32, (everyone, classes), 1) == label.astype(jnp.int32)
    cond = dot(time_act, cond_cols[:, :width], NT) + dot(
        jnp.where(onehot, 1.0, 0.0).astype(low), cond_cols[:, width:], NT
    )
    cond_out[...] = cond
    cond_act = (cond * jax.nn.sigmoid(cond)).astype(low)
    for i in range(per_core):
        lanes = pl.ds(pl.multiple_of((my_core * per_core + i) * width, 128), width)
        got = dot(cond_act, mod_rows[:, lanes], NN)
        for j in range(devices):
            for b in range(samples):
                at = j * mod_slots + b * per_core + i
                part[0, at : at + 1] = got[b * devices + j : b * devices + j + 1]
        if i == per_core // 2:
            gather_more(1)
    gather_more(1)
    mod_low[...] = part[0].reshape(devices, mod_slots, width).astype(low)
    mod_copies = [
        small(1, i, mod_low.at[peer[0]], mod_box.at[i], peer) for i, peer in enumerate(dp_peers)
    ]
    small_start(mod_copies)
    gather_more(6)
    total_mod = part[0, pl.ds(pl.multiple_of(my_dp * mod_slots, mod_slots), mod_slots)]
    for i, copy in enumerate(mod_copies):
        copy.wait_recv()
        total_mod = total_mod + mod_box[i].astype(jnp.float32)
    mod[my_core] = total_mod
    mod_pair = small(2, 0, mod.at[my_core], mod.at[my_core], partner)
    small_start([mod_pair])
    gather_more()
    mod_pair.wait_recv()
    for layer in range(layers):
        row = 6 * layer
        sa, sb, sc, sd = (8 * layer + i for i in range(4))

        def first(b):
            if layer == 0:
                x = hidden[0, b]
            else:
                x = middle[layer - 1, b] + vec(b, row - 1) * outer[layer - 1, b]
            if layer > 0:
                hidden[layer, b] = x
            spread(gathered, 2 * layer, sa, b, norm_forward(x, vec(b, row), vec(b, row + 1)))

        each_sample(first, gather_more)
        gather_until(3 * layer)

        def attention(b):
            spread_copy(gathered, 2 * layer, sa, b).wait_recv()
            for kind in range(3):
                lanes = pl.ds(kind * heads_wide, heads_wide)
                qkv[layer, b, :, lanes] = dot(
                    gathered[2 * layer, b], weight_lanes(3 * layer, lanes, heads_wide), NN
                ).astype(low)
            for p in range(pairs):
                q = qkv[layer, b, :, pair_lanes(0, p)]
                k = qkv[layer, b, :, pair_lanes(1, p)]
                v = qkv[layer, b, :, pair_lanes(2, p)]
                got = []
                for h in range(2):
                    s = dot(q, k * keep[h], NT) * factor
                    e = jnp.exp(s - jnp.max(s, axis=-1, keepdims=True))
                    e = e / jnp.sum(e, axis=-1, keepdims=True)
                    got.append(dot(e.astype(low), v, NN))
                attended[layer, b, :, pl.ds(p * 2 * HDIM, 2 * HDIM)] = jnp.where(
                    first_head, got[0], got[1]
                ).astype(low)
            fold(
                4 * layer,
                sb,
                b,
                dot(
                    attended[layer, b],
                    weight_lanes(3 * layer, pl.ds(3 * heads_wide, heads_wide), heads_wide),
                    NT,
                ),
            )

        each_sample(attention, gather_more)

        def second(b):
            got = folded(4 * layer, sb, b)
            branch[layer, b] = got
            x = layer_input(layer, b) + vec(b, row + 2) * got
            middle[layer, b] = x
            spread(gathered, 2 * layer + 1, sc, b, norm_forward(x, vec(b, row + 3), vec(b, row + 4)))

        each_sample(second, gather_more)
        gather_until(3 * layer + 1)

        def widen(b):
            spread_copy(gathered, 2 * layer + 1, sc, b).wait_recv()

            def body(n, carry):
                lanes = pl.ds(pl.multiple_of(n * tile, tile), tile)
                x = dot(gathered[2 * layer + 1, b], weight_lanes(3 * layer + 1, lanes, tile), NN)
                inner[b, :, lanes] = x
                t = jnp.tanh(GELU_C * (x + 0.044715 * x * x * x))
                act[b, :, lanes] = (0.5 * x * (1.0 + t)).astype(low)
                return carry

            lax.fori_loop(0, columns // tile, body, 0)

        each_sample(widen, gather_more)
        gather_until(3 * layer + 2)

        def narrow(b):
            fold(4 * layer + 1, sd, b, dot(act[b], weight(3 * layer + 2), NT))

        each_sample(narrow, gather_more)

        def third(b):
            outer[layer, b] = folded(4 * layer + 1, sd, b)

        each_sample(third)

    for copy, there in unsent:
        when(there, copy.wait_send)

    last = layers - 1
    loss_row[...] = jnp.zeros_like(loss_row)
    ends[...] = jnp.zeros_like(ends)
    pad = pl.ds(PATCH, PATCH)

    def head(b):
        x = middle[last, b] + vec(b, 6 * layers - 1) * outer[last, b]
        shift, scale = vec(b, 6 * layers), vec(b, 6 * layers + 1)
        xh, _ = norm_parts(x)
        normed = (xh * (1.0 + scale) + shift).astype(low)
        predicted = dot(head_rows, normed, NT)
        error = predicted - velocity[b]
        weighted = (0.5 + moments[b]) * error
        loss_row[...] += jnp.sum(weighted * error, axis=0, keepdims=True)
        grad_pred = (2.0 * weighted / total_count).astype(low)
        ends[pad, :width] += dot(grad_pred, normed, NN)
        dx, gshift, gscale = norm_backward(x, scale, dot(grad_pred, head_rows, TN))
        mod_grads[b, 6 * layers : 6 * layers + 1] = gshift
        mod_grads[b, 6 * layers + 1 : 6 * layers + 2] = gscale
        resid[b] = dx

    each_sample(head)

    def weight_grad(wave, left, right_of, first_tile, count):
        turned[...] = left.reshape(samples * tokens, width).T
        for n in range(count):
            got = dot(turned[...], right_of(pl.ds(n * tile, tile)), NN)
            lanes = pl.ds((first_tile + n) * tile, tile)
            full[wave, :, :, :, :, lanes] = got.astype(low).reshape(sizes + (rows, tile))
            produced.append(wave * per_wave + first_tile + n)
            if len(produced) <= LAG:
                reduce_step()

    for layer in reversed(range(layers)):
        row = 6 * layer
        se, sf, sg, sh = (8 * layer + 4 + i for i in range(4))

        def grad_first(b):
            g = resid[b]
            mod_grads[b, row + 5 : row + 6] = jnp.sum(g * outer[layer, b], axis=0, keepdims=True)
            spread(grad_spread, 2 * layer, se, b, (vec(b, row + 5) * g).astype(low))

        each_sample(grad_first, reduce_more)

        def grad_wide(b):
            spread_copy(grad_spread, 2 * layer, se, b).wait_recv()

            def body(n, carry):
                lanes = pl.ds(pl.multiple_of(n * tile, tile), tile)
                if layer == last:
                    x = inner[b, :, lanes]
                else:
                    x = dot(
                        gathered[2 * layer + 1, b], weight_lanes(3 * layer + 1, lanes, tile), NN
                    )
                g = dot(grad_spread[2 * layer, b], weight_lanes(3 * layer + 2, lanes, tile), NN)
                t = jnp.tanh(GELU_C * (x + 0.044715 * x * x * x))
                if layer != last:
                    act[b, :, lanes] = (0.5 * x * (1.0 + t)).astype(low)
                slope = 0.5 * (1.0 + t) + 0.5 * x * (1.0 - t * t) * (
                    GELU_C * (1.0 + 3.0 * 0.044715 * x * x)
                )
                grad_inner[b, :, lanes] = (g * slope).astype(low)
                return carry

            lax.fori_loop(0, columns // tile, body, 0)
            fold(4 * layer + 2, sf, b, dot(grad_inner[b], weight(3 * layer + 1), NT))

        each_sample(grad_wide, reduce_more)

        def wide_of(source):
            return lambda lanes: source[:, :, lanes].reshape(samples * tokens, tile)

        weight_grad(3 * layer + 2, grad_spread[2 * layer], wide_of(act), 0, per_wave)
        reduce_more()
        weight_grad(3 * layer + 1, gathered[2 * layer + 1], wide_of(grad_inner), 0, per_wave)
        reduce_more()

        def grad_second(b):
            dy = folded(4 * layer + 2, sf, b)
            dx, gshift, gscale = norm_backward(middle[layer, b], vec(b, row + 4), dy)
            g = dx + resid[b]
            resid[b] = g
            mod_grads[b, row + 3 : row + 4] = gshift
            mod_grads[b, row + 4 : row + 5] = gscale
            mod_grads[b, row + 2 : row + 3] = jnp.sum(g * branch[layer, b], axis=0, keepdims=True)
            spread(grad_spread, 2 * layer + 1, sg, b, (vec(b, row + 2) * g).astype(low))

        each_sample(grad_second, reduce_more)

        def grad_attention(b):
            spread_copy(grad_spread, 2 * layer + 1, sg, b).wait_recv()
            got_all = dot(
                grad_spread[2 * layer + 1, b],
                weight_lanes(3 * layer, pl.ds(3 * heads_wide, heads_wide), heads_wide),
                NN,
            ).astype(low)
            for p in range(pairs):
                ga = got_all[:, p * 2 * HDIM : (p + 1) * 2 * HDIM]
                q = qkv[layer, b, :, pair_lanes(0, p)]
                k = qkv[layer, b, :, pair_lanes(1, p)]
                v = qkv[layer, b, :, pair_lanes(2, p)]
                gq, gk, gv = [], [], []
                for h in range(2):
                    s = dot(k * keep[h], q, NT) * factor
                    e = jnp.exp(s - jnp.max(s, axis=0, keepdims=True))
                    e = e / jnp.sum(e, axis=0, keepdims=True)
                    dp = dot(v * keep[h], ga, NT)
                    ds = (e * (dp - jnp.sum(e * dp, axis=0, keepdims=True))).astype(low)
                    gv.append(dot(e.astype(low), ga, NN))
                    gk.append(dot(ds, q, NN))
                    gq.append(dot(ds, k, TN))
                for kind, got, scale in ((0, gq, factor), (1, gk, factor), (2, gv, 1.0)):
                    grad_mixed[b, :, pair_lanes(kind, p)] = (
                        jnp.where(first_head, got[0], got[1]) * scale
                    ).astype(low)
            fold(
                4 * layer + 3,
                sh,
                b,
                dot(
                    grad_mixed[b],
                    weight_lanes(3 * layer, pl.ds(0, 3 * heads_wide), 3 * heads_wide),
                    NT,
                ),
            )

        each_sample(grad_attention, reduce_more)
        weight_grad(3 * layer, gathered[2 * layer], wide_of(grad_mixed), 0, 3)
        weight_grad(3 * layer, grad_spread[2 * layer + 1], wide_of(attended.at[layer]), 3, 1)

        def grad_third(b):
            dy = folded(4 * layer + 3, sh, b)
            dx, gshift, gscale = norm_backward(layer_input(layer, b), vec(b, row + 1), dy)
            resid[b] = dx + resid[b]
            mod_grads[b, row : row + 1] = gshift
            mod_grads[b, row + 1 : row + 2] = gscale

        reduce_more()
        each_sample(grad_third)

    def patch(b):
        ends[pl.ds(0, PATCH), :width] += dot(blended[b], resid[b].astype(low), NN)

    each_sample(patch)
    ends[0:1, width:] = loss_row[0:1]
    for b in range(samples):
        mod_grads_low[b] = mod_grads[b].astype(low)
    first_pair = small(2, 1, mod_grads_low.at[1 - my_core], mod_grads_box, partner)
    ends_pair = small(2, 2, ends, ends_box, partner)
    small_start([first_pair, ends_pair])
    reduce_more()
    first_pair.wait_recv()
    grad_mods[my_core, my_dp] = (
        mod_grads_low[my_core].astype(jnp.float32) + mod_grads_box[...].astype(jnp.float32)
    ).astype(low)
    share_copies = [
        small(3, i, grad_mods.at[my_core, my_dp], grad_mods.at[my_core, my_dp], peer)
        for i, peer in enumerate(dp_peers)
    ]
    small_start(share_copies)
    reduce_more(2)
    for copy in share_copies:
        copy.wait_recv()
    share_pair = small(2, 3, grad_mods.at[my_core], grad_mods.at[my_core], partner)
    small_start([share_pair])
    reduce_more()
    share_pair.wait_recv()
    slots = grad_mods.shape[2]
    every_row = grad_mods[...].reshape(everyone * slots, width)
    slot = lax.broadcasted_iota(jnp.int32, (everyone * slots, 1), 0) % slots
    grad_cond_act = jnp.zeros((everyone * slots, rows), jnp.float32)
    for i in range(vectors):
        got = dot(every_row, mod_rows[:, pl.ds(i * width, width)], NT)
        grad_cond_act = grad_cond_act + jnp.where(slot == i, got, 0.0)
    grad_cond_act = jnp.sum(grad_cond_act.reshape(everyone, slots, rows), axis=1)
    reduce_more()
    cond = cond_out[...]
    gate = jax.nn.sigmoid(cond)
    grad_cond = grad_cond_act * gate * (1.0 + cond * (1.0 - gate))
    grad_cond_out[...] = grad_cond
    grad_time_act = dot(grad_cond.astype(low), cond_cols[:, :width], NN)
    ends_pair.wait_recv()
    ends_sum = ends[...] + ends_box[...]
    is_first = my_core == 0
    picked = jnp.where(is_first, ends_sum[:everyone, :width], grad_time_act)
    extra = jnp.where(is_first, ends_sum[0:1, width:], 0.0)
    for j in range(devices):
        for b in range(samples):
            sum_part[j, b : b + 1, :width] = picked[b * devices + j : b * devices + j + 1]
            sum_part[j, b : b + 1, width:] = extra
    sum_copies = [
        small(4, i, sum_part.at[peer[0]], sum_box.at[i], peer) for i, peer in enumerate(dp_peers)
    ]
    small_start(sum_copies)
    reduce_more(2)
    total_sum = sum_part[my_dp]
    for i, copy in enumerate(sum_copies):
        copy.wait_recv()
        total_sum = total_sum + sum_box[i]
    sums[my_core, my_dp] = total_sum
    back_copies = [
        small(5, i, sums.at[my_core, my_dp], sums.at[my_core, my_dp], peer)
        for i, peer in enumerate(dp_peers)
    ]
    small_start(back_copies)
    reduce_more(2)
    for copy in back_copies:
        copy.wait_recv()
    sums_pair = small(2, 4, sums.at[my_core], sums.at[my_core], partner)
    small_start([sums_pair])
    spread_act = jnp.broadcast_to(
        (cond * gate)[:, None, :], (everyone, slots, rows)
    ).reshape(everyone * slots, rows)
    stores = []
    per_line = columns // width
    for i in range(vectors):
        left = jnp.where(slot == i, spread_act, 0.0).astype(low)
        line, at = i // per_line, i % per_line * width
        where, start = line % 2, line // 2 * rows
        inner[where, start : start + rows, at : at + width] = dot(left, every_row, TN)
    for line in range(vectors // per_line):
        where, start = line % 2, line // 2 * rows
        copy = pltpu.make_async_copy(
            inner.at[where, pl.ds(start, rows)],
            grad_mod_out.at[:, pl.ds(line * columns, columns)],
            load_sem.at[line],
        )
        copy.start()
        stores.append(copy)
    reduce_more(2)
    sums_pair.wait_recv()
    for core in range(2):
        for j in range(devices):
            for b in range(samples):
                at = b * devices + j
                sums_out[core, at : at + 1] = sums[core, j, b : b + 1]
    while reduce_step():
        pass
    for copy in stores:
        copy.wait()
    for copy in small_unsent:
        copy.wait_send()
    for copy in rs_unsent:
        copy.wait_send()

    for copy in pair_unsent + list(out_last.values()):
        copy.wait_send()


def train_step(
    own_weights,
    places,
    latents,
    gaussian,
    moments,
    timing,
    cond_own,
    mod_rows,
    velocity,
    dp_count,
    layers,
    total,
):
    sizes = grid_of(dp_count)
    rows, columns = own_weights[2].shape[1:]
    waves = 3 * layers
    samples, (half_rows, width) = latents.shape[0], places.shape
    tokens = 2 * half_rows
    tile = columns // 4
    chunks = 4 * waves
    heads_wide = columns // 4
    most = max(sizes)
    slots = 16
    low, wide = jnp.bfloat16, jnp.float32
    in_vmem = pl.BlockSpec(memory_space=pltpu.VMEM)
    in_hbm = pl.BlockSpec(memory_space=pl.ANY)
    stages = 8 * layers
    resid_shape = (layers, samples, half_rows, width)
    dma = pltpu.SemaphoreType.DMA
    everyone = samples * dp_count
    return pl.pallas_call(
        lambda *refs: step_kernel(sizes, layers, total, *refs),
        out_shape=(
            jax.ShapeDtypeStruct((waves, rows, columns), wide),
            jax.ShapeDtypeStruct((everyone, timing.shape[1]), wide),
            jax.ShapeDtypeStruct((everyone, rows), wide),
            jax.ShapeDtypeStruct((everyone, rows), wide),
            jax.ShapeDtypeStruct((rows, mod_rows.shape[1]), wide),
            jax.ShapeDtypeStruct((2, everyone, width + 128), wide),
        ),
        in_specs=[in_hbm] * 5 + [in_vmem] * 8,
        out_specs=(in_vmem,) * 4 + (in_hbm, in_vmem),
        scratch_shapes=[
            pltpu.VMEM((waves,) + sizes + (rows, columns), low),
            pltpu.VMEM((chunks, sizes[2] - 1, sizes[0], sizes[1], rows, tile), low),
            pltpu.VMEM((chunks, sizes[1] - 1, sizes[0], rows, tile), low),
            pltpu.VMEM((chunks, sizes[0] - 1, rows, tile), low),
            pltpu.VMEM((2 * layers, samples, tokens, width), low),
            pltpu.VMEM((2 * layers, samples, tokens, width), low),
            pltpu.VMEM((2, samples, half_rows, width), low),
            pltpu.VMEM((4 * layers, samples, half_rows, width), low),
            pltpu.VMEM((layers, samples, tokens, 3 * heads_wide), low),
            pltpu.VMEM((layers, samples, tokens, heads_wide), low),
            pltpu.VMEM(resid_shape, wide),
            pltpu.VMEM(resid_shape, wide),
            pltpu.VMEM(resid_shape, wide),
            pltpu.VMEM(resid_shape, wide),
            pltpu.VMEM((samples, tokens, columns), wide),
            pltpu.VMEM((samples, tokens, columns), low),
            pltpu.VMEM((samples, tokens, columns), low),
            pltpu.VMEM((samples, tokens, 3 * heads_wide), low),
            pltpu.VMEM((samples, half_rows, width), wide),
            pltpu.VMEM((samples, tokens, width), wide),
            pltpu.VMEM((width, samples * tokens), low),
            pltpu.VMEM((rows, cond_own.shape[1] + -cond_own.shape[1] % 128), low),
            pltpu.VMEM((2 * PATCH, width), wide),
            pltpu.VMEM(latents.shape, low),
            pltpu.VMEM((dp_count,) + timing.shape, wide),
            pltpu.VMEM((dp_count, slots, width), low),
            pltpu.VMEM((dp_count - 1, slots, width), low),
            pltpu.VMEM((2, slots, width), wide),
            pltpu.VMEM((samples, slots, width), wide),
            pltpu.VMEM((samples, slots, width), low),
            pltpu.VMEM((slots, width), low),
            pltpu.VMEM((2 * PATCH, width + 128), wide),
            pltpu.VMEM((8, half_rows), wide),
            pltpu.VMEM((2 * PATCH, width + 128), wide),
            pltpu.VMEM((dp_count, samples, width + 128), wide),
            pltpu.VMEM((dp_count - 1, samples, width + 128), wide),
            pltpu.VMEM((2, dp_count, slots, width), low),
            pltpu.VMEM((2, dp_count, samples, width + 128), wide),
            dma((6, max(dp_count, 8))),
            dma((6, max(dp_count, 8))),
            dma((waves * len(GATHER_PLAN), 3, most)),
            dma((waves * len(GATHER_PLAN), 3, most)),
            dma((chunks, 3, most)),
            dma((chunks, 3, most)),
            dma((stages, samples)),
            dma((stages, samples)),
            dma((6 * layers + 2,)),
        ],
        compiler_params=pltpu.CompilerParams(
            collective_id=0, has_side_effects=True, vmem_limit_bytes=64 * 2**20 - 2**17
        ),
    )(
        *own_weights,
        places,
        latents,
        gaussian,
        moments,
        timing,
        cond_own,
        mod_rows,
        velocity,
    )


def all_peers(dp_count, with_cores):
    me, core = lax.axis_index("dp"), lax.axis_index("tensor")
    peers = []
    for offset in range(1, dp_count):
        peers.append(((me + offset) % dp_count, core))
    if with_cores:
        for offset in range(dp_count):
            peers.append(((me + offset) % dp_count, 1 - core))
    return peers


def push(source, target, sems, slot, device):
    return pltpu.make_async_remote_copy(
        src_ref=source,
        dst_ref=target,
        send_sem=sems[0].at[slot],
        recv_sem=sems[1].at[slot],
        device_id=device,
        device_id_type=MESH_ID,
    )


def norm_kernel(dp_count, x, out, box, send, recv):
    peers = all_peers(dp_count, True)
    greet(peers)
    copies = [push(x, box.at[i], (send, recv), i, p) for i, p in enumerate(peers)]
    for copy in copies:
        copy.start()
    total = x[...]
    for i, copy in enumerate(copies):
        copy.wait_recv()
        total = total + box[i]
    out[...] = total
    for copy in copies:
        copy.wait_send()


def sum_norms(x, dp_count):
    dma = pltpu.SemaphoreType.DMA
    count = 2 * dp_count - 1
    return pl.pallas_call(
        lambda *refs: norm_kernel(dp_count, *refs),
        out_shape=jax.ShapeDtypeStruct(x.shape, x.dtype),
        in_specs=[pl.BlockSpec(memory_space=pltpu.VMEM)],
        out_specs=pl.BlockSpec(memory_space=pltpu.VMEM),
        scratch_shapes=[pltpu.VMEM((count,) + x.shape, x.dtype), dma((count,)), dma((count,))],
        compiler_params=pltpu.CompilerParams(collective_id=5, has_side_effects=True),
    )(x)


def gather_plain(blob, dp_count):
    waves, rows, columns = blob.shape
    return lax.all_gather(blob, "dp", axis=1, tiled=True)


def reduce_plain(grads, dp_count):
    return jnp.stack(
        [
            lax.psum_scatter(g.astype(jnp.float32), "dp", scatter_dimension=0, tiled=True)
            for g in grads
        ]
    )


KINDS = 7


def pieces_of(kind, shape, layers):
    if kind == 0:
        return [((pl.ds(r, 48), slice(None)), 0) for r in range(0, shape[0], 48)]
    if kind == 1:
        split = [0] + list(range(768, shape[1], 512)) + [shape[1]]
        return [((slice(None), pl.ds(a, b - a)), 1) for a, b in zip(split, split[1:])]
    if kind == 2:
        return [((slice(None), pl.ds(c, 768)), 2) for c in range(0, shape[1], 768)]
    found = []
    for layer in range(layers):
        column = 3 + (kind - 3) * layers + layer
        if kind == 3:
            found += [((layer, part), column) for part in range(3)]
        else:
            found.append(((layer,), column))
    return found


def lamb_kernel(layers, shares, *refs):
    weights, firsts, seconds = refs[:7], refs[7:14], refs[14:21]
    own_grads, grad_mod, timing_all, grad_cond, sums = refs[21:26]
    first_out, second_out, update_out = refs[26:33], refs[33:40], refs[40:47]
    norms_out = refs[47]
    w_buf, m_buf, v_buf = refs[48:55], refs[55:62], refs[62:69]
    block_grads, mod_buf, small_buf, cond_buf, in_sem, out_sem, grad_sem = refs[69:]
    low = jnp.bfloat16
    width = small_buf.shape[1]
    heads_wide = w_buf[3].shape[3]
    sequence = (5, 6, 3, 4, 2, 1, 0)
    loads = {}
    block_load = pltpu.make_async_copy(own_grads, block_grads, grad_sem.at[0])
    block_load.start()
    mod_load = pltpu.make_async_copy(grad_mod, mod_buf, grad_sem.at[1])
    for kind in sequence:
        loads[kind] = [
            pltpu.make_async_copy(source[kind], target[kind], in_sem.at[kind, i])
            for i, (source, target) in enumerate(
                ((weights, w_buf), (firsts, m_buf), (seconds, v_buf))
            )
        ]
        for copy in loads[kind]:
            copy.start()
        if kind == 2:
            mod_load.start()

    time_pre = timing_all[:, :width]
    gate = jax.nn.sigmoid(time_pre)
    time_act = (time_pre * gate).astype(low)
    grad_time_act = sums[1, :, :width]
    grad_pre = (grad_time_act * gate * (1.0 + time_pre * (1.0 - gate))).astype(low)
    small_buf[:PATCH] = sums[0, :PATCH, :width]
    small_buf[PATCH : PATCH + FREQ] = dot(
        timing_all[:, width : width + FREQ].astype(low), grad_pre, TN
    )
    small_buf[PATCH + FREQ :] = sums[0, PATCH:, :width]
    label = timing_all[:, width + FREQ : width + FREQ + 1].astype(jnp.int32)
    classes = cond_buf.shape[1] - width
    onehot = lax.broadcasted_iota(jnp.int32, (timing_all.shape[0], classes), 1) == label
    cond_buf[:, :width] = dot(grad_cond[...].astype(low), time_act, TN)
    cond_buf[:, width:] = lax.dot_general(
        grad_cond[...],
        jnp.where(onehot, 1.0, 0.0),
        TN,
        precision=HIGHEST_PREC,
        preferred_element_type=jnp.float32,
    )

    def gradient(kind, index):
        if kind < 3:
            return (small_buf, cond_buf, mod_buf)[kind][index]
        layer = index[0]
        if kind == 3:
            return block_grads[3 * layer, :, pl.ds(index[1] * heads_wide, heads_wide)]
        if kind == 4:
            return block_grads[3 * layer, :, pl.ds(3 * heads_wide, heads_wide)]
        return block_grads[3 * layer + kind - 4]

    lane = lax.broadcasted_iota(jnp.int32, (1, 128), 1)
    norm_rows = [jnp.zeros((1, 128), jnp.float32), jnp.zeros((1, 128), jnp.float32)]
    stores = []
    block_load.wait()
    for kind in sequence:
        for copy in loads[kind]:
            copy.wait()
        if kind == 2:
            mod_load.wait()
        share = shares[kind]
        for index, column in pieces_of(kind, w_buf[kind].shape, layers):
            g = gradient(kind, index)
            weight = w_buf[kind][index]
            first, second, update = lamb_parts(weight, m_buf[kind][index], v_buf[kind][index], g)
            m_buf[kind][index] = first
            v_buf[kind][index] = second
            w_buf[kind][index] = update
            for row, value in enumerate((weight, update)):
                norm_rows[row] = norm_rows[row] + jnp.where(
                    lane == column, share * jnp.sum(value * value), 0.0
                )
        for i, (source, target) in enumerate(
            ((m_buf, first_out), (v_buf, second_out), (w_buf, update_out))
        ):
            copy = pltpu.make_async_copy(source[kind], target[kind], out_sem.at[kind, i])
            copy.start()
            stores.append(copy)
    norms_out[...] = jnp.zeros_like(norms_out)
    norms_out[0:1] = norm_rows[0]
    norms_out[1:2] = norm_rows[1]
    for copy in stores:
        copy.wait()


def lamb_first(weights, firsts, seconds, own_grads, grad_mod, timing_all, grad_cond, sums, shares):
    layers = weights[3].shape[0]
    in_hbm = pl.BlockSpec(memory_space=pl.ANY)
    in_vmem = pl.BlockSpec(memory_space=pltpu.VMEM)
    wide = jnp.float32
    like = [jax.ShapeDtypeStruct(w.shape, wide) for w in weights]
    held = [pltpu.VMEM(w.shape, wide) for w in weights]
    dma = pltpu.SemaphoreType.DMA
    out = pl.pallas_call(
        lambda *refs: lamb_kernel(layers, shares, *refs),
        out_shape=tuple(like * 3 + [jax.ShapeDtypeStruct((8, 128), wide)]),
        in_specs=[in_hbm] * 23 + [in_vmem] * 3,
        out_specs=tuple([in_hbm] * 21 + [in_vmem]),
        scratch_shapes=held * 3
        + [
            pltpu.VMEM(own_grads.shape, wide),
            pltpu.VMEM(grad_mod.shape, wide),
            held[0],
            held[1],
            dma((KINDS, 3)),
            dma((KINDS, 3)),
            dma((2,)),
        ],
        compiler_params=pltpu.CompilerParams(vmem_limit_bytes=64 * 2**20 - 2**17),
    )(*weights, *firsts, *seconds, own_grads, grad_mod, timing_all, grad_cond, sums)
    return out[:7], out[7:14], out[14:21], out[21]


def apply_kernel(layers, *refs):
    norms, weights, updates = refs[0], refs[1:8], refs[8:15]
    outs, w_buf, u_buf, in_sem, out_sem = refs[15:22], refs[22:29], refs[29:36], refs[36], refs[37]
    sequence = (5, 6, 3, 4, 1, 0, 2)
    loads = {}
    for kind in sequence:
        loads[kind] = [
            pltpu.make_async_copy(source[kind], target[kind], in_sem.at[kind, i])
            for i, (source, target) in enumerate(((weights, w_buf), (updates, u_buf)))
        ]
        for copy in loads[kind]:
            copy.start()
    lane = lax.broadcasted_iota(jnp.int32, (1, 128), 1)
    ratio = jnp.sqrt(norms[0:1] + EPS_NORM) / jnp.sqrt(norms[1:2] + EPS_NORM)
    stores = []
    for kind in sequence:
        for copy in loads[kind]:
            copy.wait()
        for index, column in pieces_of(kind, w_buf[kind].shape, layers):
            factor = LEARN_RATE * jnp.sum(jnp.where(lane == column, ratio, 0.0))
            w_buf[kind][index] = w_buf[kind][index] - factor * u_buf[kind][index]
        copy = pltpu.make_async_copy(w_buf[kind], outs[kind], out_sem.at[kind])
        copy.start()
        stores.append(copy)
    for copy in stores:
        copy.wait()


def lamb_last(norms, weights, updates):
    layers = weights[3].shape[0]
    in_hbm = pl.BlockSpec(memory_space=pl.ANY)
    wide = jnp.float32
    held = [pltpu.VMEM(w.shape, wide) for w in weights]
    dma = pltpu.SemaphoreType.DMA
    return pl.pallas_call(
        lambda *refs: apply_kernel(layers, *refs),
        out_shape=tuple(jax.ShapeDtypeStruct(w.shape, wide) for w in weights),
        in_specs=[pl.BlockSpec(memory_space=pltpu.VMEM)] + [in_hbm] * 14,
        out_specs=(in_hbm,) * 7,
        scratch_shapes=held * 2 + [dma((KINDS, 2)), dma((KINDS,))],
        compiler_params=pltpu.CompilerParams(vmem_limit_bytes=64 * 2**20 - 2**17),
    )(norms, *weights, *updates)


def turned_views(small, cond, mod, qkv, proj, up, down):
    return [
        small,
        cond.T,
        mod,
        qkv.transpose(0, 2, 1, 3),
        proj.transpose(0, 2, 1),
        up,
        down.transpose(0, 2, 1),
    ]


def local(
    latents,
    gaussian,
    velocity,
    time_ids,
    labels,
    small_w,
    small_m,
    small_v,
    cond_w,
    cond_m,
    cond_v,
    mod_w,
    mod_m,
    mod_v,
    qkv_w,
    qkv_m,
    qkv_v,
    proj_w,
    proj_m,
    proj_v,
    up_w,
    up_m,
    up_v,
    down_w,
    down_m,
    down_v,
):
    layer_count = qkv_w.shape[0]
    model_width = mod_w.shape[1] // (6 * layer_count + 2)
    dp_count = lax.axis_size("dp")
    tensor_count = lax.axis_size("tensor")
    samples = latents.shape[0]
    half_rows = latents.shape[2]
    rows = qkv_w.shape[1]
    kernels = rows % 16 == 0 and 2 * layer_count * rows <= 2 * half_rows
    kernels = kernels and dp_count * 16 == 2 * half_rows
    my_dp = lax.axis_index("dp")
    low = jnp.bfloat16

    heads_wide = qkv_w.shape[3]

    small_low = small_w.astype(low)
    patch_rows = small_low[:PATCH]
    time_rows = small_low[PATCH : PATCH + FREQ]
    head_rows = small_low[PATCH + FREQ :]
    mod_low = mod_w.astype(low)

    moment = (time_ids.astype(jnp.float32) + 0.5) / TSTEPS
    token_index = lax.axis_index("tensor") * half_rows + jnp.arange(half_rows)
    time_weight = 0.5 + moment
    total_count = samples * dp_count * half_rows * tensor_count * PATCH
    features = time_features(moment).astype(low)
    time_pre = jnp.dot(features, time_rows, preferred_element_type=jnp.float32)
    timing = jnp.concatenate(
        [
            time_pre,
            features.astype(jnp.float32),
            jnp.broadcast_to(labels.astype(jnp.float32)[:, None], (samples, 128)),
        ],
        axis=1,
    )
    if kernels:
        own_grads, timing_all, cond, grad_cond, grad_mod_w, sums = train_step(
            (
                qkv_w.transpose(0, 2, 1, 3),
                proj_w.transpose(0, 2, 1),
                up_w,
                down_w.transpose(0, 2, 1),
                small_w,
            ),
            position_table(token_index, model_width),
            latents,
            gaussian,
            jnp.broadcast_to(moment[:, None, None], latents.shape),
            timing,
            cond_w.T,
            mod_low,
            velocity,
            dp_count,
            layer_count,
            float(total_count),
        )
        loss_sum = jnp.sum(sums[0, 0, model_width:])
        shares = [1.0 / (dp_count * tensor_count), 1.0 / tensor_count, 1.0 / tensor_count]
        weights = turned_views(small_w, cond_w, mod_w, qkv_w, proj_w, up_w, down_w)
        firsts, seconds, updates, squares_sum = lamb_first(
            weights,
            turned_views(small_m, cond_m, mod_m, qkv_m, proj_m, up_m, down_m),
            turned_views(small_v, cond_v, mod_v, qkv_v, proj_v, up_v, down_v),
            own_grads,
            grad_mod_w,
            timing_all,
            grad_cond,
            sums,
            shares + [1.0] * 4,
        )
        squares_sum = sum_norms(squares_sum, dp_count)
        renewed = lamb_last(squares_sum, weights, updates)
        outputs = []
        for triple in zip(*(turned_views(*kind) for kind in (renewed, firsts, seconds))):
            outputs += list(triple)
        norms = jnp.sqrt(squares_sum[:2, : 3 + 4 * layer_count] + EPS_NORM)
        return tuple(outputs) + (loss_sum, norms)
    else:
        blended = ((1.0 - moment)[:, None, None] * latents + moment[:, None, None] * gaussian).astype(
            jnp.bfloat16
        )
        hidden = (
            jnp.einsum("bpn,pd->bnd", blended, patch_rows, preferred_element_type=jnp.float32)
            + position_table(token_index, model_width)[None]
        )
        timing_all = lax.all_gather(timing, "dp", axis=1, tiled=False)
        timing_all = timing_all.reshape(samples * dp_count, -1)
        time_act = jax.nn.silu(timing_all[:, :model_width]).astype(low)
        all_labels = timing_all[:, model_width + FREQ].astype(jnp.int32)
        onehot = (all_labels[:, None] == jnp.arange(CLASSES)[None, :]).astype(low)
        cond_low = cond_w.astype(low)
        cond = jnp.dot(
            time_act, cond_low[:model_width], preferred_element_type=jnp.float32
        ) + jnp.dot(onehot, cond_low[model_width:], preferred_element_type=jnp.float32)
        modulation = jnp.dot(
            jax.nn.silu(cond).astype(low), mod_low, preferred_element_type=jnp.float32
        ).reshape(samples, dp_count, -1)
        modulation = lax.psum_scatter(modulation, "dp", scatter_dimension=1, tiled=True)[:, 0]
        parts = []
        for i in range(layer_count):
            parts.append(
                jnp.concatenate(
                    [qkv_w[i, :, 0], qkv_w[i, :, 1], qkv_w[i, :, 2], proj_w[i].T], axis=1
                ).astype(low)
            )
            parts.append(up_w[i].astype(low))
            parts.append(down_w[i].T.astype(low))
        blob = jnp.stack(parts)
        full = gather_plain(blob, dp_count)
        saved_list = []
        fetched = []
        for layer_id in range(layer_count):
            packed = full[3 * layer_id]
            weights = (
                packed[:, : 3 * heads_wide].reshape(model_width, 3, heads_wide),
                packed[:, 3 * heads_wide :],
                full[3 * layer_id + 1],
                full[3 * layer_id + 2],
            )
            layer_mod = modulation[
                :, 6 * layer_id * model_width : (6 * layer_id + 6) * model_width
            ].reshape(samples, 6, model_width)
            hidden, saved_state = block_forward(hidden, layer_mod, weights)
            saved_list.append(saved_state)
            fetched.append(weights)
        final_mod = modulation[:, 6 * layer_count * model_width :].reshape(samples, 2, model_width)
        final_normed = modulated_norm(hidden, final_mod[:, 0], final_mod[:, 1]).astype(jnp.bfloat16)
        predicted = jnp.einsum(
            "bnd,pd->bpn", final_normed, head_rows, preferred_element_type=jnp.float32
        )
        error = predicted - velocity
        loss_part = jnp.sum(time_weight[:, None, None] * error * error)
        grad_pred = (time_weight[:, None, None] * (2.0 * error) / total_count).astype(jnp.bfloat16)
        grad_head = jnp.einsum(
            "bpn,bnd->pd", grad_pred, final_normed, preferred_element_type=jnp.float32
        )
        grad_final = jnp.einsum("bpn,pd->bnd", grad_pred, head_rows, preferred_element_type=jnp.float32)
        _, final_back = jax.vjp(modulated_norm, hidden, final_mod[:, 0], final_mod[:, 1])
        grad_hidden, grad_fshift, grad_fscale = final_back(grad_final)
        mod_grads = [None] * layer_count
        layer_grads = [None] * (3 * layer_count)
        for layer_id in reversed(range(layer_count)):
            layer_mod = modulation[
                :, 6 * layer_id * model_width : (6 * layer_id + 6) * model_width
            ].reshape(samples, 6, model_width)
            grad_hidden, grad_layer_mod, grads = block_backward(
                grad_hidden, layer_mod, fetched[layer_id], saved_list[layer_id]
            )
            layer_grads[3 * layer_id] = jnp.concatenate(
                [grads[0].reshape(model_width, 3 * heads_wide).astype(low), grads[1].astype(low)],
                axis=1,
            )
            layer_grads[3 * layer_id + 1] = grads[2].astype(low)
            layer_grads[3 * layer_id + 2] = grads[3].astype(low)
            mod_grads[layer_id] = grad_layer_mod.reshape(samples, 6 * model_width)
        own_grads = reduce_plain(layer_grads, dp_count)
        grad_patch = jnp.einsum(
            "bpn,bnd->pd", blended, grad_hidden.astype(jnp.bfloat16), preferred_element_type=jnp.float32
        )
        ends = jnp.concatenate([grad_patch, grad_head], axis=0)
        all_mods = jnp.concatenate(
            mod_grads
            + [jnp.stack([grad_fshift, grad_fscale], axis=1).reshape(samples, 2 * model_width)],
            axis=1,
        )
        grad_mods = lax.all_gather(lax.psum(all_mods.astype(low), "tensor"), "dp", axis=1)
        grad_mods = grad_mods.reshape(samples * dp_count, -1)
        grad_cond_act = jnp.einsum(
            "be,de->bd", grad_mods, mod_low, preferred_element_type=jnp.float32
        )
        cond_act, silu_back = jax.vjp(jax.nn.silu, cond)
        grad_mod_w = jnp.einsum(
            "bd,be->de", cond_act.astype(low), grad_mods, preferred_element_type=jnp.float32
        )
        grad_cond = silu_back(grad_cond_act)[0]
        grad_time_act = jnp.einsum(
            "be,de->bd",
            grad_cond.astype(low),
            cond_low[:model_width],
            preferred_element_type=jnp.float32,
        )
        ends, grad_time_act, loss_sum = lax.psum(
            (ends, grad_time_act / tensor_count, loss_part), ("dp", "tensor")
        )
    time_pre = timing_all[:, :model_width]
    features = timing_all[:, model_width : model_width + FREQ].astype(low)
    all_labels = timing_all[:, model_width + FREQ].astype(jnp.int32)
    onehot = all_labels[:, None] == jnp.arange(CLASSES)[None, :]
    time_act = jax.nn.silu(time_pre).astype(low)
    grad_temb = grad_cond.astype(low)
    grad_table = jnp.einsum(
        "bc,bd->cd", onehot.astype(jnp.float32), grad_cond, precision=HIGHEST_PREC
    )
    grad_time_two = jnp.einsum("bd,be->de", time_act, grad_temb, preferred_element_type=jnp.float32)
    grad_cond_w = jnp.concatenate([grad_time_two, grad_table], axis=0)
    _, silu_back_two = jax.vjp(jax.nn.silu, time_pre)
    grad_pre = silu_back_two(grad_time_act)[0].astype(low)
    grad_time_one = jnp.einsum("bf,bd->fd", features, grad_pre, preferred_element_type=jnp.float32)
    grad_small = jnp.concatenate([ends[:PATCH], grad_time_one, ends[PATCH:]], axis=0)

    def stacked(kind):
        return jnp.stack([kind(i) for i in range(layer_count)])

    grads_list = [
        grad_small,
        grad_cond_w,
        grad_mod_w,
        stacked(lambda i: own_grads[3 * i][:, : 3 * heads_wide].reshape(rows, 3, heads_wide)),
        stacked(lambda i: own_grads[3 * i][:, 3 * heads_wide :].T),
        stacked(lambda i: own_grads[3 * i + 1]),
        stacked(lambda i: own_grads[3 * i + 2].T),
    ]
    weights_list = [small_w, cond_w, mod_w, qkv_w, proj_w, up_w, down_w]
    firsts_list = [small_m, cond_m, mod_m, qkv_m, proj_m, up_m, down_m]
    seconds_list = [small_v, cond_v, mod_v, qkv_v, proj_v, up_v, down_v]
    shares = [1.0 / (dp_count * tensor_count), 1.0 / tensor_count, 1.0 / tensor_count]
    shares = shares + [1.0] * 4

    def squares(arrays):
        sums = []
        for kind_id, a in enumerate(arrays):
            axes = None if kind_id < 3 else tuple(range(1, a.ndim))
            sums.append(jnp.sum(a * a, axis=axes).reshape(-1) * shares[kind_id])
        return jnp.concatenate(sums)

    results = [
        lamb_parts(weights_list[i], firsts_list[i], seconds_list[i], grads_list[i])
        for i in range(len(weights_list))
    ]
    updates = [r[2] for r in results]
    total_sq = jnp.stack([squares(weights_list), squares(updates)])
    total_sq = lax.psum(total_sq, ("dp", "tensor"))
    norms = jnp.sqrt(total_sq + EPS_NORM)
    ratio = norms[0] / norms[1]
    outputs = []
    for kind_id in range(7):
        if kind_id < 3:
            factor = ratio[kind_id]
        else:
            first = 3 + (kind_id - 3) * layer_count
            factor = ratio[first : first + layer_count].reshape(
                (layer_count,) + (1,) * (weights_list[kind_id].ndim - 1)
            )
        outputs.append(weights_list[kind_id] - LEARN_RATE * factor * updates[kind_id])
        outputs.append(results[kind_id][0])
        outputs.append(results[kind_id][1])
    return tuple(outputs) + (loss_sum, norms)


def solution(mesh):
    return jax.shard_map(
        local,
        mesh=mesh,
        in_specs=(
            P("dp", None, "tensor"),
            P("dp", None, "tensor"),
            P("dp", None, "tensor"),
            P("dp"),
            P("dp"),
            P(),
            P(),
            P(),
            P(None, "dp"),
            P(None, "dp"),
            P(None, "dp"),
            P("dp", None),
            P("dp", None),
            P("dp", None),
            P(None, "dp", None, "tensor"),
            P(None, "dp", None, "tensor"),
            P(None, "dp", None, "tensor"),
            P(None, "tensor", "dp"),
            P(None, "tensor", "dp"),
            P(None, "tensor", "dp"),
            P(None, "dp", "tensor"),
            P(None, "dp", "tensor"),
            P(None, "dp", "tensor"),
            P(None, "tensor", "dp"),
            P(None, "tensor", "dp"),
            P(None, "tensor", "dp"),
        ),
        out_specs=(
            P(),
            P(),
            P(),
            P(None, "dp"),
            P(None, "dp"),
            P(None, "dp"),
            P("dp", None),
            P("dp", None),
            P("dp", None),
            P(None, "dp", None, "tensor"),
            P(None, "dp", None, "tensor"),
            P(None, "dp", None, "tensor"),
            P(None, "tensor", "dp"),
            P(None, "tensor", "dp"),
            P(None, "tensor", "dp"),
            P(None, "dp", "tensor"),
            P(None, "dp", "tensor"),
            P(None, "dp", "tensor"),
            P(None, "tensor", "dp"),
            P(None, "tensor", "dp"),
            P(None, "tensor", "dp"),
            P(),
            P(),
        ),
        check_vma=False,
    )
```
